32 devices in a mesh: dp: 8 (over z, y), narrow: 4 (over x, core).
Axes of the slice: x: 2, y: 2, z: 4, core: 2. Of those that a mesh axis runs over, the one named last changes fastest.
Arguments:
- patches: bfloat16 [8, 768, 48], P('dp', 'narrow'), may hold values from -6 to 6
- segment_ids: int32 [8, 768], P('dp'), may hold values from 0 to 11, as said below
- labels: int32 [8, 12], P('dp'), may hold values from 0 to 999
- embed_weight: bfloat16 [48, 768], replicated, may hold values from -0.875 to 0.875
- embed_bias: bfloat16 [768], replicated, may hold values from -3 to 3
- position_table: bfloat16 [256, 768], replicated, may hold values from -3 to 3
- class_table: bfloat16 [1000, 768], replicated, may hold values from -3 to 3
- attn_gain: bfloat16 [768], replicated, may hold values from 0.5 to 1.5
- qkv_weight: bfloat16 [768, 2304], replicated, may hold values from -0.21875 to 0.21875
- proj_weight: bfloat16 [768, 768], replicated, may hold values from -0.875 to 0.875
- mlp_gain: bfloat16 [768], replicated, may hold values from 0.5 to 1.5
- up_weight: bfloat16 [768, 3072], replicated, may hold values from -0.21875 to 0.21875
- down_weight: bfloat16 [3072, 768], replicated, may hold values from -0.109375 to 0.109375
- head_weight: bfloat16 [768, 96], replicated, may hold values from -0.0546875 to 0.0546875
- latent_grad: bfloat16 [8, 768, 48], P('dp', 'narrow'), may hold values from -6 to 6
- logdet_grad: float32 [8, 768], P('dp', 'narrow'), may hold values from -3 to 3
Outputs:
- latent: float32 [8, 768, 48], P('dp', 'narrow')
- logdet: float32 [8, 768], P('dp', 'narrow')
- patches_grad: float32 [8, 768, 48], P('dp', 'narrow')
- embed_grad: float32 [48, 768], P(None, 'dp')
- bias_grad: float32 [768], P('dp')
- position_grad: float32 [256, 768], P(None, 'dp')
- class_grad: float32 [1000, 768], P(None, 'dp')
- attngain_grad: float32 [768], P('dp')
- qkv_grad: float32 [768, 2304], P('dp')
- proj_grad: float32 [768, 768], P('dp')
- mlpgain_grad: float32 [768], P('dp')
- up_grad: float32 [768, 3072], P('dp')
- down_grad: float32 [3072, 768], P(None, 'dp')
- head_grad: float32 [768, 96], P('dp')
The draws below stay inside these ranges and needn't reach their ends.
Inputs may be any that keep to these rules, and one draw needn't show every extreme that they name: `segment_ids`: each row holds whole images one after another, numbered 0, 1, 2 and so on in order; an image covers 64 or 256 patches in a row and starts at a multiple of 64; every row is full. `labels`: entry s is the class of image s of the row; entries past the row's last image are not read.
All inputs are finite; a program needn't handle non-finite values.
Results may differ from the reference program's by a relative error of at most 0.018.
Values may be sent and summed in bfloat16 or wider, within the bound.
No kernel may reach another device: no remote copies, remote signals or barrier semaphores. Data moves between devices by JAX's collectives and lax.ppermute only.
A program may use at most 192 MiB of HBM per device.

```python
import math
import jax
import jax.numpy as jnp
from jax import lax

D = 768
H = 12
HD = 64
FF = 3072
P_SIZE = 48
NCLASS = 1000
UNIT = 64
SEGS = 12
BIG = 256
L = 768
ROWS_DEV = 1
ROWS = 8
N_DP = 8


def draw_segment_ids(key, part):
    row_keys = jax.random.split(key, ROWS)
    row_numbers = jnp.arange(ROWS, dtype=jnp.int32)

    def one_row(row_key, row_number):
        count_key, order_key = jax.random.split(row_key)
        drawn_count = jax.random.randint(count_key, (), 0, SEGS // 4 + 1)
        big_count = jnp.where(row_number == 0, 0, drawn_count)
        item_count = SEGS - 3 * big_count
        index = jnp.arange(SEGS, dtype=jnp.int32)
        scores = jax.random.randint(order_key, (SEGS,), 0, 1 << 20) * SEGS + index
        valid = index < item_count
        smaller = jnp.sum(((scores[None, :] < scores[:, None]) & valid[None, :]).astype(jnp.int32), axis=1)
        is_big = valid & (smaller < big_count)
        units = jnp.where(valid, jnp.where(is_big, 4, 1), 0).astype(jnp.int32)
        ends = jnp.cumsum(units)
        unit_of = jnp.arange(L, dtype=jnp.int32) // UNIT
        return jnp.sum((ends[None, :] <= unit_of[:, None]).astype(jnp.int32), axis=1).astype(jnp.int32)
    return jax.vmap(one_row)(row_keys, row_numbers)


def touch_ends(drawn, stream_key, least, top_value):
    extent = drawn.shape
    place = [jax.random.randint(jax.random.fold_in(stream_key, axis), (), 0, extent[axis]) for axis in range(len(extent))]
    drawn = drawn.at[tuple(place)].set(least)
    longest = extent.index(max(extent))
    place[longest] = (place[longest] + 1) % extent[longest]
    return drawn.at[tuple(place)].set(top_value)


def level_of(stream_key, extent, pieces, low, top_value):
    def one(position, shards_of):
        draws = jax.random.uniform(jax.random.fold_in(jax.random.fold_in(stream_key, 6), position), (shards_of,), jnp.float32, low / len(pieces), top_value / len(pieces))
        return jnp.repeat(jnp.exp(draws), extent[position] // shards_of).reshape((-1,) + (1,) * (len(extent) - position - 1))

    factor_of = one(*pieces[0])
    for cut in pieces[1:]:
        factor_of = factor_of * one(*cut)
    return factor_of


def normal_values(rng, extent, deviation, bound, cuts=(), held_as=jnp.bfloat16):
    factor_of = level_of(rng, extent, cuts, -0.22, 0.18) if cuts else 1.0
    entries = jax.random.normal(rng, extent, jnp.float32) * deviation * factor_of
    return jnp.minimum(jnp.maximum(entries, -bound), bound).astype(held_as)


def setup_inputs(seed: int = 0) -> dict:
    key_list = jax.random.split(jax.random.key(seed), 17)
    patches = normal_values(key_list[0], (ROWS, L, P_SIZE), 1.0, 6.0, ((0, 8), (1, 4)))
    segment_ids = draw_segment_ids(jax.random.fold_in(key_list[16], 71), 0)
    labels = touch_ends(jax.random.randint(key_list[2], (ROWS, SEGS), 0, NCLASS), jax.random.fold_in(key_list[2], 1), 0, NCLASS - 1).astype(jnp.int32)
    embed_weight = normal_values(key_list[3], (P_SIZE, D), P_SIZE ** -0.5, 0.875)
    embed_bias = normal_values(key_list[4], (D,), 0.5, 3.0)
    position_table = normal_values(key_list[5], (BIG, D), 0.5, 3.0)
    class_table = normal_values(key_list[6], (NCLASS, D), 0.5, 3.0)
    attn_gain = jnp.clip(1.0 + 0.1 * jax.random.normal(key_list[7], (D,), jnp.float32), 0.5, 1.5).astype(jnp.bfloat16)
    qkv_weight = normal_values(key_list[8], (D, 3 * D), D ** -0.5, 0.21875)
    proj_weight = normal_values(key_list[9], (D, D), (D // 16) ** -0.5, 0.875)
    mlp_gain = jnp.clip(1.0 + 0.1 * jax.random.normal(key_list[10], (D,), jnp.float32), 0.5, 1.5).astype(jnp.bfloat16)
    up_weight = normal_values(key_list[11], (D, FF), D ** -0.5, 0.21875)
    down_weight = normal_values(key_list[12], (FF, D), FF ** -0.5, 0.109375)
    head_weight = normal_values(key_list[13], (D, 2 * P_SIZE), (16 * D) ** -0.5, 0.0546875)
    latent_grad = normal_values(key_list[14], (ROWS, L, P_SIZE), 1.0, 6.0, ((0, 8), (1, 4)))
    logdet_grad = normal_values(key_list[15], (ROWS, L), 0.5, 3.0, ((0, 8), (1, 4)), jnp.float32)
    return {"patches": patches, "segment_ids": segment_ids, "labels": labels, "embed_weight": embed_weight, "embed_bias": embed_bias, "position_table": position_table, "class_table": class_table, "attn_gain": attn_gain, "qkv_weight": qkv_weight, "proj_weight": proj_weight, "mlp_gain": mlp_gain, "up_weight": up_weight, "down_weight": down_weight, "head_weight": head_weight, "latent_grad": latent_grad, "logdet_grad": logdet_grad}


@jax.custom_vjp
def low(v):
    return lax.optimization_barrier(v.astype(jnp.bfloat16)).astype(jnp.float32)

@jax.custom_vjp
def low_back(v):
    return v

def low_keep(v):
    return (low(v), None)

def low_pass(kept, grad):
    return (grad,)

def back_keep(v):
    return (v, None)

def back_low(kept, grad):
    return (low(grad),)
low.defvjp(low_keep, low_pass)
low_back.defvjp(back_keep, back_low)
highest = lax.Precision.HIGHEST
epsilon = 1e-05
masked_score = -1e+30

def layer_norm(values, norm_gain):
    center = lax.optimization_barrier(jnp.mean(values, axis=-1, keepdims=True))
    offsets = values - center
    spread = lax.optimization_barrier(jnp.mean(offsets * offsets, axis=-1, keepdims=True))
    return offsets * lax.rsqrt(spread + epsilon) * norm_gain

def row_layout(segment_row):
    length = segment_row.shape[0]
    index = jnp.arange(length, dtype=jnp.int32)
    before = jnp.concatenate([jnp.full((1,), -1, jnp.int32), segment_row[:-1]])
    opening = segment_row != before
    first_index = lax.cummax(jnp.where(opening, index, jnp.zeros_like(index)), axis=0)
    return ((index - first_index).astype(jnp.int32), jnp.logical_not(opening))

def allowed_pairs(segment_row):
    length = segment_row.shape[0]
    index = jnp.arange(length, dtype=jnp.int32)
    return (segment_row[:, None] == segment_row[None, :]) & (index[None, :] <= index[:, None])

def product(left, right):
    return jnp.matmul(left, right, precision=highest)

def attend_row(row_items):
    packed, segment_row = row_items
    queries = packed[:, 0]
    keys_in = packed[:, 1]
    values_in = packed[:, 2]
    score_scale = 1.0 / math.sqrt(packed.shape[-1])
    scores = low_back(jnp.einsum('qhd,khd->hqk', queries, keys_in, precision=highest) * score_scale)
    masked = jnp.where(allowed_pairs(segment_row)[None], scores, masked_score)
    weights = jax.nn.softmax(masked, axis=-1)
    return jnp.einsum('hqk,khd->qhd', low(weights), values_in, precision=highest)

def forward(weights_all, patch_rows, segment_rows, label_rows):
    embed_weight, embed_bias, position_table, class_table, attn_gain, qkv_weight, proj_weight, mlp_gain, up_weight, down_weight, head_weight = weights_all
    row_count, length, channels = patch_rows.shape
    model_width = qkv_weight.shape[0]
    positions, kept_rows = jax.vmap(row_layout)(segment_rows)
    shifted = jnp.concatenate([jnp.zeros_like(patch_rows[:, :1]), patch_rows[:, :-1]], axis=1)
    previous = jnp.where(kept_rows[..., None], shifted, jnp.zeros_like(shifted))
    class_rows = jnp.take(class_table, label_rows, axis=0)
    class_tokens = jax.vmap(lambda table_rows, image_ids: jnp.take(table_rows, image_ids, axis=0))(class_rows, segment_rows)
    embedded = low_back(product(previous, embed_weight) + embed_bias + jnp.take(position_table, positions, axis=0) + class_tokens)
    normed_one = low(layer_norm(embedded, attn_gain))
    qkv_all = low(low_back(product(normed_one, qkv_weight)))
    packed = qkv_all.reshape(row_count, length, 3, H, HD)
    attended = lax.map(jax.checkpoint(attend_row), (packed, segment_rows))
    mixed_heads = low(low_back(attended)).reshape(row_count, length, model_width)
    stream_one = embedded + low_back(product(mixed_heads, proj_weight))
    normed_two = low(layer_norm(stream_one, mlp_gain))
    hidden_pre = low_back(product(normed_two, up_weight))
    hidden = low(jax.nn.gelu(hidden_pre, approximate=False))
    stream_two = stream_one + low_back(product(hidden, down_weight))
    head_out = low_back(product(low(stream_two), head_weight))
    mean_shift = head_out[..., :channels]
    logscale = head_out[..., channels:]
    latent = (patch_rows - mean_shift) * jnp.exp(-logscale)
    logdet = -lax.optimization_barrier(jnp.sum(logscale, axis=-1))
    return (latent, logdet)

def reference(patches, segment_ids, labels, embed_weight, embed_bias, position_table, class_table, attn_gain, qkv_weight, proj_weight, mlp_gain, up_weight, down_weight, head_weight, latent_grad, logdet_grad):
    weights_all = tuple((source.astype(jnp.float32) for source in (embed_weight, embed_bias, position_table, class_table, attn_gain, qkv_weight, proj_weight, mlp_gain, up_weight, down_weight, head_weight)))
    patch_groups = patches.astype(jnp.float32).reshape(N_DP, ROWS_DEV, L, P_SIZE)
    segment_groups = segment_ids.reshape(N_DP, ROWS_DEV, L)
    label_groups = labels.reshape(N_DP, ROWS_DEV, SEGS)
    latent_groups = latent_grad.astype(jnp.float32).reshape(N_DP, ROWS_DEV, L, P_SIZE)
    logdet_groups = logdet_grad.astype(jnp.float32).reshape(N_DP, ROWS_DEV, L)

    def group_step(totals, group_items):
        patch_rows, segment_rows, label_rows, latent_rows, logdet_rows = group_items

        def forward_group(weights_in, patch_in):
            return forward(weights_in, patch_in, segment_rows, label_rows)
        outputs, pull = jax.vjp(forward_group, weights_all, patch_rows)
        weight_grads, patch_grads = pull((latent_rows, logdet_rows))
        totals = jax.tree.map(lambda left, right: left + right, totals, weight_grads)
        return (totals, (outputs[0], outputs[1], patch_grads))
    start_totals = tuple((jnp.zeros_like(source) for source in weights_all))
    totals, (latent, logdet, patches_grad) = lax.scan(group_step, start_totals, (patch_groups, segment_groups, label_groups, latent_groups, logdet_groups))
    return (latent.reshape(ROWS, L, P_SIZE), logdet.reshape(ROWS, L), patches_grad.reshape(ROWS, L, P_SIZE), totals[0], totals[1], totals[2], totals[3], totals[4], totals[5], totals[6], totals[7], totals[8], totals[9], totals[10])
```

```python
import math

import jax
import jax.numpy as jnp
from jax import lax
from jax.sharding import PartitionSpec as P

HD = 64
UNIT = 64
bf16, f32 = jnp.bfloat16, jnp.float32
epsilon = 1e-05
masked_score = -1e30


def dot(left, right):
    return jnp.dot(left, right, preferred_element_type=f32)


def token_sum(left, right):
    return lax.dot_general(left, right, (((0,), (0,)), ((), ())), preferred_element_type=f32)


def back_dot(grads, weight):
    return lax.dot_general(grads, weight, (((1,), (1,)), ((), ())), preferred_element_type=f32)


def swap(value, axis, step):
    count = lax.axis_size(axis)
    return lax.ppermute(value, axis, [(i, i ^ step) for i in range(count)])


def normalised(values):
    center = jnp.mean(values, axis=-1, keepdims=True)
    offsets = values - center
    inverse = lax.rsqrt(jnp.mean(offsets * offsets, axis=-1, keepdims=True) + epsilon)
    return offsets * inverse, inverse


def norm_back(grads, gain, normed, inverse):
    e = grads * gain
    mean_e = jnp.mean(e, axis=-1, keepdims=True)
    mean_en = jnp.mean(e * normed, axis=-1, keepdims=True)
    return inverse * (e - mean_e - normed * mean_en)


def bit_reversed(count):
    bits = count.bit_length() - 1
    return [int(format(k, f"0{bits}b")[::-1], 2) if bits else 0 for k in range(count)]


def relative_blocks(grad, me, count):
    size = grad.shape[0] // count
    return jnp.stack(
        [lax.dynamic_slice_in_dim(grad, (me ^ j) * size, size, 0) for j in bit_reversed(count)]
    )


def reduce_rows(blocks):
    step = 1
    while blocks.shape[0] > 1:
        half = blocks.shape[0] // 2
        arrived = swap(blocks[half:], "dp", step)
        blocks = (blocks[:half].astype(f32) + arrived.astype(f32)).astype(bf16)
        step *= 2
    return blocks[0]


def row_attention(q, k, v, segments):
    length = q.shape[0]
    index = jnp.arange(length, dtype=jnp.int32)
    allowed = (segments[:, None] == segments[None, :]) & (index[None, :] <= index[:, None])
    scores = jnp.einsum("qhd,khd->hqk", q, k, preferred_element_type=f32) / math.sqrt(HD)
    masked = jnp.where(allowed[None], scores, masked_score)
    peak = jnp.max(masked, axis=-1, keepdims=True)
    raised = jnp.exp(masked - peak)
    weights = raised / jnp.sum(raised, axis=-1, keepdims=True)
    out = jnp.einsum("hqk,khd->qhd", weights.astype(bf16), v, preferred_element_type=f32)
    return out.astype(bf16), weights


def row_attention_back(q, k, v, weights, grads):
    scale = 1.0 / math.sqrt(HD)
    grad_weights = jnp.einsum("qhd,khd->hqk", grads, v, preferred_element_type=f32)
    centre = jnp.sum(weights * grad_weights, axis=-1, keepdims=True)
    ds = (weights * (grad_weights - centre)).astype(bf16)
    dq = jnp.einsum("hqk,khd->qhd", ds, k, preferred_element_type=f32) * scale
    dk = jnp.einsum("hqk,qhd->khd", ds, q, preferred_element_type=f32) * scale
    dv = jnp.einsum("hqk,qhd->khd", weights.astype(bf16), grads, preferred_element_type=f32)
    return jnp.stack([dq, dk, dv], axis=1).astype(bf16)


def shards(
    patches,
    segment_ids,
    labels,
    embed_weight,
    embed_bias,
    position_table,
    class_table,
    attn_gain,
    qkv_weight,
    proj_weight,
    mlp_gain,
    up_weight,
    down_weight,
    head_weight,
    latent_grad,
    logdet_grad,
):
    _, quarter, channels = patches.shape
    length = segment_ids.shape[1]
    width = qkv_weight.shape[0]
    hidden_width = up_weight.shape[1]
    count = lax.axis_size("dp")
    me = lax.axis_index("dp")
    r = lax.axis_index("narrow")
    core, far = r & 1, r >> 1
    half_width = width // 2
    heads = half_width // HD

    def own_rows(full):
        return jnp.concatenate(
            [
                lax.dynamic_slice_in_dim(full, core * quarter, quarter, 0),
                lax.dynamic_slice_in_dim(full, (core + 2) * quarter, quarter, 0),
            ]
        )

    def peer_rows(full):
        return jnp.concatenate(
            [
                lax.dynamic_slice_in_dim(full, (1 - core) * quarter, quarter, 0),
                lax.dynamic_slice_in_dim(full, (3 - core) * quarter, quarter, 0),
            ]
        )

    def natural(mine, peers):
        a, b, c, d = mine[:quarter], mine[quarter:], peers[:quarter], peers[quarter:]
        return jnp.where(core == 0, jnp.concatenate([a, c, b, d]), jnp.concatenate([c, a, d, b]))

    def pair_order(own, other):
        return jnp.where(far == 0, jnp.concatenate([own, other]), jnp.concatenate([other, own]))

    logdet_col = logdet_grad.reshape(quarter, 1)
    coarse = lax.reduce_precision(logdet_col, 8, 7)
    fine = logdet_col - coarse
    own_in = jnp.concatenate(
        [patches[0], latent_grad[0], coarse.astype(bf16), fine.astype(bf16)], axis=1
    )
    half_in = pair_order(own_in, swap(own_in, "narrow", 2))
    patches_half = half_in[:, :channels]
    latent_cot = half_in[:, channels : 2 * channels].astype(f32)
    logdet_cot = half_in[:, 2 * channels].astype(f32) + half_in[:, 2 * channels + 1].astype(f32)
    patches_all = natural(patches_half, swap(patches_half, "narrow", 1))

    segments = segment_ids[0]
    units = length // UNIT
    unit_ids = segments.reshape(units, UNIT)[:, 0]
    first_unit = jnp.sum((unit_ids[None, :] < unit_ids[:, None]).astype(jnp.int32), axis=1)
    blocks = jnp.arange(units, dtype=jnp.int32) - first_unit
    inner = jnp.arange(UNIT, dtype=jnp.int32)
    positions = (blocks[:, None] * UNIT + inner[None, :]).reshape(length)
    kept = (positions > 0)[:, None]
    shifted = jnp.concatenate([jnp.zeros_like(patches_all[:1]), patches_all[:-1]])
    previous = jnp.where(kept, shifted, jnp.zeros_like(shifted))
    position_hot = (
        positions[:, None] == jnp.arange(position_table.shape[0], dtype=jnp.int32)[None, :]
    ).astype(bf16)
    segment_hot = (
        segments[:, None] == jnp.arange(labels.shape[1], dtype=jnp.int32)[None, :]
    ).astype(bf16)
    label_hot = (labels[0][:, None] == jnp.arange(class_table.shape[0], dtype=jnp.int32)).astype(
        bf16
    )
    class_rows = dot(label_hot, class_table).astype(bf16)
    sources = jnp.concatenate([previous, position_hot, segment_hot], axis=1)
    tables = jnp.concatenate([embed_weight, position_table, class_rows])
    embedded_all = dot(sources, tables) + embed_bias.astype(f32)
    gain_attn = attn_gain.astype(f32)
    gain_mlp = mlp_gain.astype(f32)
    n_one_all, inverse_all = normalised(embedded_all)
    normed_one_all = (n_one_all * gain_attn).astype(bf16)
    embedded = own_rows(embedded_all)
    n_one, inverse_one = own_rows(n_one_all), own_rows(inverse_all)

    qkv_own = lax.dynamic_index_in_dim(
        qkv_weight.reshape(width, 3, 2, half_width), core, 2, keepdims=False
    ).reshape(width, 3 * half_width)
    qkv = dot(normed_one_all, qkv_own).astype(bf16).reshape(length, 3, heads, HD)
    q, k, v = qkv[:, 0], qkv[:, 1], qkv[:, 2]
    attended_own, weights = row_attention(q, k, v, segments)
    attended_own = attended_own.reshape(length, half_width)
    attended_peer = swap(attended_own, "narrow", 1)
    mixed_all = jnp.where(
        core == 0,
        jnp.concatenate([attended_own, attended_peer], axis=1),
        jnp.concatenate([attended_peer, attended_own], axis=1),
    )
    mixed = own_rows(mixed_all)

    stream_one = embedded + dot(mixed, proj_weight)
    n_two, inverse_two = normalised(stream_one)
    normed_two = (n_two * gain_mlp).astype(bf16)
    hidden_pre = dot(normed_two, up_weight)
    cdf = 0.5 * (1.0 + lax.erf(hidden_pre * math.sqrt(0.5)))
    hidden = (hidden_pre * cdf).astype(bf16)
    slope = cdf + hidden_pre * jnp.exp(-0.5 * hidden_pre * hidden_pre) / math.sqrt(2 * math.pi)
    stream_low = (stream_one + dot(hidden, down_weight)).astype(bf16)
    head_out = dot(stream_low, head_weight)
    mean_shift, logscale = head_out[:, :channels], head_out[:, channels:]
    factor = jnp.exp(-logscale)
    latent = (patches_half.astype(f32) - mean_shift) * factor
    logdet = -jnp.sum(logscale, axis=-1)
    direct = latent_cot * factor
    d_head = jnp.concatenate([-direct, -latent_cot * latent - logdet_cot[:, None]], axis=1).astype(
        bf16
    )
    d_two = back_dot(d_head, head_weight)
    d_mlp = d_two.astype(bf16)
    d_hidden = (back_dot(d_mlp, down_weight) * slope).astype(bf16)
    d_normed_two = back_dot(d_hidden, up_weight)
    gain_part_two = jnp.sum(d_normed_two * n_two, axis=0)
    d_one = d_two + norm_back(d_normed_two, gain_mlp, n_two, inverse_two)
    d_attn = d_one.astype(bf16)

    d_attn_all = natural(d_attn, swap(d_attn, "narrow", 1))
    proj_own = lax.dynamic_slice_in_dim(proj_weight, core * half_width, half_width, 0)
    d_mixed = back_dot(d_attn_all, proj_own).astype(bf16).reshape(length, heads, HD)
    d_qkv = row_attention_back(q, k, v, weights, d_mixed).reshape(length, 3, half_width)
    d_qkv_peer = swap(peer_rows(d_qkv), "narrow", 1)
    d_qkv_mine = own_rows(d_qkv)
    d_qkv_half = jnp.where(
        core == 0,
        jnp.concatenate([d_qkv_mine, d_qkv_peer], axis=2),
        jnp.concatenate([d_qkv_peer, d_qkv_mine], axis=2),
    ).reshape(2 * quarter, 3 * width)
    d_normed_one = back_dot(d_qkv_half, qkv_weight)
    gain_part_one = jnp.sum(d_normed_one * n_one, axis=0)
    d_embed = (d_one + norm_back(d_normed_one, gain_attn, n_one, inverse_one)).astype(bf16)
    parts = jnp.stack([gain_part_one, gain_part_two])
    parts_high = lax.reduce_precision(parts, 8, 7)
    parts_low = parts - parts_high
    d_embed_peer = swap(
        jnp.concatenate([d_embed, parts_high.astype(bf16), parts_low.astype(bf16)]), "narrow", 1
    )
    d_embed_all = natural(d_embed, d_embed_peer[: 2 * quarter])
    parts = parts + d_embed_peer[2 * quarter : 2 * quarter + 2] + d_embed_peer[2 * quarter + 2 :]

    d_previous = jnp.where(kept, back_dot(d_embed_all, embed_weight), 0.0)
    carried = jnp.concatenate([d_previous[1:], jnp.zeros_like(d_previous[:1])])
    carried = lax.dynamic_slice_in_dim(carried, r * quarter, quarter, 0)

    def own_quarter(half):
        return lax.dynamic_slice_in_dim(half, far * quarter, quarter, 0)

    latent_out = own_quarter(latent)
    logdet_out = own_quarter(logdet)
    patches_grad = own_quarter(direct) + carried

    ff = hidden_width // 4

    def ff_part(array, index):
        return lax.dynamic_slice_in_dim(array, index * ff, ff, 1)

    hidden_all = jnp.concatenate(
        [ff_part(hidden, r), swap(ff_part(hidden, r ^ 1), "narrow", 1)]
    )
    d_hidden_all = jnp.concatenate(
        [ff_part(d_hidden, r), swap(ff_part(d_hidden, r ^ 1), "narrow", 1)]
    )
    d_mlp_all = jnp.concatenate([d_mlp, swap(d_mlp, "narrow", 1)])
    normed_two_all = jnp.concatenate([normed_two, swap(normed_two, "narrow", 1)])
    down_part = token_sum(d_mlp_all, hidden_all)
    up_part = token_sum(normed_two_all, d_hidden_all)
    head_own = token_sum(stream_low, d_head)
    head_cols = 2 * channels // 4

    def head_part_of(index):
        return lax.dynamic_slice_in_dim(head_own, index * head_cols, head_cols, 1)

    head_part = head_part_of(r) + swap(head_part_of(r ^ 1).astype(bf16), "narrow", 1).astype(f32)
    proj_cols = width // 4
    proj_part = token_sum(
        mixed_all, lax.dynamic_slice_in_dim(d_attn_all, r * proj_cols, proj_cols, 1)
    )
    group = half_width // 2
    qkv_part = token_sum(
        normed_one_all,
        lax.dynamic_slice_in_dim(d_qkv, far * group, group, 2).reshape(length, 3 * group),
    )
    table_rows = channels + position_table.shape[0]
    table_cols = table_rows // 4
    embed_part = token_sum(
        d_embed_all, lax.dynamic_slice_in_dim(sources, r * table_cols, table_cols, 1)
    )
    segment_part = token_sum(d_embed_all, segment_hot)
    bias_part = jnp.sum(segment_part, axis=1, keepdims=True)
    class_part = dot(segment_part.astype(bf16), label_hot)
    class_cols = class_table.shape[0] // 4
    class_part = lax.dynamic_slice_in_dim(class_part, r * class_cols, class_cols, 1)

    def reduced(*columns):
        joined = jnp.concatenate([part.astype(bf16) for part in columns], axis=1)
        return reduce_rows(relative_blocks(joined, me, count))

    def gathered(part):
        pair = jnp.stack([part, swap(part, "narrow", 1)])
        four = jnp.concatenate([pair, swap(pair, "narrow", 2)])
        return [lax.dynamic_index_in_dim(four, r ^ i, 0, keepdims=False).astype(f32) for i in range(4)]

    def joined(pieces, start, size, axis=1):
        return jnp.concatenate([piece[:, start : start + size] for piece in pieces], axis=axis)

    first = gathered(reduced(down_part, head_part))
    second = gathered(reduced(up_part))
    third = gathered(reduced(proj_part, qkv_part))
    last = gathered(reduced(embed_part, class_part, bias_part, parts.T))
    down_grad = joined(first, 0, ff).T
    head_grad = joined(first, ff, head_cols)
    up_grad = joined(second, 0, ff)
    proj_grad = joined(third, 0, proj_cols)
    qkv_pieces = [third[i] for i in (0, 2, 1, 3)]
    qkv_grad = jnp.concatenate(
        [joined(qkv_pieces, proj_cols + t * group, group) for t in range(3)], axis=1
    )
    tables_grad = joined(last, 0, table_cols).T
    embed_grad, position_grad = tables_grad[:channels], tables_grad[channels:]
    class_grad = joined(last, table_cols, class_cols).T
    vectors = last[0][:, table_cols + class_cols :]
    return (
        latent_out[None],
        logdet_out[None],
        patches_grad[None],
        embed_grad,
        vectors[:, 0],
        position_grad,
        class_grad,
        vectors[:, 1],
        qkv_grad,
        proj_grad,
        vectors[:, 2],
        up_grad,
        down_grad,
        head_grad,
    )


def solution(mesh):
    return jax.shard_map(
        shards,
        mesh=mesh,
        in_specs=(
            P("dp", "narrow", None),
            P("dp", None),
            P("dp", None),
            P(),
            P(),
            P(),
            P(),
            P(),
            P(),
            P(),
            P(),
            P(),
            P(),
            P(),
            P("dp", "narrow", None),
            P("dp", "narrow"),
        ),
        out_specs=(
            P("dp", "narrow", None),
            P("dp", "narrow"),
            P("dp", "narrow", None),
            P(None, "dp"),
            P("dp"),
            P(None, "dp"),
            P(None, "dp"),
            P("dp"),
            P("dp", None),
            P("dp", None),
            P("dp"),
            P("dp", None),
            P(None, "dp"),
            P("dp", None),
        ),
        check_vma=False,
    )
```

```python
import functools
import math

import jax
import jax.numpy as jnp
from jax import lax
from jax.experimental import pallas as pl
from jax.experimental.pallas import tpu as pltpu
from jax.sharding import PartitionSpec as P

HD = 64
UNIT = 64
BIG = 256
TILE = 128
EXTRA = 16
LANES = 128
bf16, f32 = jnp.bfloat16, jnp.float32
epsilon = 1e-05
masked_score = -1e30


def dot(left, right):
    return jnp.dot(left, right, preferred_element_type=f32)


def token_sum(left, right):
    return lax.dot_general(left, right, (((0,), (0,)), ((), ())), preferred_element_type=f32)


def back_dot(grads, weight):
    return lax.dot_general(grads, weight, (((1,), (1,)), ((), ())), preferred_element_type=f32)


def swap(value, axis, step):
    count = lax.axis_size(axis)
    return lax.ppermute(value, axis, [(i, i ^ step) for i in range(count)])


def normalised(values):
    center = jnp.mean(values, axis=-1, keepdims=True)
    offsets = values - center
    inverse = lax.rsqrt(jnp.mean(offsets * offsets, axis=-1, keepdims=True) + epsilon)
    return offsets * inverse, inverse


def norm_back(grads, gain, normed, inverse):
    e = grads * gain
    mean_e = jnp.mean(e, axis=-1, keepdims=True)
    mean_en = jnp.mean(e * normed, axis=-1, keepdims=True)
    return inverse * (e - mean_e - normed * mean_en)


def bit_reversed(count):
    bits = count.bit_length() - 1
    return [int(format(k, f"0{bits}b")[::-1], 2) if bits else 0 for k in range(count)]


def relative_blocks(grad, me, count):
    size = grad.shape[0] // count
    return jnp.stack(
        [lax.dynamic_slice_in_dim(grad, (me ^ j) * size, size, 0) for j in bit_reversed(count)]
    )


def reduce_rows(blocks):
    step = 1
    while blocks.shape[0] > 1:
        half = blocks.shape[0] // 2
        arrived = swap(blocks[half:], "dp", step)
        blocks = (blocks[:half].astype(f32) + arrived.astype(f32)).astype(bf16)
        step *= 2
    return blocks[0]


def block_weights(scores, row_start, key_start, first_ref):
    shape = scores.shape
    row = lax.broadcasted_iota(jnp.int32, shape, 0)
    key = lax.broadcasted_iota(jnp.int32, shape, 1) + key_start
    unit = row_start // UNIT
    first = jnp.where(row < UNIT, first_ref[unit], first_ref[unit + 1])
    allowed = (key >= first) & (key <= row + row_start)
    masked = jnp.where(allowed, scores * (1.0 / math.sqrt(HD)), masked_score)
    raised = jnp.exp(masked - jnp.max(masked, axis=-1, keepdims=True))
    return raised * (1.0 / jnp.sum(raised, axis=-1, keepdims=True))


def head_masks():
    lane = lax.broadcasted_iota(jnp.int32, (1, 2 * HD), 1)
    low = (lane < HD).astype(f32)
    return low.astype(bf16), (1.0 - low).astype(bf16)


def window_of(start):
    return max(0, start - BIG), start + TILE


def front_kernel(
    first_ref,
    block_ref,
    image_ref,
    core_ref,
    previous_ref,
    embed_ref,
    bias_ref,
    position_ref,
    class_ref,
    gain_ref,
    weight_ref,
    embedded_ref,
    normed_ref,
    qkv_ref,
    attended_ref,
    own_weight,
    sems,
):
    length, width = normed_ref.shape
    half = width // 2
    quarter = length // 4
    core = core_ref[0]
    copies = []
    for t in range(3):
        start = pl.multiple_of(t * width + core * half, 128)
        copies.append(
            pltpu.make_async_copy(weight_ref.at[:, pl.ds(start, half)], own_weight.at[t], sems.at[t])
        )
        copies[-1].start()
    gain = gain_ref[...]
    for u in range(length // UNIT):
        rows = pl.ds(u * UNIT, UNIT)
        table = position_ref[pl.ds(pl.multiple_of(block_ref[u] * UNIT, UNIT), UNIT), :]
        image = class_ref[pl.ds(image_ref[u], 1), :]
        values = (
            dot(previous_ref[rows, :], embed_ref[...])
            + bias_ref[...]
            + table.astype(f32)
            + image
        )
        q = u * UNIT // quarter
        inside = (q >> 1) * quarter + u * UNIT - q * quarter

        @pl.when(core == (q & 1))
        def _():
            embedded_ref[pl.ds(inside, UNIT), :] = values

        normed_ref[rows, :] = (normalised(values)[0] * gain).astype(bf16)
    for t in range(3):
        copies[t].wait()
        qkv_ref[:, t * half : (t + 1) * half] = dot(normed_ref[...], own_weight[t]).astype(bf16)
    masks = head_masks()
    low_lanes = lax.broadcasted_iota(jnp.int32, (TILE, 2 * HD), 1) < HD

    def pair_step(pair, carry):
        lanes = [pl.ds(pl.multiple_of(t * half + pair * 2 * HD, 128), 2 * HD) for t in range(3)]
        for start in range(0, length, TILE):
            begin, end = window_of(start)
            q = qkv_ref[start : start + TILE, lanes[0]]
            k = qkv_ref[begin:end, lanes[1]]
            v = qkv_ref[begin:end, lanes[2]]
            outs = []
            for mask in masks:
                weights = block_weights(back_dot(q * mask, k), start, begin, first_ref)
                outs.append(dot(weights.astype(bf16), v))
            attended_ref[start : start + TILE, lanes[0]] = jnp.where(
                low_lanes, outs[0], outs[1]
            ).astype(bf16)
        return carry

    lax.fori_loop(0, half // (2 * HD), pair_step, 0)


def back_attention_kernel(
    first_ref,
    core_ref,
    qkv_ref,
    mine_ref,
    peer_ref,
    proj_ref,
    own_ref,
    send_ref,
    mixed,
    key_total,
    value_total,
):
    length = qkv_ref.shape[0]
    half = qkv_ref.shape[1] // 3
    quarter = length // 4
    core = core_ref[0]
    proj = proj_ref[pl.ds(pl.multiple_of(core * half, 128), half), :]
    for ref, side in ((mine_ref, core), (peer_ref, 1 - core)):
        product = back_dot(ref[...], proj).astype(bf16)
        for i in range(2):
            rows = pl.ds(pl.multiple_of((2 * i + side) * quarter, 16), quarter)
            mixed[rows, :] = product[i * quarter : (i + 1) * quarter]
    masks = head_masks()
    low_lanes = lax.broadcasted_iota(jnp.int32, (TILE, 2 * HD), 1) < HD
    scale = 1.0 / math.sqrt(HD)

    def pair_step(pair, carry):
        lanes = [pl.ds(pl.multiple_of(t * half + pair * 2 * HD, 128), 2 * HD) for t in range(3)]
        key_total[...] = jnp.zeros_like(key_total)
        value_total[...] = jnp.zeros_like(value_total)

        def put(start, rows, t, value):
            at = start
            while at < start + rows:
                q = at // quarter
                stop = min(start + rows, (q + 1) * quarter)
                piece = value[at - start : stop - start]
                inside = (q >> 1) * quarter + at - q * quarter
                for side, ref in ((0, own_ref), (1, send_ref)):

                    @pl.when((core ^ side) == (q & 1))
                    def _():
                        ref[inside : inside + stop - at, lanes[t]] = piece

                at = stop

        for start in range(0, length, TILE):
            begin, end = window_of(start)
            q = qkv_ref[start : start + TILE, lanes[0]]
            k = qkv_ref[begin:end, lanes[1]]
            v = qkv_ref[begin:end, lanes[2]]
            grads = mixed[start : start + TILE, lanes[0]]
            outs = []
            for mask in masks:
                q_one, grads_one = q * mask, grads * mask
                weights = block_weights(back_dot(q_one, k), start, begin, first_ref)
                d_weights = back_dot(grads_one, v)
                centre = jnp.sum(weights * d_weights, axis=-1, keepdims=True)
                d_scores = (weights * (d_weights - centre)).astype(bf16)
                outs.append(dot(d_scores, k))
                key_total[begin:end, :] += token_sum(d_scores, q_one)
                value_total[begin:end, :] += token_sum(weights.astype(bf16), grads_one)
            d_q = jnp.where(low_lanes, outs[0], outs[1]) * scale
            put(start, TILE, 0, d_q.astype(bf16))
        for q in range(4):
            rows = slice(q * quarter, (q + 1) * quarter)
            put(q * quarter, quarter, 1, (key_total[rows, :] * scale).astype(bf16))
            put(q * quarter, quarter, 2, value_total[rows, :].astype(bf16))
        return carry

    lax.fori_loop(0, half // (2 * HD), pair_step, 0)


def middle_kernel(
    core_ref,
    place_ref,
    embedded_ref,
    own_ref,
    peer_ref,
    gain_ref,
    shift_ref,
    scale_ref,
    pick_ref,
    patches_ref,
    cot_ref,
    logdet_cot_ref,
    proj_hbm,
    up_hbm,
    down_hbm,
    latent_ref,
    logdet_ref,
    direct_ref,
    normed_ref,
    hidden_ref,
    d_mlp_ref,
    d_hidden_ref,
    d_one_ref,
    d_attn_ref,
    gain_part_ref,
    head_ref,
    head_send_ref,
    proj,
    up,
    down,
    hidden_rest,
    d_hidden_rest,
    slope,
    stream,
    low,
    sems,
):
    tokens, width = embedded_ref.shape
    quarter = tokens // 2
    half = width // 2
    ff = up.shape[2]
    chunk = 256
    core, place = core_ref[0], place_ref[0]
    copies = [pltpu.make_async_copy(proj_hbm, proj, sems.at[0])]
    copies[0].start()
    for j in range(4):
        columns = pl.ds(pl.multiple_of((place ^ j) * ff, 128), ff)
        copies.append(pltpu.make_async_copy(up_hbm.at[:, columns], up.at[j], sems.at[1 + j]))
        copies[-1].start()
    for j in range(4):
        rows = pl.ds(pl.multiple_of((place ^ j) * ff, 128), ff)
        copies.append(pltpu.make_async_copy(down_hbm.at[rows, :], down.at[j], sems.at[5 + j]))
        copies[-1].start()
    copies[0].wait()
    gain = gain_ref[...]
    for i in range(2):
        source = pl.ds(pl.multiple_of((2 * i + core) * quarter, 16), quarter)
        rows = slice(i * quarter, (i + 1) * quarter)
        values = embedded_ref[rows, :]
        for ref, side in ((own_ref, core), (peer_ref, 1 - core)):
            weight = proj[pl.ds(pl.multiple_of(side * half, 128), half), :]
            values += dot(ref[source, :], weight)
        stream[rows, :] = values
        normed_ref[rows, :] = (normalised(values)[0] * gain).astype(bf16)
    for j in range(4):
        copies[1 + j].wait()

        def up_step(i, carry):
            columns = pl.ds(pl.multiple_of(i * chunk, 128), chunk)
            pre = dot(normed_ref[...], up[j, :, columns])
            cdf = 0.5 * (1.0 + lax.erf(pre * math.sqrt(0.5)))
            density = jnp.exp(-0.5 * pre * pre) * (1.0 / math.sqrt(2 * math.pi))
            slope[j, :, columns] = cdf + pre * density
            value = (pre * cdf).astype(bf16)
            if j < 2:
                hidden_ref[j, :, columns] = value
            else:
                hidden_rest[j - 2, :, columns] = value
            return carry

        lax.fori_loop(0, ff // chunk, up_step, 0)
    total = stream[...]
    for j in range(4):
        copies[5 + j].wait()
        total += dot(hidden_ref[j] if j < 2 else hidden_rest[j - 2], down[j])
    low[...] = total.astype(bf16)
    mean_shift = dot(low[...], shift_ref[...])
    logscale = dot(low[...], scale_ref[...])
    factor = jnp.exp(-logscale)
    latent = (patches_ref[...].astype(f32) - mean_shift) * factor
    latent_ref[...] = latent
    logdet_ref[...] = -jnp.sum(logscale, axis=-1, keepdims=True)
    cot = cot_ref[...].astype(f32)
    direct = cot * factor
    direct_ref[...] = direct
    d_shift = (-direct).astype(bf16)
    d_scale = (-cot * latent - logdet_cot_ref[...]).astype(bf16)
    channels = d_shift.shape[1]
    for i, ref in enumerate((head_ref, head_send_ref)):
        picked = dot(d_shift, pick_ref[i, :channels]) + dot(d_scale, pick_ref[i, channels:])
        ref[...] = token_sum(low[...], picked.astype(bf16)).astype(ref.dtype)
    d_two = back_dot(d_shift, shift_ref[...]) + back_dot(d_scale, scale_ref[...])
    d_one_ref[...] = d_two
    d_mlp_ref[...] = d_two.astype(bf16)
    for j in range(4):

        def down_step(i, carry):
            columns = pl.ds(pl.multiple_of(i * chunk, 128), chunk)
            value = (back_dot(d_mlp_ref[...], down[j, columns, :]) * slope[j, :, columns]).astype(
                bf16
            )
            if j < 2:
                d_hidden_ref[j, :, columns] = value
            else:
                d_hidden_rest[j - 2, :, columns] = value
            return carry

        lax.fori_loop(0, ff // chunk, down_step, 0)
    for i in range(2):
        rows = slice(i * quarter, (i + 1) * quarter)
        grads = jnp.zeros((quarter, width), f32)
        for j in range(4):
            value = d_hidden_ref[j, rows, :] if j < 2 else d_hidden_rest[j - 2, rows, :]
            grads += back_dot(value, up[j])
        n, inverse = normalised(stream[rows, :])
        part = jnp.sum(grads * n, axis=0, keepdims=True)
        gain_part_ref[...] = part if i == 0 else gain_part_ref[...] + part
        d_one = d_one_ref[rows, :] + norm_back(grads, gain, n, inverse)
        d_one_ref[rows, :] = d_one
        d_attn_ref[rows, :] = d_one.astype(bf16)


def back_front_kernel(
    core_ref,
    own_ref,
    peer_ref,
    embedded_ref,
    d_one_ref,
    gain_ref,
    part_ref,
    weight_ref,
    d_embed_ref,
):
    tokens, width = embedded_ref.shape
    half = width // 2
    core = core_ref[0]
    gain = gain_ref[...]
    rows_step = tokens // 2
    for i in range(2):
        rows = slice(i * rows_step, (i + 1) * rows_step)
        grads = jnp.zeros((rows_step, width), f32)
        for ref, side in ((own_ref, core), (peer_ref, 1 - core)):
            for t in range(3):
                columns = pl.ds(pl.multiple_of(t * width + side * half, 128), half)
                grads += back_dot(ref[rows, t * half : (t + 1) * half], weight_ref[:, columns])
        n, inverse = normalised(embedded_ref[rows, :])
        part = jnp.sum(grads * n, axis=0, keepdims=True)
        total = part if i == 0 else total + part
        d_embed_ref[rows, :] = (d_one_ref[rows, :] + norm_back(grads, gain, n, inverse)).astype(
            bf16
        )
    row = lax.broadcasted_iota(jnp.int32, (EXTRA, width), 0)
    both = jnp.where(row % 2 == 0, total, part_ref[...])
    coarse = both.astype(bf16).astype(f32)
    rest = jnp.where(row < 2, coarse, jnp.where(row < 4, both - coarse, 0.0))
    d_embed_ref[tokens : tokens + EXTRA, :] = rest.astype(bf16)


def place_blocks(total, outs, me, size):
    if len(outs) == 1:
        outs[0][...] = total[...].astype(bf16)
        return
    keep, send = outs
    order = bit_reversed(2 * keep.shape[0])
    for k, j in enumerate(order):
        block = total[pl.ds(pl.multiple_of((me ^ j) * size, 16), size), :].astype(bf16)
        if k < keep.shape[0]:
            keep[k] = block
        else:
            send[k - keep.shape[0]] = block


def pair_sum_kernel(size, me_ref, left_ref, left_peer_ref, right_ref, right_peer_ref, *rest):
    *outs, total = rest
    total[...] = token_sum(left_ref[...], right_ref[...]) + token_sum(
        left_peer_ref[...], right_peer_ref[...]
    )
    place_blocks(total, outs, me_ref[0], size)


def up_proj_kernel(
    size,
    me_ref,
    place_ref,
    normed_ref,
    normed_peer_ref,
    d_hidden_ref,
    d_hidden_peer_ref,
    attended_ref,
    attended_peer_ref,
    d_attn_ref,
    d_attn_peer_ref,
    *rest,
):
    *outs, natural, total = rest
    place = place_ref[0]
    core, far = place & 1, place >> 1
    tokens, width = normed_ref.shape
    quarter, half = tokens // 2, width // 2
    ff = d_hidden_ref.shape[1]
    total[:, :ff] = token_sum(normed_ref[...], d_hidden_ref[...]) + token_sum(
        normed_peer_ref[...], d_hidden_peer_ref[...]
    )
    columns = pl.ds(pl.multiple_of(far * half, 128), half)
    for ref, side in ((d_attn_ref, core), (d_attn_peer_ref, 1 - core)):
        for i in range(2):
            rows = pl.ds(pl.multiple_of((2 * i + side) * quarter, 16), quarter)
            natural[rows, :] = ref[i * quarter : (i + 1) * quarter, columns]
    for ref, side in ((attended_ref, core), (attended_peer_ref, 1 - core)):
        sums = token_sum(ref[...], natural[...])
        rows = pl.ds(pl.multiple_of(side * half, 16), half)
        total[rows, ff:] = jnp.where(core == 0, sums[:, : half // 2], sums[:, half // 2 :])
    place_blocks(total, outs, me_ref[0], size)


def qkv_sum_kernel(size, me_ref, place_ref, normed_ref, own_ref, send_ref, *rest):
    *outs, natural, total = rest
    place = place_ref[0]
    core, far = place & 1, place >> 1
    length = normed_ref.shape[0]
    quarter, half = length // 4, own_ref.shape[1] // 3
    group = half // 2
    for ref, side in ((own_ref, core), (send_ref, 1 - core)):
        for i in range(2):
            rows = pl.ds(pl.multiple_of((2 * i + side) * quarter, 16), quarter)
            natural[rows, :] = ref[i * quarter : (i + 1) * quarter, :]
    for t in range(3):
        low = natural[:, t * half : t * half + group]
        high = natural[:, t * half + group : (t + 1) * half]
        picked = jnp.where(far == 0, low.astype(f32), high.astype(f32)).astype(bf16)
        total[:, t * group : (t + 1) * group] = token_sum(normed_ref[...], picked)
    place_blocks(total, outs, me_ref[0], size)


def table_sum_kernel(
    size, me_ref, d_ref, d_peer_ref, to_ref, to_peer_ref, head_ref, head_peer_ref, more_ref, *rest
):
    *outs, total = rest
    total[...] = (
        token_sum(d_ref[...], to_ref[...])
        + token_sum(d_peer_ref[...], to_peer_ref[...])
        + head_ref[...]
        + head_peer_ref[...].astype(f32)
        + more_ref[...].astype(f32)
    )
    place_blocks(total, outs, me_ref[0], size)


def turned(block):
    rows = block.shape[0]
    one = lax.broadcasted_iota(jnp.int32, (rows, rows), 0)
    two = lax.broadcasted_iota(jnp.int32, (rows, rows), 1)
    return token_sum(block, (one == two).astype(f32).astype(bf16))


def down_out_kernel(place_ref, *refs):
    *parts, out_ref = refs
    ff = parts[0].shape[1]
    for j, part in enumerate(parts):
        rows = pl.ds(pl.multiple_of((place_ref[0] ^ j) * ff, 16), ff)
        out_ref[rows, :] = turned(part[...])


def up_out_kernel(place_ref, *refs):
    *parts, up_ref, proj_ref, stack = refs
    ff = up_ref.shape[1] // 4
    group = proj_ref.shape[1] // 4
    for j, part in enumerate(parts):
        owner = place_ref[0] ^ j
        up_ref[:, pl.ds(pl.multiple_of(owner * ff, 128), ff)] = part[:, :ff].astype(f32)
        stack[owner] = part[:, ff:].astype(f32)
    for q in range(4):
        proj_ref[:, q * group : (q + 1) * group] = stack[q]


def qkv_out_kernel(place_ref, *refs):
    *parts, out_ref, stack = refs
    width = out_ref.shape[1] // 3
    group = width // 4
    for j, part in enumerate(parts):
        stack[place_ref[0] ^ j] = part[...].astype(f32)
    for t in range(3):
        for i, q in enumerate((0, 2, 1, 3)):
            at = t * width + i * group
            out_ref[:, at : at + group] = stack[q][:, t * group : (t + 1) * group]


def pick(rows, lanes, to_lane):
    row = lax.broadcasted_iota(jnp.int32, (rows, lanes), 0)
    lane = lax.broadcasted_iota(jnp.int32, (rows, lanes), 1)
    return to_lane(row, lane).astype(f32).astype(bf16)


def table_out_kernel(
    plan, place_ref, *refs
):
    *parts, embed_ref, position_ref, class_ref, head_ref, vector_ref, stack = refs
    position_cols, embed_cols, slot_cols, head_cols = plan
    slot_at = position_cols + embed_cols
    label_at = slot_at + slot_cols
    gain_at = label_at + 2
    head_at = gain_at + 2
    for j, part in enumerate(parts):
        stack[place_ref[0] ^ j] = part[...].astype(f32)
    embed = head = slots = bias = None
    for q in range(4):
        part = stack[q].astype(bf16)
        turn = turned(part)
        position_ref[q * position_cols : (q + 1) * position_cols, :] = turn[:position_cols]
        rows = embed_ref.shape[0]
        term = back_dot(
            pick(rows, LANES, lambda row, lane: (row == lane - position_cols + q * embed_cols)
                 & (lane >= position_cols) & (lane < slot_at)),
            part,
        )
        embed = term if q == 0 else embed + term
        term = back_dot(
            pick(4 * slot_cols, LANES, lambda row, lane: (row == lane - slot_at + q * slot_cols)
                 & (lane >= slot_at) & (lane < label_at)),
            part,
        )
        slots = term if q == 0 else slots + term
        term = back_dot(
            pick(8, LANES, lambda row, lane: (row == 2) & (lane >= slot_at) & (lane < label_at)),
            part,
        )
        bias = term if q == 0 else bias + term
        term = dot(
            part,
            pick(LANES, 4 * head_cols, lambda row, lane: (lane == row - head_at + q * head_cols)
                 & (row >= head_at)),
        )
        head = term if q == 0 else head + term
    embed_ref[...] = embed
    head_ref[...] = head
    first = stack[0].astype(bf16)
    gains = back_dot(pick(8, LANES, lambda row, lane: (lane == row + gain_at) & (row < 2)), first)
    vector_ref[...] = bias + gains
    coded = back_dot(pick(8, LANES, lambda row, lane: (lane == row + label_at) & (row < 2)), first)
    label = (coded[0:1, :] * 8.0 + coded[1:2, :]).astype(jnp.int32)
    classes = class_ref.shape[0]
    hot = lax.broadcasted_iota(jnp.int32, (classes, label.shape[1]), 0) == label
    class_ref[...] = dot(hot.astype(f32).astype(bf16), slots.astype(bf16))


def shape_of(dims, dtype):
    return jax.ShapeDtypeStruct(dims, dtype)


def call(kernel, places, outs, scratch, operands, flops):
    spaces = {
        "s": pl.BlockSpec(memory_space=pltpu.SMEM),
        "v": pl.BlockSpec(memory_space=pltpu.VMEM),
        "h": pl.BlockSpec(memory_space=pl.ANY),
    }
    return pl.pallas_call(
        kernel,
        out_shape=outs,
        in_specs=[spaces[p] for p in places],
        out_specs=[spaces["v"]] * len(outs),
        scratch_shapes=scratch,
        compiler_params=pltpu.CompilerParams(vmem_limit_bytes=50 * 2**20),
        cost_estimate=pl.CostEstimate(flops=flops, bytes_accessed=8 * 2**20, transcendentals=2**20),
    )(*operands)


def shards(
    patches,
    segment_ids,
    labels,
    embed_weight,
    embed_bias,
    position_table,
    class_table,
    attn_gain,
    qkv_weight,
    proj_weight,
    mlp_gain,
    up_weight,
    down_weight,
    head_weight,
    latent_grad,
    logdet_grad,
):
    _, quarter, channels = patches.shape
    length = segment_ids.shape[1]
    width = qkv_weight.shape[0]
    hidden_width = up_weight.shape[1]
    tokens = 2 * quarter
    ff = hidden_width // 4
    count = lax.axis_size("dp")
    me = lax.axis_index("dp")
    r = lax.axis_index("narrow")
    core, far = r & 1, r >> 1
    core_id, place = core.reshape(1), r.reshape(1)
    half_width = width // 2

    def natural(mine, peers):
        a, b, c, d = mine[:quarter], mine[quarter:], peers[:quarter], peers[quarter:]
        return jnp.where(core == 0, jnp.concatenate([a, c, b, d]), jnp.concatenate([c, a, d, b]))

    def pair_order(own, other):
        return jnp.where(far == 0, jnp.concatenate([own, other]), jnp.concatenate([other, own]))

    logdet_col = logdet_grad.reshape(quarter, 1)
    coarse = lax.reduce_precision(logdet_col, 8, 7)
    fine = logdet_col - coarse
    own_in = jnp.concatenate(
        [patches[0], latent_grad[0], coarse.astype(bf16), fine.astype(bf16)], axis=1
    )
    half_in = pair_order(own_in, swap(own_in, "narrow", 2))
    patches_half = half_in[:, :channels]
    latent_cot = half_in[:, channels : 2 * channels]
    logdet_cot = half_in[:, 2 * channels :].astype(f32).sum(axis=1, keepdims=True)
    patches_all = natural(patches_half, swap(patches_half, "narrow", 1))

    segments = segment_ids[0]
    units = length // UNIT
    unit_ids = segments.reshape(units, UNIT)[:, 0]
    first_unit = jnp.sum((unit_ids[None, :] < unit_ids[:, None]).astype(jnp.int32), axis=1)
    blocks = jnp.arange(units, dtype=jnp.int32) - first_unit
    first_patch = first_unit * UNIT
    inner = jnp.arange(UNIT, dtype=jnp.int32)
    positions = (blocks[:, None] * UNIT + inner[None, :]).reshape(length)
    kept = (positions > 0)[:, None]
    shifted = jnp.concatenate([jnp.zeros_like(patches_all[:1]), patches_all[:-1]])
    previous = jnp.where(kept, shifted, jnp.zeros_like(shifted))
    position_hot = (
        positions[:, None] == jnp.arange(position_table.shape[0], dtype=jnp.int32)[None, :]
    ).astype(bf16)
    segment_hot = (
        segments[:, None] == jnp.arange(labels.shape[1], dtype=jnp.int32)[None, :]
    ).astype(bf16)
    label_hot = (labels[0][:, None] == jnp.arange(class_table.shape[0], dtype=jnp.int32)).astype(
        bf16
    )
    class_rows = dot(label_hot, class_table)
    gain_attn = attn_gain.astype(f32).reshape(1, width)
    gain_mlp = mlp_gain.astype(f32).reshape(1, width)

    sem = pltpu.SemaphoreType.DMA
    embedded, normed_one, qkv, attended = call(
        front_kernel,
        "ssssvvvvvvh",
        [
            shape_of((tokens, width), f32),
            shape_of((length, width), bf16),
            shape_of((length, 3 * half_width), bf16),
            shape_of((length, half_width), bf16),
        ],
        [pltpu.VMEM((3, width, half_width), bf16), sem((3,))],
        (
            first_patch,
            blocks,
            unit_ids,
            core_id,
            previous,
            embed_weight,
            embed_bias.astype(f32).reshape(1, width),
            position_table,
            class_rows,
            gain_attn,
            qkv_weight,
        ),
        2 * length * width * 3 * half_width,
    )
    attended_peer = swap(attended, "narrow", 1)

    slots = labels.shape[1] * count
    position_cols, embed_cols = position_table.shape[0] // 4, channels // 4
    slot_cols, head_cols = slots // 4, channels // 2
    slot_at = position_cols + embed_cols
    label_at = slot_at + slot_cols
    gain_at = label_at + 2
    head_at = gain_at + 2
    size = width // count
    compact = head_at + head_cols <= LANES and slots <= size
    lane = jnp.arange(LANES, dtype=jnp.int32)[None, :]
    columns = 2 * channels

    def head_pick(index):
        source = jnp.arange(columns, dtype=jnp.int32)[:, None]
        return (
            (lane - (LANES - head_cols) + index * head_cols == source)
            & (lane >= LANES - head_cols)
        ).astype(bf16)

    (
        latent,
        logdet,
        direct,
        normed_two,
        hidden,
        d_mlp,
        d_hidden,
        d_one,
        d_attn,
        gain_part_two,
        head_keep,
        head_send,
    ) = call(
        middle_kernel,
        "ss" + 10 * "v" + "hhh",
        [
            shape_of((tokens, channels), f32),
            shape_of((tokens, 1), f32),
            shape_of((tokens, channels), f32),
            shape_of((tokens, width), bf16),
            shape_of((2, tokens, ff), bf16),
            shape_of((tokens, width), bf16),
            shape_of((2, tokens, ff), bf16),
            shape_of((tokens, width), f32),
            shape_of((tokens, width), bf16),
            shape_of((1, width), f32),
            shape_of((width, LANES), f32),
            shape_of((width, LANES), bf16),
        ],
        [
            pltpu.VMEM((width, width), bf16),
            pltpu.VMEM((4, width, ff), bf16),
            pltpu.VMEM((4, ff, width), bf16),
            pltpu.VMEM((2, tokens, ff), bf16),
            pltpu.VMEM((2, tokens, ff), bf16),
            pltpu.VMEM((4, tokens, ff), f32),
            pltpu.VMEM((tokens, width), f32),
            pltpu.VMEM((tokens, width), bf16),
            sem((9,)),
        ],
        (
            core_id,
            place,
            embedded,
            attended,
            attended_peer,
            gain_mlp,
            head_weight[:, :channels],
            head_weight[:, channels:],
            jnp.stack([head_pick(r), head_pick(r ^ 1)]),
            patches_half,
            latent_cot,
            logdet_cot,
            proj_weight,
            up_weight,
            down_weight,
        ),
        8 * tokens * width * hidden_width,
    )

    me_id = me.reshape(1)
    aligned = size % 16 == 0 and count > 1

    def block_shapes(cols):
        if aligned:
            return [shape_of((count // 2, size, cols), bf16)] * 2
        return [shape_of((width, cols), bf16)]

    def blocks_of(outs):
        if aligned:
            return outs
        blocks = relative_blocks(outs[0], me, count)
        return blocks[: max(1, count // 2)], blocks[max(1, count // 2) :]

    def reduced(blocks):
        keep, send = blocks
        step = 1
        while send.shape[0]:
            total = keep.astype(f32) + swap(send, "dp", step).astype(f32)
            half = (total.shape[0] + 1) // 2
            keep, send = total[:half].astype(bf16), total[half:].astype(bf16)
            step *= 2
        return keep[0]

    def four(part):
        far_part = swap(part, "narrow", 2)
        return [part, swap(part, "narrow", 1), far_part, swap(far_part, "narrow", 1)]

    group = half_width // 2
    d_attn_peer = swap(d_attn, "narrow", 1)
    down_blocks = blocks_of(
        call(
            functools.partial(pair_sum_kernel, size),
            "svvvv",
            block_shapes(ff),
            [pltpu.VMEM((width, ff), f32)],
            (me_id, d_mlp, swap(d_mlp, "narrow", 1), hidden[0], swap(hidden[1], "narrow", 1)),
            4 * tokens * width * ff,
        )
    )
    up_blocks = blocks_of(
        call(
            functools.partial(up_proj_kernel, size),
            "ss" + 8 * "v",
            block_shapes(ff + group),
            [pltpu.VMEM((length, half_width), bf16), pltpu.VMEM((width, ff + group), f32)],
            (
                me_id,
                place,
                normed_two,
                swap(normed_two, "narrow", 1),
                d_hidden[0],
                swap(d_hidden[1], "narrow", 1),
                attended,
                attended_peer,
                d_attn,
                d_attn_peer,
            ),
            4 * tokens * width * (ff + half_width),
        )
    )
    qkv, d_attn_peer, down_blocks, up_blocks = lax.optimization_barrier(
        (qkv, d_attn_peer, down_blocks, up_blocks)
    )
    d_qkv, d_qkv_send = call(
        back_attention_kernel,
        "ss" + 4 * "v",
        [shape_of((tokens, 3 * half_width), bf16)] * 2,
        [
            pltpu.VMEM((length, half_width), bf16),
            pltpu.VMEM((length, 2 * HD), f32),
            pltpu.VMEM((length, 2 * HD), f32),
        ],
        (first_patch, core_id, qkv, d_attn, d_attn_peer, proj_weight),
        10 * length * length * half_width,
    )
    qkv_blocks = blocks_of(
        call(
            functools.partial(qkv_sum_kernel, size),
            "ssvvv",
            block_shapes(3 * group),
            [pltpu.VMEM((length, 3 * half_width), bf16), pltpu.VMEM((width, 3 * group), f32)],
            (me_id, place, normed_one, d_qkv, d_qkv_send),
            2 * length * width * 3 * group,
        )
    )
    d_qkv_peer = swap(d_qkv_send, "narrow", 1)
    d_qkv_peer, qkv_blocks = lax.optimization_barrier((d_qkv_peer, qkv_blocks))
    [d_embed] = call(
        back_front_kernel,
        "s" + 7 * "v",
        [shape_of((tokens + EXTRA, width), bf16)],
        [],
        (core_id, d_qkv, d_qkv_peer, embedded, d_one, gain_attn, gain_part_two, qkv_weight),
        6 * tokens * width * width,
    )
    d_embed_peer = swap(d_embed, "narrow", 1)

    def quarter_of(array, cols):
        return lax.dynamic_slice_in_dim(array, r * cols, cols, 1)

    image = segments[:, None] + me * labels.shape[1]
    slot_hot = (image == r * slot_cols + jnp.arange(slot_cols, dtype=jnp.int32)[None, :]).astype(
        bf16
    )
    to_columns = jnp.concatenate(
        [
            quarter_of(position_hot, position_cols),
            quarter_of(previous, embed_cols),
            slot_hot if compact else jnp.zeros((length, 0), bf16),
        ],
        axis=1,
    )
    to_columns = jnp.pad(to_columns, ((0, 0), (0, LANES - to_columns.shape[1])))
    gain_col = gain_at if compact else slot_at
    extra_row = jnp.arange(EXTRA, dtype=jnp.int32)[:, None]
    gain_rows = ((lane == gain_col + extra_row % 2) & (extra_row < 4)).astype(bf16)

    def half_rows(full, side):
        return jnp.concatenate(
            [
                lax.dynamic_slice_in_dim(full, side * quarter, quarter, 0),
                lax.dynamic_slice_in_dim(full, (side + 2) * quarter, quarter, 0),
                gain_rows,
            ]
        )

    if compact:
        slot_row = jnp.arange(size, dtype=jnp.int32)
        mine = slot_row // labels.shape[1] == me
        label = jnp.where(mine, labels[0][slot_row % labels.shape[1]], 0)[:, None]
        code = jnp.where(lane == label_at, label // 8, jnp.where(lane == label_at + 1, label % 8, 0))
        more = jnp.tile(code.astype(bf16), (count, 1))
    else:
        more = jnp.zeros((width, LANES), bf16)
    table_outs = call(
        functools.partial(table_sum_kernel, size),
        "s" + 7 * "v",
        block_shapes(LANES),
        [pltpu.VMEM((width, LANES), f32)],
        (
            me_id,
            d_embed,
            d_embed_peer,
            half_rows(to_columns, core),
            half_rows(to_columns, 1 - core),
            head_keep,
            swap(head_send, "narrow", 1),
            more,
        ),
        2 * length * width * LANES,
    )
    d_embed_all = natural(d_embed[:tokens], d_embed_peer[:tokens])

    d_previous = jnp.where(kept, back_dot(d_embed_all, embed_weight), 0.0)
    carried = jnp.concatenate([d_previous[1:], jnp.zeros_like(d_previous[:1])])
    carried = lax.dynamic_slice_in_dim(carried, r * quarter, quarter, 0)

    def own_quarter(half):
        return lax.dynamic_slice_in_dim(half, far * quarter, quarter, 0)

    latent_out = own_quarter(latent)
    logdet_out = own_quarter(logdet)[:, 0]
    patches_grad = own_quarter(direct) + carried

    [down_grad] = call(
        down_out_kernel,
        "svvvv",
        [shape_of((hidden_width, size), f32)],
        [],
        (place, *four(reduced(down_blocks))),
        0,
    )
    up_grad, proj_grad = call(
        up_out_kernel,
        "svvvv",
        [shape_of((size, hidden_width), f32), shape_of((size, width), f32)],
        [pltpu.VMEM((4, size, group), f32)],
        (place, *four(reduced(up_blocks))),
        0,
    )
    [qkv_grad] = call(
        qkv_out_kernel,
        "svvvv",
        [shape_of((size, 3 * width), f32)],
        [pltpu.VMEM((4, size, 3 * group), f32)],
        (place, *four(reduced(qkv_blocks))),
        0,
    )
    if compact:
        embed_grad, position_grad, class_grad, head_grad, vectors = call(
            functools.partial(
                table_out_kernel, (position_cols, embed_cols, slot_cols, head_cols)
            ),
            "svvvv",
            [
                shape_of((channels, size), f32),
                shape_of((position_table.shape[0], size), f32),
                shape_of((class_table.shape[0], size), f32),
                shape_of((size, columns), f32),
                shape_of((8, size), f32),
            ],
            [pltpu.VMEM((4, size, LANES), f32)],
            (place, *four(reduced(blocks_of(table_outs)))),
            0,
        )
        attngain_grad, mlpgain_grad, bias_grad = vectors[0], vectors[1], vectors[2]
    else:
        segment_part = token_sum(d_embed_all, segment_hot)
        class_part = dot(segment_part.astype(bf16), label_hot).astype(bf16)
        class_cols = class_table.shape[0] // 4
        keep, send = blocks_of(table_outs)
        more_blocks = relative_blocks(
            jnp.concatenate(
                [
                    lax.dynamic_slice_in_dim(class_part, r * class_cols, class_cols, 1),
                    jnp.sum(segment_part, axis=1, keepdims=True).astype(bf16),
                ],
                axis=1,
            ),
            me,
            count,
        )
        near = keep.shape[0]
        keep = jnp.concatenate([keep, more_blocks[:near]], axis=2)
        send = jnp.concatenate([send, more_blocks[near:]], axis=2)
        parts = jnp.stack(four(reduced((keep, send)))).astype(f32)
        parts = [lax.dynamic_index_in_dim(parts, r ^ i, 0, keepdims=False) for i in range(4)]

        def joined(start, cols):
            return jnp.concatenate([part[:, start : start + cols] for part in parts], axis=1)

        position_grad = joined(0, position_cols).T
        embed_grad = joined(position_cols, embed_cols).T
        class_grad = joined(LANES, class_cols).T
        head_grad = joined(LANES - head_cols, head_cols)
        attngain_grad = parts[0][:, gain_col]
        mlpgain_grad = parts[0][:, gain_col + 1]
        bias_grad = parts[0][:, LANES + class_cols]
    return (
        latent_out[None],
        logdet_out[None],
        patches_grad[None],
        embed_grad,
        bias_grad,
        position_grad,
        class_grad,
        attngain_grad,
        qkv_grad,
        proj_grad,
        mlpgain_grad,
        up_grad,
        down_grad,
        head_grad,
    )


def solution(mesh):
    return jax.shard_map(
        shards,
        mesh=mesh,
        in_specs=(
            P("dp", "narrow", None),
            P("dp", None),
            P("dp", None),
            P(),
            P(),
            P(),
            P(),
            P(),
            P(),
            P(),
            P(),
            P(),
            P(),
            P(),
            P("dp", "narrow", None),
            P("dp", "narrow"),
        ),
        out_specs=(
            P("dp", "narrow", None),
            P("dp", "narrow"),
            P("dp", "narrow", None),
            P(None, "dp"),
            P("dp"),
            P(None, "dp"),
            P(None, "dp"),
            P("dp"),
            P("dp", None),
            P("dp", None),
            P("dp"),
            P("dp", None),
            P(None, "dp"),
            P("dp", None),
        ),
        check_vma=False,
    )
```

```python
import functools
import math

import jax
import jax.numpy as jnp
from jax import lax
from jax.experimental import pallas as pl
from jax.experimental.pallas import tpu as pltpu
from jax.sharding import PartitionSpec as P

HD = 64
UNIT = 64
BIG = 256
TILE = 128
EXTRA = 16
LANES = 128
bf16, f32 = jnp.bfloat16, jnp.float32
epsilon = 1e-05
masked_score = -1e30


def dot(left, right):
    return jnp.dot(left, right, preferred_element_type=f32)


def token_sum(left, right):
    return lax.dot_general(left, right, (((0,), (0,)), ((), ())), preferred_element_type=f32)


def back_dot(grads, weight):
    return lax.dot_general(grads, weight, (((1,), (1,)), ((), ())), preferred_element_type=f32)


def swap(value, axis, step, turn=0):
    count = lax.axis_size(axis)
    turned = [(i + turn) % count for i in range(count)]
    return lax.ppermute(value, axis, [(i, i ^ step) for i in turned])


def normalised(values):
    center = jnp.mean(values, axis=-1, keepdims=True)
    offsets = values - center
    inverse = lax.rsqrt(jnp.mean(offsets * offsets, axis=-1, keepdims=True) + epsilon)
    return offsets * inverse, inverse


def norm_back(grads, gain, normed, inverse):
    e = grads * gain
    mean_e = jnp.mean(e, axis=-1, keepdims=True)
    mean_en = jnp.mean(e * normed, axis=-1, keepdims=True)
    return inverse * (e - mean_e - normed * mean_en)


def halving_steps(count, far_first=False):
    steps = [1 << i for i in range(count.bit_length() - 1)]
    if far_first and len(steps) > 1:
        steps[:2] = steps[1], steps[0]
    return steps


def block_order(steps):
    order = [0]
    for step in reversed(steps):
        order = order + [j ^ step for j in order]
    return order


def relative_blocks(grad, me, steps):
    order = block_order(steps)
    size = grad.shape[0] // len(order)
    return jnp.stack([lax.dynamic_slice_in_dim(grad, (me ^ j) * size, size, 0) for j in order])


UNITS_AT = 2


def unit_firsts(ids_ref, units):
    firsts = [jnp.int32(0)]
    for u in range(1, units):
        same = ids_ref[UNITS_AT + u] == ids_ref[UNITS_AT + u - 1]
        firsts.append(jnp.where(same, firsts[-1], u))
    return firsts


def allowed_bias(row_start, firsts):
    begin, end = window_of(row_start)
    shape = (TILE, end - begin)
    row = lax.broadcasted_iota(jnp.int32, shape, 0)
    key = lax.broadcasted_iota(jnp.int32, shape, 1) + begin
    unit = row_start // UNIT
    first = jnp.where(row < UNIT, firsts[unit] * UNIT, firsts[unit + 1] * UNIT)
    return jnp.where((key >= first) & (key <= row + row_start), 0.0, masked_score)


def stacked(block, masks):
    return jnp.concatenate([block * masks[0], block * masks[1]])


def head_masks():
    lane = lax.broadcasted_iota(jnp.int32, (1, 2 * HD), 1)
    low = (lane < HD).astype(f32)
    return low.astype(bf16), (1.0 - low).astype(bf16)


def window_of(start):
    return max(0, start - BIG), start + TILE


def pick(rows, lanes, to_lane):
    row = lax.broadcasted_iota(jnp.int32, (rows, lanes), 0)
    lane = lax.broadcasted_iota(jnp.int32, (rows, lanes), 1)
    return to_lane(row, lane).astype(f32).astype(bf16)


def base_kernel(
    ids_ref, vector_ref, class_hbm, position_hbm, base_ref, allowed_ref, position_ref, class_ref, image_rows, sems
):
    tables = [
        pltpu.make_async_copy(class_hbm, class_ref, sems.at[0]),
        pltpu.make_async_copy(position_hbm, position_ref, sems.at[1]),
    ]
    for table in tables:
        table.start()
    length = base_ref.shape[0]
    units = length // UNIT
    firsts = unit_firsts(ids_ref, units)
    for start in range(0, length, TILE):
        begin, end = window_of(start)
        allowed_ref[start : start + TILE, : end - begin] = allowed_bias(start, firsts)
    shape = (image_rows.shape[0], class_ref.shape[0])
    row = lax.broadcasted_iota(jnp.int32, shape, 0)
    label = jnp.full(shape, -1, jnp.int32)
    for s in range(ids_ref.shape[0] - UNITS_AT - units):
        label = jnp.where(row == s, ids_ref[UNITS_AT + units + s], label)
    hot = (lax.broadcasted_iota(jnp.int32, shape, 1) == label).astype(f32).astype(bf16)
    tables[0].wait()
    image_rows[...] = dot(hot, class_ref[...]) + vector_ref[0:1, :].astype(f32)
    tables[1].wait()
    for u in range(units):
        block = u - firsts[u]
        table = position_ref[pl.ds(pl.multiple_of(block * UNIT, UNIT), UNIT), :]
        image = image_rows[pl.ds(ids_ref[UNITS_AT + u], 1), :]
        base_ref[u * UNIT : (u + 1) * UNIT, :] = table.astype(f32) + image


def front_kernel(
    ids_ref,
    part_0_ref,
    part_1_ref,
    part_2_ref,
    part_3_ref,
    base_ref,
    allowed,
    vector_ref,
    embed_ref,
    weight_ref,
    embedded_ref,
    normed_ref,
    qkv_ref,
    attended_ref,
    own_weight,
    patch_rows,
    sems,
):
    length, width = normed_ref.shape
    half = width // 2
    quarter = length // 4
    channels = embed_ref.shape[0]
    place = ids_ref[1]
    core = place & 1
    copies = []
    for t in range(3):
        start = pl.multiple_of(t * width + core * half, 128)
        copies.append(
            pltpu.make_async_copy(weight_ref.at[:, pl.ds(start, half)], own_weight.at[t], sems.at[t])
        )
        copies[-1].start()
    firsts = unit_firsts(ids_ref, length // UNIT)
    starts = range(0, length, TILE)
    patch_rows[0:8, :] = jnp.zeros((8, width), f32)
    for j, part in enumerate((part_0_ref, part_1_ref, part_2_ref, part_3_ref)):
        at = pl.multiple_of((place ^ j) * quarter + 8, 8)
        patch_rows[pl.ds(at, quarter), :] = token_sum(part[:channels, :], embed_ref[...])
    gain = vector_ref[1:2, :].astype(f32)
    inner = lax.broadcasted_iota(jnp.int32, (UNIT, width), 0)
    for u in range(length // UNIT):
        rows = slice(u * UNIT, (u + 1) * UNIT)
        before = patch_rows[u * UNIT + 7 : u * UNIT + 7 + UNIT, :]
        before = jnp.where((inner == 0) & (firsts[u] == u), 0.0, before)
        values = before + base_ref[rows, :]
        q = u * UNIT // quarter
        inside = (q >> 1) * quarter + u * UNIT - q * quarter

        @pl.when(core == (q & 1))
        def _():
            embedded_ref[pl.ds(inside, UNIT), :] = values

        normed_ref[rows, :] = (normalised(values)[0] * gain).astype(bf16)
    for t in range(3):
        copies[t].wait()
        qkv_ref[:, t * half : (t + 1) * half] = dot(normed_ref[...], own_weight[t]).astype(bf16)
    masks = head_masks()
    low_lanes = lax.broadcasted_iota(jnp.int32, (TILE, 2 * HD), 1) < HD

    def pair_step(pair, carry):
        lanes = [pl.ds(pl.multiple_of(t * half + pair * 2 * HD, 128), 2 * HD) for t in range(3)]
        scores = []
        for start in starts:
            begin, end = window_of(start)
            q = stacked(qkv_ref[start : start + TILE, lanes[0]], masks)
            scores.append(back_dot(q, qkv_ref[begin:end, lanes[1]]))
        raised, totals = [], []
        for start, block in zip(starts, scores):
            begin, end = window_of(start)
            bias = allowed[start : start + TILE, : end - begin]
            masked = block * (1.0 / math.sqrt(HD)) + jnp.concatenate([bias, bias])
            power = jnp.exp(masked - jnp.max(masked, axis=-1, keepdims=True))
            raised.append(power.astype(bf16))
            totals.append(1.0 / jnp.sum(power, axis=-1, keepdims=True))
        for start, power, inverse in zip(starts, raised, totals):
            begin, end = window_of(start)
            out = dot(power, qkv_ref[begin:end, lanes[2]]) * inverse
            attended_ref[start : start + TILE, lanes[0]] = jnp.where(
                low_lanes, out[:TILE], out[TILE:]
            ).astype(bf16)
        return carry

    lax.fori_loop(0, half // (2 * HD), pair_step, 0, unroll=True)


def back_attention_kernel(
    ids_ref,
    qkv_ref,
    mine_ref,
    peer_ref,
    proj_ref,
    allowed,
    own_ref,
    send_ref,
    mixed,
    grads,
):
    length = qkv_ref.shape[0]
    half = qkv_ref.shape[1] // 3
    quarter = length // 4
    core = ids_ref[1] & 1
    proj = proj_ref[pl.ds(pl.multiple_of(core * half, 128), half), :]
    for ref, side in ((mine_ref, core), (peer_ref, 1 - core)):
        product = back_dot(ref[...], proj).astype(bf16)
        for i in range(2):
            rows = pl.ds(pl.multiple_of((2 * i + side) * quarter, 16), quarter)
            mixed[rows, :] = product[i * quarter : (i + 1) * quarter]
    masks = head_masks()
    low_lanes = lax.broadcasted_iota(jnp.int32, (TILE, 2 * HD), 1) < HD
    scale = 1.0 / math.sqrt(HD)
    starts = range(0, length, TILE)

    def pair_step(pair, carry):
        lanes = [pl.ds(pl.multiple_of(t * half + pair * 2 * HD, 128), 2 * HD) for t in range(3)]
        queries, outer, scores, d_weights = [], [], [], []
        for start in starts:
            begin, end = window_of(start)
            queries.append(stacked(qkv_ref[start : start + TILE, lanes[0]], masks))
            outer.append(stacked(mixed[start : start + TILE, lanes[0]], masks))
            scores.append(back_dot(queries[-1], qkv_ref[begin:end, lanes[1]]))
            d_weights.append(back_dot(outer[-1], qkv_ref[begin:end, lanes[2]]))
        weights, d_scores = [], []
        for start, block, d_block in zip(starts, scores, d_weights):
            begin, end = window_of(start)
            bias = allowed[start : start + TILE, : end - begin]
            masked = block * scale + jnp.concatenate([bias, bias])
            power = jnp.exp(masked - jnp.max(masked, axis=-1, keepdims=True))
            weight = power * (1.0 / jnp.sum(power, axis=-1, keepdims=True))
            centre = jnp.sum(weight * d_block, axis=-1, keepdims=True)
            weights.append(weight.astype(bf16))
            d_scores.append((weight * (d_block - centre)).astype(bf16))
        for i, start in enumerate(starts):
            begin, end = window_of(start)
            out = dot(d_scores[i], qkv_ref[begin:end, lanes[1]])
            grads[start : start + TILE, lanes[0]] = (
                jnp.where(low_lanes, out[:TILE], out[TILE:]) * scale
            ).astype(bf16)
        d_keys = [token_sum(d, q) for d, q in zip(d_scores, queries)]
        d_values = [token_sum(w, o) for w, o in zip(weights, outer)]
        for at in starts:
            for t, sums, factor in ((1, d_keys, scale), (2, d_values, 1.0)):
                total = None
                for start, block in zip(starts, sums):
                    begin, end = window_of(start)
                    if begin <= at < end:
                        term = block[at - begin : at - begin + TILE]
                        total = term if total is None else total + term
                grads[at : at + TILE, lanes[t]] = (total * factor).astype(bf16)
        return carry

    lax.fori_loop(0, half // (2 * HD), pair_step, 0, unroll=True)
    for ref, side in ((own_ref, core), (send_ref, 1 - core)):
        for i in range(2):
            rows = pl.ds(pl.multiple_of((2 * i + side) * quarter, 16), quarter)
            ref[i * quarter : (i + 1) * quarter, :] = grads[rows, :]


def middle_kernel(
    ids_ref,
    embedded_ref,
    own_ref,
    peer_ref,
    gain_ref,
    head_weight_ref,
    near_ref,
    far_ref,
    proj_hbm,
    up_hbm,
    down_hbm,
    latent_ref,
    logdet_ref,
    direct_ref,
    normed_ref,
    hidden_ref,
    d_mlp_ref,
    d_hidden_ref,
    d_one_ref,
    d_attn_ref,
    gain_part_ref,
    head_ref,
    head_send_ref,
    proj,
    up,
    down,
    hidden_rest,
    d_hidden_rest,
    slope,
    stream,
    low,
    sems,
):
    tokens, width = embedded_ref.shape
    quarter = tokens // 2
    half = width // 2
    ff = up.shape[2]
    place = ids_ref[1]
    core, far = place & 1, place >> 1
    channels = latent_ref.shape[0]
    copies = [pltpu.make_async_copy(proj_hbm, proj, sems.at[0])]
    copies[0].start()
    for j in range(4):
        columns = pl.ds(pl.multiple_of((place ^ j) * ff, 128), ff)
        copies.append(pltpu.make_async_copy(up_hbm.at[:, columns], up.at[j], sems.at[1 + j]))
        copies[-1].start()
    for j in range(4):
        rows = pl.ds(pl.multiple_of((place ^ j) * ff, 128), ff)
        copies.append(pltpu.make_async_copy(down_hbm.at[rows, :], down.at[j], sems.at[5 + j]))
        copies[-1].start()
    copies[0].wait()
    gain = gain_ref[2:3, :].astype(f32)
    for i in range(2):
        source = pl.ds(pl.multiple_of((2 * i + core) * quarter, 16), quarter)
        rows = slice(i * quarter, (i + 1) * quarter)
        values = embedded_ref[rows, :]
        for ref, side in ((own_ref, core), (peer_ref, 1 - core)):
            weight = proj[pl.ds(pl.multiple_of(side * half, 128), half), :]
            values += dot(ref[source, :], weight)
        stream[rows, :] = values
        normed_ref[rows, :] = (normalised(values)[0] * gain).astype(bf16)
    for j in range(4):
        copies[1 + j].wait()

        pre = dot(normed_ref[...], up[j])
        cdf = 0.5 * (1.0 + lax.erf(pre * math.sqrt(0.5)))
        density = jnp.exp(-0.5 * pre * pre) * (1.0 / math.sqrt(2 * math.pi))
        slope[j] = cdf + pre * density
        value = (pre * cdf).astype(bf16)
        if j < 2:
            hidden_ref[j] = value
        else:
            hidden_rest[j - 2] = value
    total = stream[...]
    for j in range(4):
        copies[5 + j].wait()
        total += dot(hidden_ref[j] if j < 2 else hidden_rest[j - 2], down[j])
    low[...] = total.astype(bf16)
    head_sums = [jnp.zeros(head_ref.shape, f32)] * 2
    head_cols = channels // 2
    lane_at = LANES - head_cols
    for i in range(2):
        rows = slice(i * quarter, (i + 1) * quarter)
        part = jnp.where(far == i, near_ref[...].astype(f32), far_ref[...].astype(f32))
        patches, cot = part[:channels], part[channels : 2 * channels]
        logdet_cot = jnp.sum(part[2 * channels :], axis=0, keepdims=True)
        head_out = back_dot(head_weight_ref[...], low[rows, :])
        mean_shift, logscale = head_out[:channels], head_out[channels:]
        factor = jnp.exp(-logscale)
        latent = (patches - mean_shift) * factor
        direct = cot * factor

        @pl.when(far == i)
        def _():
            latent_ref[...] = latent
            logdet_ref[...] = -jnp.sum(logscale, axis=0, keepdims=True)
            direct_ref[...] = direct

        d_head = jnp.concatenate([-direct, -cot * latent - logdet_cot]).astype(bf16)
        d_two = token_sum(d_head, head_weight_ref[...])
        d_one_ref[rows, :] = d_two
        d_mlp_ref[rows, :] = d_two.astype(bf16)
        for k, index in enumerate((place, place ^ 1)):
            chosen = pick(
                2 * channels,
                LANES,
                lambda row, lane: (lane - lane_at + index * head_cols == row) & (lane >= lane_at),
            )
            columns = token_sum(d_head, chosen).astype(bf16)
            head_sums[k] += token_sum(low[rows, :], columns)
    head_ref[...] = head_sums[0]
    head_send_ref[...] = head_sums[1].astype(bf16)
    for j in range(4):
        value = (back_dot(d_mlp_ref[...], down[j]) * slope[j]).astype(bf16)
        if j < 2:
            d_hidden_ref[j] = value
        else:
            d_hidden_rest[j - 2] = value
    for i in range(2):
        rows = slice(i * quarter, (i + 1) * quarter)
        grads = jnp.zeros((quarter, width), f32)
        for j in range(4):
            value = d_hidden_ref[j, rows, :] if j < 2 else d_hidden_rest[j - 2, rows, :]
            grads += back_dot(value, up[j])
        n, inverse = normalised(stream[rows, :])
        part = jnp.sum(grads * n, axis=0, keepdims=True)
        gain_part_ref[...] = part if i == 0 else gain_part_ref[...] + part
        d_one = d_one_ref[rows, :] + norm_back(grads, gain, n, inverse)
        d_one_ref[rows, :] = d_one
        d_attn_ref[rows, :] = d_one.astype(bf16)


def back_front_kernel(
    ids_ref,
    own_ref,
    peer_ref,
    embedded_ref,
    d_one_ref,
    gain_ref,
    part_ref,
    weight_ref,
    d_embed_ref,
):
    tokens, width = embedded_ref.shape
    half = width // 2
    core = ids_ref[1] & 1
    gain = gain_ref[1:2, :].astype(f32)
    rows_step = tokens // 2
    for i in range(2):
        rows = slice(i * rows_step, (i + 1) * rows_step)
        grads = jnp.zeros((rows_step, width), f32)
        for ref, side in ((own_ref, core), (peer_ref, 1 - core)):
            for t in range(3):
                columns = pl.ds(pl.multiple_of(t * width + side * half, 128), half)
                grads += back_dot(ref[rows, t * half : (t + 1) * half], weight_ref[:, columns])
        n, inverse = normalised(embedded_ref[rows, :])
        part = jnp.sum(grads * n, axis=0, keepdims=True)
        total = part if i == 0 else total + part
        d_embed_ref[rows, :] = (d_one_ref[rows, :] + norm_back(grads, gain, n, inverse)).astype(
            bf16
        )
    row = lax.broadcasted_iota(jnp.int32, (EXTRA, width), 0)
    both = jnp.where(row % 2 == 0, total, part_ref[...])
    coarse = both.astype(bf16).astype(f32)
    rest = jnp.where(row < 2, coarse, jnp.where(row < 4, both - coarse, 0.0))
    d_embed_ref[tokens : tokens + EXTRA, :] = rest.astype(bf16)


def place_blocks(total, outs, me, size, steps):
    if len(outs) == 1:
        outs[0][...] = total[...].astype(bf16)
        return
    keep, send = outs
    for k, j in enumerate(block_order(steps)):
        block = total[pl.ds(pl.multiple_of((me ^ j) * size, 16), size), :].astype(bf16)
        if k < keep.shape[0]:
            keep[k] = block
        else:
            send[k - keep.shape[0]] = block


def pair_sum_kernel(size, steps, ids_ref, left_ref, left_peer_ref, right_ref, right_peer_ref, *rest):
    *outs, total = rest
    total[...] = token_sum(left_ref[...], right_ref[...]) + token_sum(
        left_peer_ref[...], right_peer_ref[...]
    )
    place_blocks(total, outs, ids_ref[0], size, steps)


def up_proj_kernel(
    size,
    steps,
    ids_ref,
    normed_ref,
    normed_peer_ref,
    d_hidden_ref,
    d_hidden_peer_ref,
    attended_ref,
    attended_peer_ref,
    d_attn_ref,
    d_attn_peer_ref,
    *rest,
):
    *outs, natural, total = rest
    place = ids_ref[1]
    core, far = place & 1, place >> 1
    tokens, width = normed_ref.shape
    quarter, half = tokens // 2, width // 2
    ff = d_hidden_ref.shape[1]
    total[:, :ff] = token_sum(normed_ref[...], d_hidden_ref[...]) + token_sum(
        normed_peer_ref[...], d_hidden_peer_ref[...]
    )
    columns = pl.ds(pl.multiple_of(far * half, 128), half)
    for ref, side in ((d_attn_ref, core), (d_attn_peer_ref, 1 - core)):
        for i in range(2):
            rows = pl.ds(pl.multiple_of((2 * i + side) * quarter, 16), quarter)
            natural[rows, :] = ref[i * quarter : (i + 1) * quarter, columns]
    for ref, side in ((attended_ref, core), (attended_peer_ref, 1 - core)):
        sums = token_sum(ref[...], natural[...])
        rows = pl.ds(pl.multiple_of(side * half, 16), half)
        total[rows, ff:] = jnp.where(core == 0, sums[:, : half // 2], sums[:, half // 2 :])
    place_blocks(total, outs, ids_ref[0], size, steps)


def qkv_sum_kernel(size, steps, ids_ref, normed_ref, own_ref, send_ref, *rest):
    *outs, natural, total = rest
    place = ids_ref[1]
    core, far = place & 1, place >> 1
    length = normed_ref.shape[0]
    quarter, half = length // 4, own_ref.shape[1] // 3
    group = half // 2
    for ref, side in ((own_ref, core), (send_ref, 1 - core)):
        for i in range(2):
            rows = pl.ds(pl.multiple_of((2 * i + side) * quarter, 16), quarter)
            natural[rows, :] = ref[i * quarter : (i + 1) * quarter, :]
    for t in range(3):
        low = natural[:, t * half : t * half + group]
        high = natural[:, t * half + group : (t + 1) * half]
        picked = jnp.where(far == 0, low.astype(f32), high.astype(f32)).astype(bf16)
        total[:, t * group : (t + 1) * group] = token_sum(normed_ref[...], picked)
    place_blocks(total, outs, ids_ref[0], size, steps)


def table_sum_kernel(
    size,
    steps,
    plan,
    ids_ref,
    d_ref,
    d_peer_ref,
    part_0_ref,
    part_1_ref,
    part_2_ref,
    part_3_ref,
    head_ref,
    head_peer_ref,
    direct_ref,
    embed_ref,
    *rest,
):
    *outs, patches_ref, before_rows, to_own, to_peer, following, total = rest
    position_cols, embed_cols, slot_cols = plan
    slot_at = position_cols + embed_cols
    label_at = slot_at + slot_cols
    gain_at = label_at + 2
    me, place = ids_ref[0], ids_ref[1]
    core, far = place & 1, place >> 1
    channels, quarter = direct_ref.shape
    tokens = 2 * quarter
    length = 2 * tokens
    units = length // UNIT
    labels_at = UNITS_AT + units
    images = ids_ref.shape[0] - labels_at
    parts = (part_0_ref, part_1_ref, part_2_ref, part_3_ref)
    chosen = pick(
        part_0_ref.shape[0],
        LANES,
        lambda row, lane: (row == lane - position_cols + place * embed_cols)
        & (lane >= position_cols)
        & (lane < slot_at),
    )
    before_rows[0:8, :] = jnp.zeros((8, LANES), f32)
    for j, part in enumerate(parts):
        at = pl.multiple_of((place ^ j) * quarter + 8, 8)
        before_rows[pl.ds(at, quarter), :] = token_sum(part[...], chosen)
    firsts = unit_firsts(ids_ref, units)
    row = lax.broadcasted_iota(jnp.int32, (UNIT, LANES), 0)
    lane = lax.broadcasted_iota(jnp.int32, (UNIT, LANES), 1)
    for u in range(length // UNIT):
        block = u - firsts[u]
        before = before_rows[u * UNIT + 7 : u * UNIT + 7 + UNIT, :]
        before = jnp.where((row == 0) & (block == 0), 0.0, before)
        position = lane + place * position_cols == row + block * UNIT
        slot = lane - slot_at + place * slot_cols == me * images + ids_ref[UNITS_AT + u]
        ones = ((lane < position_cols) & position) | (
            (lane >= slot_at) & (lane < label_at) & slot
        )
        value = jnp.where(ones, 1.0, before).astype(bf16)
        q = u * UNIT // quarter
        inside = (q >> 1) * quarter + u * UNIT - q * quarter

        @pl.when(core == (q & 1))
        def _():
            to_own[inside : inside + UNIT, :] = value

        @pl.when(core != (q & 1))
        def _():
            to_peer[inside : inside + UNIT, :] = value

    gain_rows = pick(EXTRA, LANES, lambda row, lane: (lane == gain_at + row % 2) & (row < 4))
    to_own[tokens:, :] = gain_rows
    to_peer[tokens:, :] = gain_rows
    total[...] = (
        token_sum(d_ref[...], to_own[...])
        + token_sum(d_peer_ref[...], to_peer[...])
        + head_ref[...]
        + head_peer_ref[...].astype(f32)
    )
    if slot_cols:
        row = lax.broadcasted_iota(jnp.int32, (size, LANES), 0)
        lane = lax.broadcasted_iota(jnp.int32, (size, LANES), 1)
        label = jnp.zeros((size, LANES), jnp.int32)
        for s in range(images):
            label = jnp.where(row == me * images + s, ids_ref[labels_at + s], label)
        code = jnp.where(
            lane == label_at, label >> 3, jnp.where(lane == label_at + 1, label & 7, 0)
        ).astype(f32)
        for b in range(total.shape[0] // size):
            total[b * size : (b + 1) * size, :] += code
    place_blocks(total, outs, me, size, steps)
    following[:quarter, :] = d_ref[pl.ds(pl.multiple_of(far * quarter, 16), quarter), :].astype(f32)
    at = pl.multiple_of(((place + 1) >> 1) * quarter, 16)
    following[quarter:, :] = d_peer_ref[pl.ds(at, EXTRA), :].astype(f32)
    row = lax.broadcasted_iota(jnp.int32, (quarter, following.shape[1]), 0)
    dropped = (row == quarter - 1) & (place == 3)
    for w in range(1, quarter // UNIT + 1):
        u = jnp.minimum(place * (quarter // UNIT) + w, units - 1)
        opens = ids_ref[UNITS_AT + u] != ids_ref[UNITS_AT + u - 1]
        dropped = dropped | ((row == w * UNIT - 1) & opens)
    shifted = jnp.where(dropped, 0.0, following[1 : quarter + 1, :]).astype(bf16)
    patches_ref[...] = direct_ref[...] + back_dot(embed_ref[...], shifted)


def down_out_kernel(ids_ref, *refs):
    *parts, out_ref = refs
    ff = parts[0].shape[1]
    for j, part in enumerate(parts):
        at = pl.multiple_of((ids_ref[1] ^ j) * ff, 128)
        out_ref[:, pl.ds(at, ff)] = part[...].astype(f32)


def up_out_kernel(ids_ref, *refs):
    *parts, up_ref, proj_ref, stack = refs
    ff = up_ref.shape[1] // 4
    group = proj_ref.shape[1] // 4
    for j, part in enumerate(parts):
        owner = ids_ref[1] ^ j
        up_ref[:, pl.ds(pl.multiple_of(owner * ff, 128), ff)] = part[:, :ff].astype(f32)
        stack[owner] = part[:, ff:].astype(f32)
    for q in range(4):
        proj_ref[:, q * group : (q + 1) * group] = stack[q]


def qkv_out_kernel(ids_ref, *refs):
    *parts, out_ref, stack = refs
    width = out_ref.shape[1] // 3
    group = width // 4
    for j, part in enumerate(parts):
        stack[ids_ref[1] ^ j] = part[...].astype(f32)
    for t in range(3):
        for i, q in enumerate((0, 2, 1, 3)):
            at = t * width + i * group
            out_ref[:, at : at + group] = stack[q][:, t * group : (t + 1) * group]


def table_out_kernel(plan, ids_ref, *refs):
    *parts, embed_ref, position_ref, class_ref, head_ref, gain_one_ref, gain_two_ref, bias_ref, stack = refs
    position_cols, embed_cols, slot_cols, head_cols = plan
    slot_at = position_cols + embed_cols
    label_at = slot_at + slot_cols
    gain_at = label_at + 2
    head_at = LANES - head_cols
    for j, part in enumerate(parts):
        stack[ids_ref[1] ^ j] = part[...].astype(f32)
    embed = position = head = slots = bias = None

    def added(total, term):
        return term if total is None else total + term

    for q in range(4):
        part = stack[q].astype(bf16)

        def placed(start, cols):
            return pick(
                LANES,
                4 * cols,
                lambda row, lane: (lane == row - start + q * cols)
                & (row >= start)
                & (row < start + cols),
            )

        position = added(position, dot(part, placed(0, position_cols)))
        head = added(head, dot(part, placed(head_at, head_cols)))
        slots = added(slots, dot(part, placed(slot_at, slot_cols)))
        chosen = pick(
            embed_ref.shape[0],
            LANES,
            lambda row, lane: (row == lane - position_cols + q * embed_cols)
            & (lane >= position_cols)
            & (lane < slot_at),
        )
        embed = added(embed, back_dot(chosen, part))
        chosen = pick(
            8, LANES, lambda row, lane: (row == 0) & (lane >= slot_at) & (lane < label_at)
        )
        bias = added(bias, back_dot(chosen, part))
    embed_ref[...] = embed
    position_ref[...] = position
    head_ref[...] = head
    bias_ref[...] = bias[0:1, :]
    first = stack[0].astype(bf16)
    gains = back_dot(pick(8, LANES, lambda row, lane: (lane == row + gain_at) & (row < 2)), first)
    gain_one_ref[...] = gains[0:1, :]
    gain_two_ref[...] = gains[1:2, :]
    coded = stack[0][:, label_at : label_at + 1] * 8.0 + stack[0][:, label_at + 1 : label_at + 2]
    shape = (4 * slot_cols, class_ref.shape[1])
    label = jnp.broadcast_to(coded[: 4 * slot_cols].astype(jnp.int32), shape)
    hot = (lax.broadcasted_iota(jnp.int32, shape, 1) == label).astype(f32).astype(bf16)
    class_ref[...] = dot(slots.astype(bf16), hot)


def after(value, *others):
    return lax.optimization_barrier((value, *others))[0]


def shape_of(dims, dtype):
    return jax.ShapeDtypeStruct(dims, dtype)


def call(kernel, places, outs, scratch, operands, flops, room=16):
    spaces = {
        "s": pl.BlockSpec(memory_space=pltpu.SMEM),
        "v": pl.BlockSpec(memory_space=pltpu.VMEM),
        "h": pl.BlockSpec(memory_space=pltpu.HBM),
    }
    return pl.pallas_call(
        kernel,
        out_shape=outs,
        in_specs=[spaces[p] for p in places],
        out_specs=[spaces["v"]] * len(outs),
        scratch_shapes=scratch,
        compiler_params=pltpu.CompilerParams(vmem_limit_bytes=room * 2**20),
        cost_estimate=pl.CostEstimate(flops=flops, bytes_accessed=8 * 2**20, transcendentals=2**20),
    )(*operands)


def shards(
    patches,
    segment_ids,
    labels,
    embed_weight,
    embed_bias,
    position_table,
    class_table,
    attn_gain,
    qkv_weight,
    proj_weight,
    mlp_gain,
    up_weight,
    down_weight,
    head_weight,
    latent_grad,
    logdet_grad,
):
    _, quarter, channels = patches.shape
    length = segment_ids.shape[1]
    width = qkv_weight.shape[0]
    hidden_width = up_weight.shape[1]
    tokens = 2 * quarter
    ff = hidden_width // 4
    half_width = width // 2
    group = half_width // 2
    count = lax.axis_size("dp")
    me = lax.axis_index("dp")
    r = lax.axis_index("narrow")
    core = r & 1
    ids = jnp.concatenate(
        [jnp.stack([me, r]).astype(jnp.int32), segment_ids[0, ::UNIT], labels[0]]
    )
    vectors = jnp.stack([embed_bias, attn_gain, mlp_gain])
    near_steps, far_steps = halving_steps(count), halving_steps(count, True)
    size = width // count
    sem = pltpu.SemaphoreType.DMA

    images = labels.shape[1]
    slots = images * count
    position_cols, embed_cols = position_table.shape[0] // 4, channels // 4
    head_cols = channels // 2
    slot_cols = slots // 4
    compact = position_cols + embed_cols + slot_cols + 4 + head_cols <= LANES and slots <= size
    slot_cols = slot_cols if compact else 0
    gain_at = position_cols + embed_cols + slot_cols + 2

    coarse = lax.reduce_precision(logdet_grad, 8, 7)
    own_part = jnp.concatenate(
        [
            patches[0].T,
            latent_grad[0].T,
            coarse.astype(bf16),
            (logdet_grad - coarse).astype(bf16),
        ]
    )
    far_part = swap(own_part, "narrow", 2)
    parts = [
        own_part,
        swap(own_part, "narrow", 1),
        far_part,
        swap(far_part, "narrow", 1),
    ]
    base, allowed = call(
        base_kernel,
        "svhh",
        [shape_of((length, width), f32), shape_of((length, BIG + TILE), f32)],
        [
            pltpu.VMEM(position_table.shape, bf16),
            pltpu.VMEM(class_table.shape, bf16),
            pltpu.VMEM((16, width), f32),
            sem((2,)),
        ],
        (ids, vectors, class_table, position_table),
        2 * 16 * width * class_table.shape[0],
    )
    embedded, normed_one, qkv, attended = call(
        front_kernel,
        "s" + 8 * "v" + "h",
        [
            shape_of((tokens, width), f32),
            shape_of((length, width), bf16),
            shape_of((length, 3 * half_width), bf16),
            shape_of((length, half_width), bf16),
        ],
        [
            pltpu.VMEM((3, width, half_width), bf16),
            pltpu.VMEM((length + 8, width), f32),
            sem((3,)),
        ],
        (ids, *parts, base, allowed, vectors, embed_weight, qkv_weight),
        2 * length * width * 3 * half_width,
        28,
    )
    attended_peer = swap(attended, "narrow", 1)
    (
        latent,
        logdet,
        direct,
        normed_two,
        hidden,
        d_mlp,
        d_hidden,
        d_one,
        d_attn,
        gain_part_two,
        head_keep,
        head_send,
    ) = call(
        middle_kernel,
        "s" + 7 * "v" + "hhh",
        [
            shape_of((channels, quarter), f32),
            shape_of((1, quarter), f32),
            shape_of((channels, quarter), f32),
            shape_of((tokens, width), bf16),
            shape_of((2, tokens, ff), bf16),
            shape_of((tokens, width), bf16),
            shape_of((2, tokens, ff), bf16),
            shape_of((tokens, width), f32),
            shape_of((tokens, width), bf16),
            shape_of((1, width), f32),
            shape_of((width, LANES), f32),
            shape_of((width, LANES), bf16),
        ],
        [
            pltpu.VMEM((width, width), bf16),
            pltpu.VMEM((4, width, ff), bf16),
            pltpu.VMEM((4, ff, width), bf16),
            pltpu.VMEM((2, tokens, ff), bf16),
            pltpu.VMEM((2, tokens, ff), bf16),
            pltpu.VMEM((4, tokens, ff), f32),
            pltpu.VMEM((tokens, width), f32),
            pltpu.VMEM((tokens, width), bf16),
            sem((9,)),
        ],
        (
            ids,
            embedded,
            attended,
            attended_peer,
            vectors,
            head_weight.T,
            own_part,
            far_part,
            proj_weight,
            up_weight,
            down_weight,
        ),
        8 * tokens * width * hidden_width,
        40,
    )

    aligned = size % 16 == 0 and count > 1

    def block_shapes(cols):
        if aligned:
            return [shape_of((count // 2, size, cols), bf16)] * 2
        return [shape_of((width, cols), bf16)]

    def blocks_of(outs, steps):
        if aligned:
            return outs
        blocks = relative_blocks(outs[0], me, steps)
        return blocks[: max(1, count // 2)], blocks[max(1, count // 2) :]

    def added(blocks, steps, turn, done, *others):
        keep, send = blocks
        keep = after(keep, *others)
        for step in steps[:done]:
            total = keep.astype(f32) + swap(send, "dp", step, turn).astype(f32)
            half = (total.shape[0] + 1) // 2
            keep, send = total[:half].astype(bf16), total[half:].astype(bf16)
        return keep, send

    def four(part, turn):
        far_one = swap(part, "narrow", 2, turn)
        return [part, swap(part, "narrow", 1), far_one, swap(far_one, "narrow", 1)]

    d_attn_peer = swap(d_attn, "narrow", 1)
    up_blocks = blocks_of(
        call(
            functools.partial(up_proj_kernel, size, near_steps),
            "s" + 8 * "v",
            block_shapes(ff + group),
            [pltpu.VMEM((length, half_width), bf16), pltpu.VMEM((width, ff + group), f32)],
            (
                ids,
                normed_two,
                swap(normed_two, "narrow", 1),
                d_hidden[0],
                swap(d_hidden[1], "narrow", 1),
                attended,
                attended_peer,
                d_attn,
                d_attn_peer,
            ),
            4 * tokens * width * (ff + half_width),
        ),
        near_steps,
    )
    down_blocks = blocks_of(
        call(
            functools.partial(pair_sum_kernel, size, far_steps),
            "svvvv",
            block_shapes(ff),
            [pltpu.VMEM((width, ff), f32)],
            (
                ids,
                after(d_mlp, *up_blocks),
                swap(d_mlp, "narrow", 1),
                hidden[0],
                swap(hidden[1], "narrow", 1),
            ),
            4 * tokens * width * ff,
        ),
        far_steps,
    )
    d_qkv, d_qkv_send = call(
        back_attention_kernel,
        "s" + 5 * "v",
        [shape_of((tokens, 3 * half_width), bf16)] * 2,
        [
            pltpu.VMEM((length, half_width), bf16),
            pltpu.VMEM((length, 3 * half_width), bf16),
        ],
        (ids, after(qkv, *down_blocks, *up_blocks), d_attn, d_attn_peer, proj_weight, allowed),
        10 * length * length * half_width,
        28,
    )
    qkv_blocks = blocks_of(
        call(
            functools.partial(qkv_sum_kernel, size, near_steps),
            "svvv",
            block_shapes(3 * group),
            [pltpu.VMEM((length, 3 * half_width), bf16), pltpu.VMEM((width, 3 * group), f32)],
            (ids, normed_one, d_qkv, d_qkv_send),
            2 * length * width * 3 * group,
        ),
        near_steps,
    )
    d_qkv_peer = after(swap(d_qkv_send, "narrow", 1), *qkv_blocks)
    [d_embed] = call(
        back_front_kernel,
        "s" + 7 * "v",
        [shape_of((tokens + EXTRA, width), bf16)],
        [],
        (ids, d_qkv, d_qkv_peer, embedded, d_one, vectors, gain_part_two, qkv_weight),
        6 * tokens * width * width,
    )
    d_embed_peer = swap(d_embed, "narrow", 1)
    *table_outs, patches_grad = call(
        functools.partial(
            table_sum_kernel, size, far_steps, (position_cols, embed_cols, slot_cols)
        ),
        "s" + 10 * "v",
        [*block_shapes(LANES), shape_of((channels, quarter), f32)],
        [
            pltpu.VMEM((length + 8, LANES), f32),
            pltpu.VMEM((tokens + EXTRA, LANES), bf16),
            pltpu.VMEM((tokens + EXTRA, LANES), bf16),
            pltpu.VMEM((quarter + EXTRA, width), f32),
            pltpu.VMEM((width, LANES), f32),
        ],
        (
            ids,
            d_embed,
            d_embed_peer,
            *parts,
            head_keep,
            swap(head_send, "narrow", 1),
            direct,
            embed_weight,
        ),
        2 * length * width * LANES,
    )
    table_blocks = blocks_of(table_outs, far_steps)

    def reduced(blocks, steps, turn, *others):
        return added(blocks, steps, turn, len(steps), *others)[0][0]

    up_grad, proj_grad = call(
        up_out_kernel,
        "svvvv",
        [shape_of((size, hidden_width), f32), shape_of((size, width), f32)],
        [pltpu.VMEM((4, size, group), f32)],
        (ids, *four(reduced(up_blocks, near_steps, 0, *qkv_blocks), 0)),
        0,
    )
    [down_grad] = call(
        down_out_kernel,
        "svvvv",
        [shape_of((size, hidden_width), f32)],
        [],
        (ids, *four(reduced(down_blocks, far_steps, 1, *qkv_blocks), 1)),
        0,
    )
    [qkv_grad] = call(
        qkv_out_kernel,
        "svvvv",
        [shape_of((size, 3 * width), f32)],
        [pltpu.VMEM((4, size, 3 * group), f32)],
        (ids, *four(reduced(qkv_blocks, near_steps, 2, *table_outs), 2)),
        0,
    )
    if compact:
        embed_grad, position_grad, class_grad, head_grad, gain_one, gain_two, bias = call(
            functools.partial(
                table_out_kernel, (position_cols, embed_cols, slot_cols, head_cols)
            ),
            "svvvv",
            [
                shape_of((channels, size), f32),
                shape_of((size, position_table.shape[0]), f32),
                shape_of((size, class_table.shape[0]), f32),
                shape_of((size, 2 * channels), f32),
                shape_of((1, size), f32),
                shape_of((1, size), f32),
                shape_of((1, size), f32),
            ],
            [pltpu.VMEM((4, size, LANES), f32)],
            (ids, *four(reduced(table_blocks, far_steps, 3), 3)),
            0,
        )
        attngain_grad, mlpgain_grad, bias_grad = gain_one[0], gain_two[0], bias[0]
    else:

        def natural(mine, peers):
            a, b, c, d = mine[:quarter], mine[quarter:], peers[:quarter], peers[quarter:]
            return jnp.where(
                core == 0, jnp.concatenate([a, c, b, d]), jnp.concatenate([c, a, d, b])
            )

        segment_hot = (
            segment_ids[0][:, None] == jnp.arange(images, dtype=jnp.int32)[None, :]
        ).astype(bf16)
        label_hot = (
            labels[0][:, None] == jnp.arange(class_table.shape[0], dtype=jnp.int32)
        ).astype(bf16)
        segment_part = token_sum(natural(d_embed[:tokens], d_embed_peer[:tokens]), segment_hot)
        class_part = dot(segment_part.astype(bf16), label_hot).astype(bf16)
        class_cols = class_table.shape[0] // 4
        keep, send = table_blocks
        more_blocks = relative_blocks(
            jnp.concatenate(
                [
                    lax.dynamic_slice_in_dim(class_part, r * class_cols, class_cols, 1),
                    jnp.sum(segment_part, axis=1, keepdims=True).astype(bf16),
                ],
                axis=1,
            ),
            me,
            far_steps,
        )
        near = keep.shape[0]
        keep = jnp.concatenate([keep, more_blocks[:near]], axis=2)
        send = jnp.concatenate([send, more_blocks[near:]], axis=2)
        shares = jnp.stack(four(reduced((keep, send), far_steps, 3), 3)).astype(f32)
        shares = [lax.dynamic_index_in_dim(shares, r ^ i, 0, keepdims=False) for i in range(4)]

        def joined(start, cols):
            return jnp.concatenate([share[:, start : start + cols] for share in shares], axis=1)

        position_grad = joined(0, position_cols)
        embed_grad = joined(position_cols, embed_cols).T
        class_grad = joined(LANES, class_cols)
        head_grad = joined(LANES - head_cols, head_cols)
        attngain_grad = shares[0][:, gain_at]
        mlpgain_grad = shares[0][:, gain_at + 1]
        bias_grad = shares[0][:, LANES + class_cols]
    return (
        latent.T[None],
        logdet,
        patches_grad.T[None],
        embed_grad,
        bias_grad,
        position_grad.T,
        class_grad.T,
        attngain_grad,
        qkv_grad,
        proj_grad,
        mlpgain_grad,
        up_grad,
        down_grad.T,
        head_grad,
    )


def solution(mesh):
    return jax.shard_map(
        shards,
        mesh=mesh,
        in_specs=(
            P("dp", "narrow", None),
            P("dp", None),
            P("dp", None),
            P(),
            P(),
            P(),
            P(),
            P(),
            P(),
            P(),
            P(),
            P(),
            P(),
            P(),
            P("dp", "narrow", None),
            P("dp", "narrow"),
        ),
        out_specs=(
            P("dp", "narrow", None),
            P("dp", "narrow"),
            P("dp", "narrow", None),
            P(None, "dp"),
            P("dp"),
            P(None, "dp"),
            P(None, "dp"),
            P("dp"),
            P("dp", None),
            P("dp", None),
            P("dp"),
            P("dp", None),
            P(None, "dp"),
            P("dp", None),
        ),
        check_vma=False,
    )
```

```python
import functools
import math

import jax
import jax.numpy as jnp
from jax import lax
from jax.experimental import pallas as pl
from jax.experimental.pallas import tpu as pltpu
from jax.sharding import PartitionSpec as P

HD = 64
UNIT = 64
BIG = 256
TILE = 128
EXTRA = 16
FRONT_ROOM = 28
LANES = 128
bf16, f32 = jnp.bfloat16, jnp.float32
epsilon = 1e-05
masked_score = -1e30


def dot(left, right):
    return jnp.dot(left, right, preferred_element_type=f32)


def token_sum(left, right):
    return lax.dot_general(left, right, (((0,), (0,)), ((), ())), preferred_element_type=f32)


def back_dot(grads, weight):
    return lax.dot_general(grads, weight, (((1,), (1,)), ((), ())), preferred_element_type=f32)


def swap(value, axis, step, turn=0):
    count = lax.axis_size(axis)
    turned = [(i + turn) % count for i in range(count)]
    return lax.ppermute(value, axis, [(i, i ^ step) for i in turned])


def normalised(values):
    center = jnp.mean(values, axis=-1, keepdims=True)
    offsets = values - center
    inverse = lax.rsqrt(jnp.mean(offsets * offsets, axis=-1, keepdims=True) + epsilon)
    return offsets * inverse, inverse


def norm_back(grads, gain, normed, inverse):
    e = grads * gain
    mean_e = jnp.mean(e, axis=-1, keepdims=True)
    mean_en = jnp.mean(e * normed, axis=-1, keepdims=True)
    return inverse * (e - mean_e - normed * mean_en)


def halving_steps(count, far_first=False):
    steps = [1 << i for i in range(count.bit_length() - 1)]
    if far_first and len(steps) > 1:
        steps[:2] = steps[1], steps[0]
    return steps


def block_order(steps):
    order = [0]
    for step in reversed(steps):
        order = order + [j ^ step for j in order]
    return order


def relative_blocks(grad, me, steps):
    order = block_order(steps)
    size = grad.shape[0] // len(order)
    return jnp.stack([lax.dynamic_slice_in_dim(grad, (me ^ j) * size, size, 0) for j in order])


UNITS_AT = 2


def unit_firsts(ids_ref, units):
    firsts = [jnp.int32(0)]
    for u in range(1, units):
        same = ids_ref[UNITS_AT + u] == ids_ref[UNITS_AT + u - 1]
        firsts.append(jnp.where(same, firsts[-1], u))
    return firsts


def allowed_bias(row_start, firsts):
    begin, end = window_of(row_start)
    shape = (TILE, end - begin)
    row = lax.broadcasted_iota(jnp.int32, shape, 0)
    key = lax.broadcasted_iota(jnp.int32, shape, 1) + begin
    unit = row_start // UNIT
    first = jnp.where(row < UNIT, firsts[unit] * UNIT, firsts[unit + 1] * UNIT)
    return jnp.where((key >= first) & (key <= row + row_start), 0.0, masked_score)


def stacked(block, masks):
    return jnp.concatenate([block * masks[0], block * masks[1]])


def head_masks():
    lane = lax.broadcasted_iota(jnp.int32, (1, 2 * HD), 1)
    low = (lane < HD).astype(f32)
    return low.astype(bf16), (1.0 - low).astype(bf16)


def window_of(start):
    return max(0, start - BIG), start + TILE


def pick(rows, lanes, to_lane):
    row = lax.broadcasted_iota(jnp.int32, (rows, lanes), 0)
    lane = lax.broadcasted_iota(jnp.int32, (rows, lanes), 1)
    return to_lane(row, lane).astype(f32).astype(bf16)


def base_kernel(
    ids_ref, vector_ref, class_ref, position_hbm, base_ref, allowed_ref, position_ref, image_rows, sems
):
    table = pltpu.make_async_copy(position_hbm, position_ref, sems.at[0])
    table.start()
    length = base_ref.shape[0]
    units = length // UNIT
    firsts = unit_firsts(ids_ref, units)
    for start in range(0, length, TILE):
        begin, end = window_of(start)
        allowed_ref[start : start + TILE, : end - begin] = allowed_bias(start, firsts)
    shape = (image_rows.shape[0], class_ref.shape[0])
    row = lax.broadcasted_iota(jnp.int32, shape, 0)
    label = jnp.full(shape, -1, jnp.int32)
    for s in range(ids_ref.shape[0] - UNITS_AT - units):
        label = jnp.where(row == s, ids_ref[UNITS_AT + units + s], label)
    hot = (lax.broadcasted_iota(jnp.int32, shape, 1) == label).astype(f32).astype(bf16)
    image_rows[...] = dot(hot, class_ref[...]) + vector_ref[0:1, :].astype(f32)
    table.wait()
    for u in range(units):
        block = u - firsts[u]
        table = position_ref[pl.ds(pl.multiple_of(block * UNIT, UNIT), UNIT), :]
        image = image_rows[pl.ds(ids_ref[UNITS_AT + u], 1), :]
        base_ref[u * UNIT : (u + 1) * UNIT, :] = table.astype(f32) + image


def front_kernel(
    ids_ref,
    part_0_ref,
    part_1_ref,
    part_2_ref,
    part_3_ref,
    base_ref,
    allowed,
    vector_ref,
    embed_ref,
    weight_ref,
    embedded_ref,
    normed_ref,
    qkv_ref,
    attended_ref,
    own_weight,
    patch_rows,
    sems,
):
    length, width = normed_ref.shape
    half = width // 2
    quarter = length // 4
    channels = embed_ref.shape[0]
    place = ids_ref[1]
    core = place & 1
    copies = []
    for t in range(3):
        start = pl.multiple_of(t * width + core * half, 128)
        copies.append(
            pltpu.make_async_copy(weight_ref.at[:, pl.ds(start, half)], own_weight.at[t], sems.at[t])
        )
        copies[-1].start()
    firsts = unit_firsts(ids_ref, length // UNIT)
    starts = range(0, length, TILE)
    patch_rows[0:8, :] = jnp.zeros((8, width), f32)
    for j, part in enumerate((part_0_ref, part_1_ref, part_2_ref, part_3_ref)):
        at = pl.multiple_of((place ^ j) * quarter + 8, 8)
        patch_rows[pl.ds(at, quarter), :] = token_sum(part[:channels, :], embed_ref[...])
    gain = vector_ref[1:2, :].astype(f32)
    inner = lax.broadcasted_iota(jnp.int32, (UNIT, width), 0)
    for u in range(length // UNIT):
        rows = slice(u * UNIT, (u + 1) * UNIT)
        before = patch_rows[u * UNIT + 7 : u * UNIT + 7 + UNIT, :]
        before = jnp.where((inner == 0) & (firsts[u] == u), 0.0, before)
        values = before + base_ref[rows, :]
        q = u * UNIT // quarter
        inside = (q >> 1) * quarter + u * UNIT - q * quarter

        @pl.when(core == (q & 1))
        def _():
            embedded_ref[pl.ds(inside, UNIT), :] = values

        normed_ref[rows, :] = (normalised(values)[0] * gain).astype(bf16)
    for t in range(3):
        copies[t].wait()
        qkv_ref[:, t * half : (t + 1) * half] = dot(normed_ref[...], own_weight[t]).astype(bf16)
    masks = head_masks()
    low_lanes = lax.broadcasted_iota(jnp.int32, (TILE, 2 * HD), 1) < HD

    def pair_step(pair, carry):
        lanes = [pl.ds(pl.multiple_of(t * half + pair * 2 * HD, 128), 2 * HD) for t in range(3)]
        scores = []
        for start in starts:
            begin, end = window_of(start)
            q = stacked(qkv_ref[start : start + TILE, lanes[0]], masks)
            scores.append(back_dot(q, qkv_ref[begin:end, lanes[1]]))
        raised, totals = [], []
        for start, block in zip(starts, scores):
            begin, end = window_of(start)
            bias = allowed[start : start + TILE, : end - begin]
            masked = block * (1.0 / math.sqrt(HD)) + jnp.concatenate([bias, bias])
            power = jnp.exp(masked - jnp.max(masked, axis=-1, keepdims=True))
            raised.append(power.astype(bf16))
            totals.append(1.0 / jnp.sum(power, axis=-1, keepdims=True))
        for start, power, inverse in zip(starts, raised, totals):
            begin, end = window_of(start)
            out = dot(power, qkv_ref[begin:end, lanes[2]]) * inverse
            attended_ref[start : start + TILE, lanes[0]] = jnp.where(
                low_lanes, out[:TILE], out[TILE:]
            ).astype(bf16)
        return carry

    lax.fori_loop(0, half // (2 * HD), pair_step, 0, unroll=True)


def back_attention_kernel(
    ids_ref,
    qkv_ref,
    mine_ref,
    peer_ref,
    proj_ref,
    allowed,
    weight_hbm,
    grads,
    own_ref,
    send_ref,
    mixed,
    own_weight,
    sems,
):
    length = qkv_ref.shape[0]
    half = qkv_ref.shape[1] // 3
    quarter = length // 4
    core = ids_ref[1] & 1
    width = weight_hbm.shape[0]
    copies = []
    for t in range(3):
        start = pl.multiple_of(t * width + core * half, 128)
        copies.append(
            pltpu.make_async_copy(weight_hbm.at[:, pl.ds(start, half)], own_weight.at[t], sems.at[t])
        )
        copies[-1].start()
    proj = proj_ref[pl.ds(pl.multiple_of(core * half, 128), half), :]
    for ref, side in ((mine_ref, core), (peer_ref, 1 - core)):
        product = back_dot(ref[...], proj).astype(bf16)
        for i in range(2):
            rows = pl.ds(pl.multiple_of((2 * i + side) * quarter, 16), quarter)
            mixed[rows, :] = product[i * quarter : (i + 1) * quarter]
    masks = head_masks()
    low_lanes = lax.broadcasted_iota(jnp.int32, (TILE, 2 * HD), 1) < HD
    scale = 1.0 / math.sqrt(HD)
    starts = range(0, length, TILE)

    def pair_step(pair, carry):
        lanes = [pl.ds(pl.multiple_of(t * half + pair * 2 * HD, 128), 2 * HD) for t in range(3)]
        queries, outer, scores, d_weights = [], [], [], []
        for start in starts:
            begin, end = window_of(start)
            queries.append(stacked(qkv_ref[start : start + TILE, lanes[0]], masks))
            outer.append(stacked(mixed[start : start + TILE, lanes[0]], masks))
            scores.append(back_dot(queries[-1], qkv_ref[begin:end, lanes[1]]))
            d_weights.append(back_dot(outer[-1], qkv_ref[begin:end, lanes[2]]))
        weights, d_scores = [], []
        for start, block, d_block in zip(starts, scores, d_weights):
            begin, end = window_of(start)
            bias = allowed[start : start + TILE, : end - begin]
            masked = block * scale + jnp.concatenate([bias, bias])
            power = jnp.exp(masked - jnp.max(masked, axis=-1, keepdims=True))
            weight = power * (1.0 / jnp.sum(power, axis=-1, keepdims=True))
            centre = jnp.sum(weight * d_block, axis=-1, keepdims=True)
            weights.append(weight.astype(bf16))
            d_scores.append((weight * (d_block - centre)).astype(bf16))
        for i, start in enumerate(starts):
            begin, end = window_of(start)
            out = dot(d_scores[i], qkv_ref[begin:end, lanes[1]])
            grads[start : start + TILE, lanes[0]] = (
                jnp.where(low_lanes, out[:TILE], out[TILE:]) * scale
            ).astype(bf16)
        d_keys = [token_sum(d, q) for d, q in zip(d_scores, queries)]
        d_values = [token_sum(w, o) for w, o in zip(weights, outer)]
        for at in starts:
            for t, sums, factor in ((1, d_keys, scale), (2, d_values, 1.0)):
                total = None
                for start, block in zip(starts, sums):
                    begin, end = window_of(start)
                    if begin <= at < end:
                        term = block[at - begin : at - begin + TILE]
                        total = term if total is None else total + term
                grads[at : at + TILE, lanes[t]] = (total * factor).astype(bf16)
        return carry

    lax.fori_loop(0, half // (2 * HD), pair_step, 0, unroll=True)
    for copy in copies:
        copy.wait()
    for ref, side in ((send_ref, 1 - core), (own_ref, core)):
        for i in range(2):
            rows = pl.ds(pl.multiple_of((2 * i + side) * quarter, 16), quarter)
            total = None
            for t in range(3):
                term = back_dot(grads[rows, t * half : (t + 1) * half], own_weight[t])
                total = term if total is None else total + term
            ref[i * quarter : (i + 1) * quarter, :] = total.astype(ref.dtype)


def middle_kernel(
    ids_ref,
    embedded_ref,
    own_ref,
    peer_ref,
    gain_ref,
    head_weight_ref,
    near_ref,
    far_ref,
    proj_hbm,
    up_hbm,
    down_hbm,
    latent_ref,
    logdet_ref,
    direct_ref,
    normed_ref,
    hidden_ref,
    hidden_send_ref,
    d_mlp_ref,
    d_hidden_ref,
    d_hidden_send_ref,
    d_one_ref,
    d_attn_ref,
    gain_part_ref,
    head_ref,
    head_send_ref,
    proj,
    up,
    down,
    hidden_rest,
    d_hidden_rest,
    slope,
    stream,
    low,
    sems,
):
    tokens, width = embedded_ref.shape
    quarter = tokens // 2
    half = width // 2
    ff = up.shape[2]
    place = ids_ref[1]
    core, far = place & 1, place >> 1
    channels = latent_ref.shape[0]
    hiddens = hidden_ref, hidden_send_ref, hidden_rest.at[0], hidden_rest.at[1]
    d_hiddens = d_hidden_ref, d_hidden_send_ref, d_hidden_rest.at[0], d_hidden_rest.at[1]
    copies = [pltpu.make_async_copy(proj_hbm, proj, sems.at[0])]
    copies[0].start()
    for j in range(4):
        columns = pl.ds(pl.multiple_of((place ^ j) * ff, 128), ff)
        copies.append(pltpu.make_async_copy(up_hbm.at[:, columns], up.at[j], sems.at[1 + j]))
        copies[-1].start()
    for j in range(4):
        rows = pl.ds(pl.multiple_of((place ^ j) * ff, 128), ff)
        copies.append(pltpu.make_async_copy(down_hbm.at[rows, :], down.at[j], sems.at[5 + j]))
        copies[-1].start()
    copies[0].wait()
    gain = gain_ref[2:3, :].astype(f32)
    for i in range(2):
        source = pl.ds(pl.multiple_of((2 * i + core) * quarter, 16), quarter)
        rows = slice(i * quarter, (i + 1) * quarter)
        values = embedded_ref[rows, :]
        for ref, side in ((own_ref, core), (peer_ref, 1 - core)):
            weight = proj[pl.ds(pl.multiple_of(side * half, 128), half), :]
            values += dot(ref[source, :], weight)
        stream[rows, :] = values
        normed_ref[rows, :] = (normalised(values)[0] * gain).astype(bf16)
    for j in range(4):
        copies[1 + j].wait()

        pre = dot(normed_ref[...], up[j])
        cdf = 0.5 * (1.0 + lax.erf(pre * math.sqrt(0.5)))
        density = jnp.exp(-0.5 * pre * pre) * (1.0 / math.sqrt(2 * math.pi))
        slope[j] = cdf + pre * density
        value = (pre * cdf).astype(bf16)
        hiddens[j][...] = value
    total = stream[...]
    for j in range(4):
        copies[5 + j].wait()
        total += dot(hiddens[j][...], down[j])
    low[...] = total.astype(bf16)
    head_sums = [jnp.zeros(head_ref.shape, f32)] * 2
    head_cols = channels // 2
    lane_at = LANES - head_cols
    for i in range(2):
        rows = slice(i * quarter, (i + 1) * quarter)
        part = jnp.where(far == i, near_ref[...].astype(f32), far_ref[...].astype(f32))
        patches, cot = part[:channels], part[channels : 2 * channels]
        logdet_cot = jnp.sum(part[2 * channels :], axis=0, keepdims=True)
        head_out = back_dot(head_weight_ref[...], low[rows, :])
        mean_shift, logscale = head_out[:channels], head_out[channels:]
        factor = jnp.exp(-logscale)
        latent = (patches - mean_shift) * factor
        direct = cot * factor

        @pl.when(far == i)
        def _():
            latent_ref[...] = latent
            logdet_ref[...] = -jnp.sum(logscale, axis=0, keepdims=True)
            direct_ref[...] = direct

        d_head = jnp.concatenate([-direct, -cot * latent - logdet_cot]).astype(bf16)
        d_two = token_sum(d_head, head_weight_ref[...])
        d_one_ref[rows, :] = d_two
        d_mlp_ref[rows, :] = d_two.astype(bf16)
        for k, index in enumerate((place, place ^ 1)):
            chosen = pick(
                2 * channels,
                LANES,
                lambda row, lane: (lane - lane_at + index * head_cols == row) & (lane >= lane_at),
            )
            columns = token_sum(d_head, chosen).astype(bf16)
            head_sums[k] += token_sum(low[rows, :], columns)
    head_ref[...] = head_sums[0]
    head_send_ref[...] = head_sums[1].astype(bf16)
    for j in range(4):
        value = (back_dot(d_mlp_ref[...], down[j]) * slope[j]).astype(bf16)
        d_hiddens[j][...] = value
    for i in range(2):
        rows = slice(i * quarter, (i + 1) * quarter)
        grads = jnp.zeros((quarter, width), f32)
        for j in range(4):
            value = d_hiddens[j][rows, :]
            grads += back_dot(value, up[j])
        n, inverse = normalised(stream[rows, :])
        part = jnp.sum(grads * n, axis=0, keepdims=True)
        gain_part_ref[...] = part if i == 0 else gain_part_ref[...] + part
        d_one = d_one_ref[rows, :] + norm_back(grads, gain, n, inverse)
        d_one_ref[rows, :] = d_one
        d_attn_ref[rows, :] = d_one.astype(bf16)


def back_front_kernel(
    own_ref,
    peer_ref,
    embedded_ref,
    d_one_ref,
    gain_ref,
    part_ref,
    d_embed_ref,
):
    tokens, width = embedded_ref.shape
    gain = gain_ref[1:2, :].astype(f32)
    step = tokens // 6
    total = jnp.zeros((1, width), f32)
    for i in range(6):
        rows = slice(i * step, (i + 1) * step)
        grads = own_ref[rows, :] + peer_ref[rows, :].astype(f32)
        n, inverse = normalised(embedded_ref[rows, :])
        total += jnp.sum(grads * n, axis=0, keepdims=True)
        d_embed_ref[rows, :] = (d_one_ref[rows, :] + norm_back(grads, gain, n, inverse)).astype(
            bf16
        )
    row = lax.broadcasted_iota(jnp.int32, (EXTRA, width), 0)
    both = jnp.where(row % 2 == 0, total, part_ref[...])
    coarse = both.astype(bf16).astype(f32)
    rest = jnp.where(row < 2, coarse, jnp.where(row < 4, both - coarse, 0.0))
    d_embed_ref[tokens : tokens + EXTRA, :] = rest.astype(bf16)


def place_blocks(total, outs, me, size, steps, start=0):
    columns = slice(start, start + outs[0].shape[-1])
    if len(outs) == 1:
        outs[0][...] = total[:, columns].astype(bf16)
        return
    keep, send = outs
    for k, j in enumerate(block_order(steps)):
        block = total[pl.ds(pl.multiple_of((me ^ j) * size, 16), size), columns].astype(bf16)
        if k < keep.shape[0]:
            keep[k] = block
        else:
            send[k - keep.shape[0]] = block


def pair_sum_kernel(size, steps, ids_ref, left_ref, left_peer_ref, right_ref, right_peer_ref, *rest):
    *outs, total = rest
    columns = total.shape[1]
    total[...] = token_sum(left_ref[...], right_ref[:, :columns]) + token_sum(
        left_peer_ref[...], right_peer_ref[:, :columns]
    )
    place_blocks(total, outs, ids_ref[0], size, steps)


def heads_sum_kernel(
    size,
    both_steps,
    ids_ref,
    normed_ref,
    d_qkv_ref,
    attended_ref,
    attended_peer_ref,
    d_attn_ref,
    d_attn_peer_ref,
    *rest,
):
    *outs, natural, total = rest
    place = ids_ref[1]
    core, far = place & 1, place >> 1
    length, width = normed_ref.shape
    quarter, half = length // 4, width // 2
    group = half // 2
    for t in range(3):
        low = d_qkv_ref[:, t * half : t * half + group]
        high = d_qkv_ref[:, t * half + group : (t + 1) * half]
        picked = jnp.where(far == 0, low.astype(f32), high.astype(f32)).astype(bf16)
        total[:, t * group : (t + 1) * group] = token_sum(normed_ref[...], picked)
    columns = pl.ds(pl.multiple_of(far * half, 128), half)
    for ref, side in ((d_attn_ref, core), (d_attn_peer_ref, 1 - core)):
        for i in range(2):
            rows = pl.ds(pl.multiple_of((2 * i + side) * quarter, 16), quarter)
            natural[rows, :] = ref[i * quarter : (i + 1) * quarter, columns]
    for ref, side in ((attended_ref, core), (attended_peer_ref, 1 - core)):
        sums = token_sum(ref[...], natural[...])
        rows = pl.ds(pl.multiple_of(side * half, 16), half)
        total[rows, 3 * group :] = jnp.where(core == 0, sums[:, : half // 2], sums[:, half // 2 :])
    outs = [outs[: len(outs) // 2], outs[len(outs) // 2 :]]
    for k, steps in enumerate(both_steps):
        place_blocks(total, outs[k], ids_ref[0], size, steps, k * 2 * group)


def table_sum_kernel(
    size,
    steps,
    plan,
    ids_ref,
    d_ref,
    d_peer_ref,
    part_0_ref,
    part_1_ref,
    part_2_ref,
    part_3_ref,
    head_ref,
    head_peer_ref,
    direct_ref,
    embed_ref,
    *rest,
):
    *outs, patches_ref, before_rows, to_own, to_peer, following, total = rest
    position_cols, embed_cols, slot_cols = plan
    slot_at = position_cols + embed_cols
    label_at = slot_at + slot_cols
    gain_at = label_at + 2
    me, place = ids_ref[0], ids_ref[1]
    core, far = place & 1, place >> 1
    channels, quarter = direct_ref.shape
    tokens = 2 * quarter
    length = 2 * tokens
    units = length // UNIT
    labels_at = UNITS_AT + units
    images = ids_ref.shape[0] - labels_at
    parts = (part_0_ref, part_1_ref, part_2_ref, part_3_ref)
    chosen = pick(
        part_0_ref.shape[0],
        LANES,
        lambda row, lane: (row == lane - position_cols + place * embed_cols)
        & (lane >= position_cols)
        & (lane < slot_at),
    )
    before_rows[0:8, :] = jnp.zeros((8, LANES), f32)
    for j, part in enumerate(parts):
        at = pl.multiple_of((place ^ j) * quarter + 8, 8)
        before_rows[pl.ds(at, quarter), :] = token_sum(part[...], chosen)
    firsts = unit_firsts(ids_ref, units)
    row = lax.broadcasted_iota(jnp.int32, (UNIT, LANES), 0)
    lane = lax.broadcasted_iota(jnp.int32, (UNIT, LANES), 1)
    for u in range(length // UNIT):
        block = u - firsts[u]
        before = before_rows[u * UNIT + 7 : u * UNIT + 7 + UNIT, :]
        before = jnp.where((row == 0) & (block == 0), 0.0, before)
        position = lane + place * position_cols == row + block * UNIT
        slot = lane - slot_at + place * slot_cols == me * images + ids_ref[UNITS_AT + u]
        ones = ((lane < position_cols) & position) | (
            (lane >= slot_at) & (lane < label_at) & slot
        )
        value = jnp.where(ones, 1.0, before).astype(bf16)
        q = u * UNIT // quarter
        inside = (q >> 1) * quarter + u * UNIT - q * quarter

        @pl.when(core == (q & 1))
        def _():
            to_own[inside : inside + UNIT, :] = value

        @pl.when(core != (q & 1))
        def _():
            to_peer[inside : inside + UNIT, :] = value

    gain_rows = pick(EXTRA, LANES, lambda row, lane: (lane == gain_at + row % 2) & (row < 4))
    to_own[tokens:, :] = gain_rows
    to_peer[tokens:, :] = gain_rows
    total[...] = (
        token_sum(d_ref[...], to_own[...])
        + token_sum(d_peer_ref[...], to_peer[...])
        + head_ref[...]
        + head_peer_ref[...].astype(f32)
    )
    if slot_cols:
        row = lax.broadcasted_iota(jnp.int32, (size, LANES), 0)
        lane = lax.broadcasted_iota(jnp.int32, (size, LANES), 1)
        label = jnp.zeros((size, LANES), jnp.int32)
        for s in range(images):
            label = jnp.where(row == me * images + s, ids_ref[labels_at + s], label)
        code = jnp.where(
            lane == label_at, label >> 3, jnp.where(lane == label_at + 1, label & 7, 0)
        ).astype(f32)
        for b in range(total.shape[0] // size):
            total[b * size : (b + 1) * size, :] += code
    place_blocks(total, outs, me, size, steps)
    following[:quarter, :] = d_ref[pl.ds(pl.multiple_of(far * quarter, 16), quarter), :].astype(f32)
    at = pl.multiple_of(((place + 1) >> 1) * quarter, 16)
    following[quarter:, :] = d_peer_ref[pl.ds(at, EXTRA), :].astype(f32)
    row = lax.broadcasted_iota(jnp.int32, (quarter, following.shape[1]), 0)
    dropped = (row == quarter - 1) & (place == 3)
    for w in range(1, quarter // UNIT + 1):
        u = jnp.minimum(place * (quarter // UNIT) + w, units - 1)
        opens = ids_ref[UNITS_AT + u] != ids_ref[UNITS_AT + u - 1]
        dropped = dropped | ((row == w * UNIT - 1) & opens)
    shifted = jnp.where(dropped, 0.0, following[1 : quarter + 1, :]).astype(bf16)
    patches_ref[...] = direct_ref[...] + back_dot(embed_ref[...], shifted)


def mlp_out_kernel(ids_ref, *refs):
    *parts, up_ref, down_ref = refs
    ff = up_ref.shape[1] // 4
    for j, part in enumerate(parts):
        columns = pl.ds(pl.multiple_of((ids_ref[1] ^ j) * ff, 128), ff)
        up_ref[:, columns] = part[:, :ff].astype(f32)
        down_ref[:, columns] = part[:, ff:].astype(f32)


def heads_out(stack, qkv_ref, proj_ref):
    width = proj_ref.shape[1]
    group = width // 4
    starts = (0, group, -2 * group, -group)
    for i, q in enumerate((0, 2, 1, 3)):
        for t, start in enumerate(starts[:3]):
            put = t * width + i * group
            qkv_ref[:, put : put + group] = stack[q, :, start % stack.shape[2] : start % stack.shape[2] + group]
        proj_ref[:, i * group : (i + 1) * group] = stack[i, :, stack.shape[2] - group :]


def heads_out_kernel(ids_ref, *refs):
    *parts, qkv_ref, proj_ref, stack = refs
    for j, part in enumerate(parts):
        stack[ids_ref[1] ^ j] = part[...].astype(f32)
    heads_out(stack, qkv_ref, proj_ref)


def last_out_kernel(plan, ids_ref, *refs):
    *parts, qkv_ref, proj_ref, embed_ref, position_ref, class_ref, head_ref, gain_one_ref, gain_two_ref, bias_ref, stack = refs
    position_cols, embed_cols, slot_cols, head_cols, at = plan
    slot_at = position_cols + embed_cols
    label_at = slot_at + slot_cols
    gain_at = label_at + 2
    head_at = LANES - head_cols
    for j, part in enumerate(parts):
        stack[ids_ref[1] ^ j] = part[...].astype(f32)
    heads_out(stack, qkv_ref, proj_ref)
    embed = position = head = slots = bias = None

    def added(total, term):
        return term if total is None else total + term

    for q in range(4):
        part = stack[q, :, at : at + LANES].astype(bf16)

        def placed(start, cols):
            return pick(
                LANES,
                4 * cols,
                lambda row, lane: (lane == row - start + q * cols)
                & (row >= start)
                & (row < start + cols),
            )

        position = added(position, dot(part, placed(0, position_cols)))
        head = added(head, dot(part, placed(head_at, head_cols)))
        slots = added(slots, dot(part, placed(slot_at, slot_cols)))
        chosen = pick(
            embed_ref.shape[0],
            LANES,
            lambda row, lane: (row == lane - position_cols + q * embed_cols)
            & (lane >= position_cols)
            & (lane < slot_at),
        )
        embed = added(embed, back_dot(chosen, part))
        chosen = pick(
            8, LANES, lambda row, lane: (row == 0) & (lane >= slot_at) & (lane < label_at)
        )
        bias = added(bias, back_dot(chosen, part))
    embed_ref[...] = embed
    position_ref[...] = position
    head_ref[...] = head
    bias_ref[...] = bias[0:1, :]
    first = stack[0, :, at : at + LANES].astype(bf16)
    gains = back_dot(pick(8, LANES, lambda row, lane: (lane == row + gain_at) & (row < 2)), first)
    gain_one_ref[...] = gains[0:1, :]
    gain_two_ref[...] = gains[1:2, :]
    codes = stack[0, :, at : at + LANES]
    coded = codes[:, label_at : label_at + 1] * 8.0 + codes[:, label_at + 1 : label_at + 2]
    shape = (4 * slot_cols, class_ref.shape[1])
    label = jnp.broadcast_to(coded[: 4 * slot_cols].astype(jnp.int32), shape)
    hot = (lax.broadcasted_iota(jnp.int32, shape, 1) == label).astype(f32).astype(bf16)
    class_ref[...] = dot(slots.astype(bf16), hot)


def after(value, *others):
    return lax.optimization_barrier((value, *others))[0]


def shape_of(dims, dtype):
    return jax.ShapeDtypeStruct(dims, dtype)


def call(kernel, places, outs, scratch, operands, flops=0, room=16, others=()):
    spaces = {
        "s": pl.BlockSpec(memory_space=pltpu.SMEM),
        "v": pl.BlockSpec(memory_space=pltpu.VMEM),
        "h": pl.BlockSpec(memory_space=pltpu.HBM),
    }
    taken = len(operands)

    def body(*refs):
        kernel(*refs[:taken], *refs[taken + len(others) :])

    return pl.pallas_call(
        body,
        name=getattr(kernel, "func", kernel).__name__,
        out_shape=outs,
        in_specs=[spaces[p] for p in places] + [pl.BlockSpec(memory_space=pl.ANY)] * len(others),
        out_specs=[spaces["v"]] * len(outs),
        scratch_shapes=scratch,
        compiler_params=pltpu.CompilerParams(vmem_limit_bytes=room * 2**20),
    )(*operands, *others)


def last_step_kernel(kept_ref, arrived_ref, out_ref):
    out_ref[...] = (kept_ref[0].astype(f32) + arrived_ref[0].astype(f32)).astype(bf16)


def shards(
    patches,
    segment_ids,
    labels,
    embed_weight,
    embed_bias,
    position_table,
    class_table,
    attn_gain,
    qkv_weight,
    proj_weight,
    mlp_gain,
    up_weight,
    down_weight,
    head_weight,
    latent_grad,
    logdet_grad,
):
    _, quarter, channels = patches.shape
    length = segment_ids.shape[1]
    width = qkv_weight.shape[0]
    hidden_width = up_weight.shape[1]
    tokens = 2 * quarter
    ff = hidden_width // 4
    half_width = width // 2
    group = half_width // 2
    count = lax.axis_size("dp")
    me = lax.axis_index("dp")
    r = lax.axis_index("narrow")
    core = r & 1
    ids = jnp.concatenate(
        [jnp.stack([me, r]).astype(jnp.int32), segment_ids[0, ::UNIT], labels[0]]
    )
    line = jnp.arange(8, dtype=jnp.int32)[:, None]
    vectors = jnp.where(
        line == 0, embed_bias[None], jnp.where(line == 1, attn_gain[None], mlp_gain[None])
    )
    near_steps, far_steps = halving_steps(count), halving_steps(count, True)
    size = width // count
    sem = pltpu.SemaphoreType.DMA

    images = labels.shape[1]
    slots = images * count
    position_cols, embed_cols = position_table.shape[0] // 4, channels // 4
    head_cols = channels // 2
    slot_cols = slots // 4
    compact = position_cols + embed_cols + slot_cols + 4 + head_cols <= LANES and slots <= size
    slot_cols = slot_cols if compact else 0
    gain_at = position_cols + embed_cols + slot_cols + 2

    coarse = lax.reduce_precision(logdet_grad, 8, 7)
    own_part = jnp.concatenate(
        [
            patches[0].T,
            latent_grad[0].T,
            coarse.astype(bf16),
            (logdet_grad - coarse).astype(bf16),
        ]
    )
    far_part = swap(own_part, "narrow", 2)
    parts = [
        own_part,
        swap(own_part, "narrow", 1),
        far_part,
        swap(far_part, "narrow", 1),
    ]
    base, allowed = call(
        base_kernel,
        "svvh",
        [shape_of((length, width), f32), shape_of((length, BIG + TILE), f32)],
        [
            pltpu.VMEM(position_table.shape, bf16),
            pltpu.VMEM((16, width), f32),
            sem((1,)),
        ],
        (ids, vectors, class_table, position_table),
        2 * 16 * width * class_table.shape[0],
    )
    embedded, normed_one, qkv, attended = call(
        front_kernel,
        "s" + 8 * "v" + "h",
        [
            shape_of((tokens, width), f32),
            shape_of((length, width), bf16),
            shape_of((length, 3 * half_width), bf16),
            shape_of((length, half_width), bf16),
        ],
        [
            pltpu.VMEM((3, width, half_width), bf16),
            pltpu.VMEM((length + 8, width), f32),
            sem((3,)),
        ],
        (ids, *parts, base, allowed, vectors, embed_weight, qkv_weight),
        2 * length * width * 3 * half_width,
        FRONT_ROOM,
    )
    attended_peer = swap(attended, "narrow", 1)
    (
        latent,
        logdet,
        direct,
        normed_two,
        hidden,
        hidden_send,
        d_mlp,
        d_hidden,
        d_hidden_send,
        d_one,
        d_attn,
        gain_part_two,
        head_keep,
        head_send,
    ) = call(
        middle_kernel,
        "s" + 7 * "v" + "hhh",
        [
            shape_of((channels, quarter), f32),
            shape_of((1, quarter), f32),
            shape_of((channels, quarter), f32),
            shape_of((tokens, width), bf16),
            shape_of((tokens, ff), bf16),
            shape_of((tokens, ff), bf16),
            shape_of((tokens, width), bf16),
            shape_of((tokens, ff), bf16),
            shape_of((tokens, ff), bf16),
            shape_of((tokens, width), f32),
            shape_of((tokens, width), bf16),
            shape_of((1, width), f32),
            shape_of((width, LANES), f32),
            shape_of((width, LANES), bf16),
        ],
        [
            pltpu.VMEM((width, width), bf16),
            pltpu.VMEM((4, width, ff), bf16),
            pltpu.VMEM((4, ff, width), bf16),
            pltpu.VMEM((2, tokens, ff), bf16),
            pltpu.VMEM((2, tokens, ff), bf16),
            pltpu.VMEM((4, tokens, ff), f32),
            pltpu.VMEM((tokens, width), f32),
            pltpu.VMEM((tokens, width), bf16),
            sem((9,)),
        ],
        (
            ids,
            embedded,
            attended,
            attended_peer,
            vectors,
            head_weight.T,
            own_part,
            far_part,
            proj_weight,
            up_weight,
            down_weight,
        ),
        8 * tokens * width * hidden_width,
        40,
    )

    aligned = size % 16 == 0 and count > 1

    def block_shapes(cols):
        if aligned:
            return [shape_of((count // 2, size, cols), bf16)] * 2
        return [shape_of((width, cols), bf16)]

    def blocks_of(outs, steps):
        if aligned:
            return outs
        blocks = relative_blocks(outs[0], me, steps)
        return blocks[: max(1, count // 2)], blocks[max(1, count // 2) :]

    def stepped(kept, arrived):
        total = kept.astype(f32) + arrived.astype(f32)
        half = (total.shape[0] + 1) // 2
        return total[:half].astype(bf16), total[half:].astype(bf16)

    def join(*blocks):
        return [jnp.concatenate(pair, axis=2) for pair in zip(*blocks)]

    def four(part, turn):
        far_one = swap(part, "narrow", 2, turn)
        return [part, swap(part, "narrow", 1), far_one, swap(far_one, "narrow", 1)]

    d_attn_peer = swap(d_attn, "narrow", 1)
    normed_pair = normed_two, swap(normed_two, "narrow", 1)
    d_hidden_pair = d_hidden, swap(d_hidden_send, "narrow", 1)
    d_mlp_pair = d_mlp, swap(d_mlp, "narrow", 1)
    hidden_pair = hidden, swap(hidden_send, "narrow", 1)

    def pair_sum(steps, left, right):
        return blocks_of(
            call(
                functools.partial(pair_sum_kernel, size, steps),
                "svvvv",
                block_shapes(ff),
                [pltpu.VMEM((width, ff), f32)],
                (ids, *left, *right),
                4 * tokens * width * ff,
            ),
            steps,
        )

    up_blocks = pair_sum(near_steps, normed_pair, d_hidden_pair)
    down_blocks = pair_sum(far_steps, (after(d_mlp, *up_blocks), d_mlp_pair[1]), hidden_pair)
    up_in = swap(up_blocks[1], "dp", near_steps[0])
    down_in = swap(down_blocks[1], "dp", far_steps[0])
    d_qkv, d_normed, d_normed_send = call(
        back_attention_kernel,
        "s" + 5 * "v" + "h",
        [
            shape_of((length, 3 * half_width), bf16),
            shape_of((tokens, width), f32),
            shape_of((tokens, width), bf16),
        ],
        [
            pltpu.VMEM((length, half_width), bf16),
            pltpu.VMEM((3, width, half_width), bf16),
            sem((3,)),
        ],
        (
            ids,
            after(qkv, *up_blocks, *down_blocks),
            d_attn,
            d_attn_peer,
            proj_weight,
            allowed,
            qkv_weight,
        ),
        10 * length * length * half_width,
        28,
    )
    d_normed_peer = swap(d_normed_send, "narrow", 1)
    up_in, down_in, _ = lax.optimization_barrier((up_in, down_in, d_normed_send))
    up_blocks = stepped(up_blocks[0], up_in)
    down_blocks = stepped(down_blocks[0], down_in)
    up_in = swap(up_blocks[1], "dp", near_steps[1])
    down_in = swap(down_blocks[1], "dp", far_steps[1])
    [d_embed] = call(
        back_front_kernel,
        6 * "v",
        [shape_of((tokens + EXTRA, width), bf16)],
        [],
        (
            d_normed,
            after(d_normed_peer, *up_blocks, *down_blocks),
            embedded,
            d_one,
            vectors,
            gain_part_two,
        ),
        6 * tokens * width * width,
    )
    d_embed_peer = swap(d_embed, "narrow", 1)
    heads_outs = call(
        functools.partial(heads_sum_kernel, size, (near_steps, far_steps)),
        "s" + 6 * "v",
        2 * block_shapes(2 * group),
        [pltpu.VMEM((length, half_width), bf16), pltpu.VMEM((width, 4 * group), f32)],
        (ids, after(normed_one, d_embed), d_qkv, attended, attended_peer, d_attn, d_attn_peer),
        2 * length * width * 4 * group,
    )
    half_outs = len(heads_outs) // 2
    one_blocks = blocks_of(heads_outs[:half_outs], near_steps)
    two_blocks = blocks_of(heads_outs[half_outs:], far_steps)
    one_in = swap(one_blocks[1], "dp", near_steps[0], 1)
    two_in = swap(two_blocks[1], "dp", far_steps[0], 1)
    up_in, down_in, _, _ = lax.optimization_barrier(
        (up_in, down_in, one_blocks[0], two_blocks[0])
    )
    mlp_blocks = join(stepped(up_blocks[0], up_in), stepped(down_blocks[0], down_in))
    mlp_in = swap(mlp_blocks[1], "dp", near_steps[2])
    def class_blocks():
        def natural(mine, peers):
            a, b, c, d = mine[:quarter], mine[quarter:], peers[:quarter], peers[quarter:]
            return jnp.where(
                core == 0, jnp.concatenate([a, c, b, d]), jnp.concatenate([c, a, d, b])
            )

        segment_hot = (
            segment_ids[0][:, None] == jnp.arange(images, dtype=jnp.int32)[None, :]
        ).astype(bf16)
        label_hot = (
            labels[0][:, None] == jnp.arange(class_table.shape[0], dtype=jnp.int32)
        ).astype(bf16)
        segment_part = token_sum(natural(d_embed[:tokens], d_embed_peer[:tokens]), segment_hot)
        class_part = dot(segment_part.astype(bf16), label_hot)
        class_cols = class_table.shape[0] // 4
        part = jnp.concatenate(
            [
                lax.dynamic_slice_in_dim(class_part, r * class_cols, class_cols, 1),
                jnp.sum(segment_part, axis=1, keepdims=True),
            ],
            axis=1,
        )
        blocks = relative_blocks(part.astype(bf16), me, near_steps)
        return blocks[: count // 2], blocks[count // 2 :]

    *table_outs, patches_grad = call(
        functools.partial(
            table_sum_kernel, size, near_steps, (position_cols, embed_cols, slot_cols)
        ),
        "s" + 10 * "v",
        [*block_shapes(LANES), shape_of((channels, quarter), f32)],
        [
            pltpu.VMEM((length + 8, LANES), f32),
            pltpu.VMEM((tokens + EXTRA, LANES), bf16),
            pltpu.VMEM((tokens + EXTRA, LANES), bf16),
            pltpu.VMEM((quarter + EXTRA, width), f32),
            pltpu.VMEM((width, LANES), f32),
        ],
        (
            ids,
            d_embed,
            after(d_embed_peer, *mlp_blocks),
            *parts,
            head_keep,
            swap(head_send, "narrow", 1),
            direct,
            embed_weight,
        ),
        2 * length * width * LANES,
    )
    table_blocks = blocks_of(table_outs, near_steps)
    if not compact:
        table_blocks = join(table_blocks, class_blocks())
    table_in = swap(table_blocks[1], "dp", near_steps[0], 2)
    one_in, two_in, table_in = lax.optimization_barrier((one_in, two_in, table_in))
    one_blocks = join(stepped(one_blocks[0], one_in), stepped(table_blocks[0], table_in))
    two_blocks = stepped(two_blocks[0], two_in)
    one_in = swap(one_blocks[1], "dp", near_steps[1], 1)
    two_in = swap(two_blocks[1], "dp", far_steps[1], 1)
    one_in, two_in = lax.optimization_barrier((one_in, two_in))
    last_blocks = join(stepped(one_blocks[0], one_in), stepped(two_blocks[0], two_in))
    last_in = swap(last_blocks[1], "dp", near_steps[2], 1)

    def finished(blocks, arrived, turn, *others):
        kept = blocks[0]
        for step in near_steps[3:]:
            kept, sent = stepped(kept, arrived)
            arrived = swap(sent, "dp", step, turn)
        [part] = call(
            last_step_kernel,
            "vv",
            [shape_of(kept.shape[1:], bf16)],
            [],
            (kept, arrived),
            others=others,
        )
        return part

    mlp_parts = four(finished(mlp_blocks, mlp_in, 0, one_blocks[0], two_blocks[0]), 0)
    up_grad, down_grad = call(
        mlp_out_kernel,
        "svvvv",
        [shape_of((size, hidden_width), f32), shape_of((size, hidden_width), f32)],
        [],
        (ids, *mlp_parts),
        0,
    )
    last_part = finished(last_blocks, last_in, 1)
    last_far = after(swap(last_part, "narrow", 2, 1), up_grad)
    last_parts = [last_part, swap(last_part, "narrow", 1), last_far, swap(last_far, "narrow", 1)]
    last_shapes = [shape_of((size, 3 * width), f32), shape_of((size, width), f32)]
    last_scratch = [pltpu.VMEM((4, *last_part.shape), f32)]
    if compact:
        (
            qkv_grad,
            proj_grad,
            embed_grad,
            position_grad,
            class_grad,
            head_grad,
            gain_one,
            gain_two,
            bias,
        ) = call(
            functools.partial(
                last_out_kernel, (position_cols, embed_cols, slot_cols, head_cols, 2 * group)
            ),
            "svvvv",
            [
                *last_shapes,
                shape_of((channels, size), f32),
                shape_of((size, position_table.shape[0]), f32),
                shape_of((size, class_table.shape[0]), f32),
                shape_of((size, 2 * channels), f32),
                shape_of((1, size), f32),
                shape_of((1, size), f32),
                shape_of((1, size), f32),
            ],
            last_scratch,
            (ids, *last_parts),
            0,
        )
        attngain_grad, mlpgain_grad, bias_grad = gain_one[0], gain_two[0], bias[0]
    else:
        qkv_grad, proj_grad = call(
            heads_out_kernel, "svvvv", last_shapes, last_scratch, (ids, *last_parts), 0
        )
        shares = jnp.stack(last_parts).astype(f32)[:, :, 2 * group : -2 * group]
        shares = [lax.dynamic_index_in_dim(shares, r ^ i, 0, keepdims=False) for i in range(4)]
        class_cols = class_table.shape[0] // 4

        def joined(start, cols):
            return jnp.concatenate([share[:, start : start + cols] for share in shares], axis=1)

        position_grad = joined(0, position_cols)
        embed_grad = joined(position_cols, embed_cols).T
        class_grad = joined(LANES, class_cols)
        head_grad = joined(LANES - head_cols, head_cols)
        attngain_grad = shares[0][:, gain_at]
        mlpgain_grad = shares[0][:, gain_at + 1]
        bias_grad = shares[0][:, LANES + class_cols]
    return (
        latent.T[None],
        logdet,
        patches_grad.T[None],
        embed_grad,
        bias_grad,
        position_grad.T,
        class_grad.T,
        attngain_grad,
        qkv_grad,
        proj_grad,
        mlpgain_grad,
        up_grad,
        down_grad.T,
        head_grad,
    )


def solution(mesh):
    return jax.shard_map(
        shards,
        mesh=mesh,
        in_specs=(
            P("dp", "narrow", None),
            P("dp", None),
            P("dp", None),
            P(),
            P(),
            P(),
            P(),
            P(),
            P(),
            P(),
            P(),
            P(),
            P(),
            P(),
            P("dp", "narrow", None),
            P("dp", "narrow"),
        ),
        out_specs=(
            P("dp", "narrow", None),
            P("dp", "narrow"),
            P("dp", "narrow", None),
            P(None, "dp"),
            P("dp"),
            P(None, "dp"),
            P(None, "dp"),
            P("dp"),
            P("dp", None),
            P("dp", None),
            P("dp"),
            P("dp", None),
            P(None, "dp"),
            P("dp", None),
        ),
        check_vma=False,
    )
```

```python
import functools
import math

import jax
import jax.numpy as jnp
from jax import lax
from jax.experimental import pallas as pl
from jax.experimental.pallas import tpu as pltpu
from jax.sharding import PartitionSpec as P

HD = 64
UNIT = 64
BIG = 256
TILE = 128
EXTRA = 16
FRONT_ROOM = 28
MIDDLE_ROOM = 36
LANES = 128
bf16, f32 = jnp.bfloat16, jnp.float32
epsilon = 1e-05
masked_score = -1e30


def dot(left, right):
    return jnp.dot(left, right, preferred_element_type=f32)


def token_sum(left, right):
    return lax.dot_general(left, right, (((0,), (0,)), ((), ())), preferred_element_type=f32)


def back_dot(grads, weight):
    return lax.dot_general(grads, weight, (((1,), (1,)), ((), ())), preferred_element_type=f32)


def swap(value, axis, step, turn=0):
    count = lax.axis_size(axis)
    turned = [(i + turn) % count for i in range(count)]
    return lax.ppermute(value, axis, [(i, i ^ step) for i in turned])


def normalised(values):
    center = jnp.mean(values, axis=-1, keepdims=True)
    offsets = values - center
    inverse = lax.rsqrt(jnp.mean(offsets * offsets, axis=-1, keepdims=True) + epsilon)
    return offsets * inverse, inverse


def norm_back(grads, gain, normed, inverse):
    e = grads * gain
    mean_e = jnp.mean(e, axis=-1, keepdims=True)
    mean_en = jnp.mean(e * normed, axis=-1, keepdims=True)
    return inverse * (e - mean_e - normed * mean_en)


def halving_steps(count, far_first=False):
    steps = [1 << i for i in range(count.bit_length() - 1)]
    if far_first and len(steps) > 1:
        steps[:2] = steps[1], steps[0]
    return steps


def block_order(steps):
    order = [0]
    for step in reversed(steps):
        order = order + [j ^ step for j in order]
    return order


def relative_blocks(grad, me, steps):
    order = block_order(steps)
    size = grad.shape[0] // len(order)
    return jnp.stack([lax.dynamic_slice_in_dim(grad, (me ^ j) * size, size, 0) for j in order])


UNITS_AT = 2


def unit_firsts(ids_ref, units):
    firsts = [jnp.int32(0)]
    for u in range(1, units):
        same = ids_ref[UNITS_AT + u] == ids_ref[UNITS_AT + u - 1]
        firsts.append(jnp.where(same, firsts[-1], u))
    return firsts


def allowed_bias(row_start, firsts):
    begin, end = window_of(row_start)
    shape = (TILE, end - begin)
    row = lax.broadcasted_iota(jnp.int32, shape, 0)
    key = lax.broadcasted_iota(jnp.int32, shape, 1) + begin
    unit = row_start // UNIT
    first = jnp.where(row < UNIT, firsts[unit] * UNIT, firsts[unit + 1] * UNIT)
    return jnp.where((key >= first) & (key <= row + row_start), 0.0, masked_score)


def stacked(block, masks):
    return jnp.concatenate([block * masks[0], block * masks[1]])


def head_masks():
    lane = lax.broadcasted_iota(jnp.int32, (1, 2 * HD), 1)
    low = (lane < HD).astype(f32)
    return low.astype(bf16), (1.0 - low).astype(bf16)


def window_of(start):
    return max(0, start - BIG), start + TILE


def pick(rows, lanes, to_lane):
    row = lax.broadcasted_iota(jnp.int32, (rows, lanes), 0)
    lane = lax.broadcasted_iota(jnp.int32, (rows, lanes), 1)
    return to_lane(row, lane).astype(f32).astype(bf16)


def base_kernel(
    ids_ref, vector_ref, class_ref, position_hbm, base_ref, allowed_ref, position_ref, image_rows, sems
):
    table = pltpu.make_async_copy(position_hbm, position_ref, sems.at[0])
    table.start()
    length = base_ref.shape[0]
    units = length // UNIT
    firsts = unit_firsts(ids_ref, units)
    for start in range(0, length, TILE):
        begin, end = window_of(start)
        allowed_ref[start : start + TILE, : end - begin] = allowed_bias(start, firsts)
    shape = (image_rows.shape[0], class_ref.shape[0])
    row = lax.broadcasted_iota(jnp.int32, shape, 0)
    label = jnp.full(shape, -1, jnp.int32)
    for s in range(ids_ref.shape[0] - UNITS_AT - units):
        label = jnp.where(row == s, ids_ref[UNITS_AT + units + s], label)
    hot = (lax.broadcasted_iota(jnp.int32, shape, 1) == label).astype(f32).astype(bf16)
    image_rows[...] = dot(hot, class_ref[...]) + vector_ref[0:1, :].astype(f32)
    table.wait()
    for u in range(units):
        block = u - firsts[u]
        table = position_ref[pl.ds(pl.multiple_of(block * UNIT, UNIT), UNIT), :]
        image = image_rows[pl.ds(ids_ref[UNITS_AT + u], 1), :]
        base_ref[u * UNIT : (u + 1) * UNIT, :] = table.astype(f32) + image


def embed_kernel(
    ids_ref,
    part_0_ref,
    part_1_ref,
    part_2_ref,
    part_3_ref,
    base_ref,
    vector_ref,
    embed_ref,
    embedded_ref,
    normed_ref,
    patch_rows,
):
    length, width = normed_ref.shape
    quarter = length // 4
    channels = embed_ref.shape[0]
    place = ids_ref[1]
    core = place & 1
    firsts = unit_firsts(ids_ref, length // UNIT)
    patch_rows[0:8, :] = jnp.zeros((8, width), f32)
    for j, part in enumerate((part_0_ref, part_1_ref, part_2_ref, part_3_ref)):
        at = pl.multiple_of((place ^ j) * quarter + 8, 8)
        patch_rows[pl.ds(at, quarter), :] = token_sum(part[:channels, :], embed_ref[...])
    gain = vector_ref[1:2, :].astype(f32)
    inner = lax.broadcasted_iota(jnp.int32, (UNIT, width), 0)
    for u in range(length // UNIT):
        rows = slice(u * UNIT, (u + 1) * UNIT)
        before = patch_rows[u * UNIT + 7 : u * UNIT + 7 + UNIT, :]
        before = jnp.where((inner == 0) & (firsts[u] == u), 0.0, before)
        values = before + base_ref[rows, :]
        q = u * UNIT // quarter
        inside = (q >> 1) * quarter + u * UNIT - q * quarter

        @pl.when(core == (q & 1))
        def _():
            embedded_ref[pl.ds(inside, UNIT), :] = values

        normed_ref[rows, :] = (normalised(values)[0] * gain).astype(bf16)


def attention_kernel(
    ids_ref, normed_ref, allowed, weight_ref, qkv_ref, attended_ref, own_weight, sems
):
    length, width = normed_ref.shape
    half = width // 2
    core = ids_ref[1] & 1
    copies = []
    for t in range(3):
        start = pl.multiple_of(t * width + core * half, 128)
        copies.append(
            pltpu.make_async_copy(weight_ref.at[:, pl.ds(start, half)], own_weight.at[t], sems.at[t])
        )
        copies[-1].start()
    starts = range(0, length, TILE)
    for t in range(3):
        copies[t].wait()
        qkv_ref[:, t * half : (t + 1) * half] = dot(normed_ref[...], own_weight[t]).astype(bf16)
    masks = head_masks()
    low_lanes = lax.broadcasted_iota(jnp.int32, (TILE, 2 * HD), 1) < HD

    def pair_step(pair, carry):
        lanes = [pl.ds(pl.multiple_of(t * half + pair * 2 * HD, 128), 2 * HD) for t in range(3)]
        scores = []
        for start in starts:
            begin, end = window_of(start)
            q = stacked(qkv_ref[start : start + TILE, lanes[0]], masks)
            scores.append(back_dot(q, qkv_ref[begin:end, lanes[1]]))
        raised, totals = [], []
        for start, block in zip(starts, scores):
            begin, end = window_of(start)
            bias = allowed[start : start + TILE, : end - begin]
            masked = block * (1.0 / math.sqrt(HD)) + jnp.concatenate([bias, bias])
            power = jnp.exp(masked - jnp.max(masked, axis=-1, keepdims=True))
            raised.append(power.astype(bf16))
            totals.append(1.0 / jnp.sum(power, axis=-1, keepdims=True))
        for start, power, inverse in zip(starts, raised, totals):
            begin, end = window_of(start)
            out = dot(power, qkv_ref[begin:end, lanes[2]]) * inverse
            attended_ref[start : start + TILE, lanes[0]] = jnp.where(
                low_lanes, out[:TILE], out[TILE:]
            ).astype(bf16)
        return carry

    lax.fori_loop(0, half // (2 * HD), pair_step, 0, unroll=True)


def back_attention_kernel(
    ids_ref,
    qkv_ref,
    mine_ref,
    peer_ref,
    proj_ref,
    allowed,
    weight_hbm,
    grads,
    own_ref,
    send_ref,
    mixed,
    own_weight,
    sems,
):
    length = qkv_ref.shape[0]
    half = qkv_ref.shape[1] // 3
    quarter = length // 4
    core = ids_ref[1] & 1
    width = weight_hbm.shape[0]
    copies = []
    for t in range(3):
        start = pl.multiple_of(t * width + core * half, 128)
        copies.append(
            pltpu.make_async_copy(weight_hbm.at[:, pl.ds(start, half)], own_weight.at[t], sems.at[t])
        )
        copies[-1].start()
    proj = proj_ref[pl.ds(pl.multiple_of(core * half, 128), half), :]
    for ref, side in ((mine_ref, core), (peer_ref, 1 - core)):
        product = back_dot(ref[...], proj).astype(bf16)
        for i in range(2):
            rows = pl.ds(pl.multiple_of((2 * i + side) * quarter, 16), quarter)
            mixed[rows, :] = product[i * quarter : (i + 1) * quarter]
    masks = head_masks()
    low_lanes = lax.broadcasted_iota(jnp.int32, (TILE, 2 * HD), 1) < HD
    scale = 1.0 / math.sqrt(HD)
    starts = range(0, length, TILE)

    def pair_step(pair, carry):
        lanes = [pl.ds(pl.multiple_of(t * half + pair * 2 * HD, 128), 2 * HD) for t in range(3)]
        queries, outer, scores, d_weights = [], [], [], []
        for start in starts:
            begin, end = window_of(start)
            queries.append(stacked(qkv_ref[start : start + TILE, lanes[0]], masks))
            outer.append(stacked(mixed[start : start + TILE, lanes[0]], masks))
            scores.append(back_dot(queries[-1], qkv_ref[begin:end, lanes[1]]))
            d_weights.append(back_dot(outer[-1], qkv_ref[begin:end, lanes[2]]))
        weights, d_scores = [], []
        for start, block, d_block in zip(starts, scores, d_weights):
            begin, end = window_of(start)
            bias = allowed[start : start + TILE, : end - begin]
            masked = block * scale + jnp.concatenate([bias, bias])
            power = jnp.exp(masked - jnp.max(masked, axis=-1, keepdims=True))
            weight = power * (1.0 / jnp.sum(power, axis=-1, keepdims=True))
            centre = jnp.sum(weight * d_block, axis=-1, keepdims=True)
            weights.append(weight.astype(bf16))
            d_scores.append((weight * (d_block - centre)).astype(bf16))
        for i, start in enumerate(starts):
            begin, end = window_of(start)
            out = dot(d_scores[i], qkv_ref[begin:end, lanes[1]])
            grads[start : start + TILE, lanes[0]] = (
                jnp.where(low_lanes, out[:TILE], out[TILE:]) * scale
            ).astype(bf16)
        d_keys = [token_sum(d, q) for d, q in zip(d_scores, queries)]
        d_values = [token_sum(w, o) for w, o in zip(weights, outer)]
        for at in starts:
            for t, sums, factor in ((1, d_keys, scale), (2, d_values, 1.0)):
                total = None
                for start, block in zip(starts, sums):
                    begin, end = window_of(start)
                    if begin <= at < end:
                        term = block[at - begin : at - begin + TILE]
                        total = term if total is None else total + term
                grads[at : at + TILE, lanes[t]] = (total * factor).astype(bf16)
        return carry

    lax.fori_loop(0, half // (2 * HD), pair_step, 0, unroll=True)
    for copy in copies:
        copy.wait()
    for ref, side in ((send_ref, 1 - core), (own_ref, core)):
        for i in range(2):
            rows = pl.ds(pl.multiple_of((2 * i + side) * quarter, 16), quarter)
            total = None
            for t in range(3):
                term = back_dot(grads[rows, t * half : (t + 1) * half], own_weight[t])
                total = term if total is None else total + term
            ref[i * quarter : (i + 1) * quarter, :] = total.astype(ref.dtype)


def middle_kernel(
    ids_ref,
    embedded_ref,
    own_ref,
    peer_ref,
    gain_ref,
    head_weight_ref,
    near_ref,
    far_ref,
    proj_hbm,
    up_hbm,
    down_hbm,
    latent_ref,
    logdet_ref,
    direct_ref,
    normed_ref,
    hidden_ref,
    hidden_send_ref,
    d_mlp_ref,
    d_hidden_ref,
    d_hidden_send_ref,
    d_hidden_rest,
    stream,
    d_two_ref,
    head_ref,
    head_send_ref,
    proj,
    up,
    down,
    hidden_rest,
    slope,
    low,
    sems,
):
    tokens, width = embedded_ref.shape
    quarter = tokens // 2
    half = width // 2
    ff = up.shape[2]
    place = ids_ref[1]
    core, far = place & 1, place >> 1
    channels = latent_ref.shape[0]
    hiddens = hidden_ref, hidden_send_ref, hidden_rest.at[0], hidden_rest.at[1]
    d_hiddens = d_hidden_ref, d_hidden_send_ref, d_hidden_rest.at[0], d_hidden_rest.at[1]
    copies = [pltpu.make_async_copy(proj_hbm, proj, sems.at[0])]
    copies[0].start()
    for j in range(4):
        columns = pl.ds(pl.multiple_of((place ^ j) * ff, 128), ff)
        copies.append(pltpu.make_async_copy(up_hbm.at[:, columns], up.at[j], sems.at[1 + j]))
        copies[-1].start()
    for j in range(4):
        rows = pl.ds(pl.multiple_of((place ^ j) * ff, 128), ff)
        copies.append(pltpu.make_async_copy(down_hbm.at[rows, :], down.at[j], sems.at[5 + j]))
        copies[-1].start()
    copies[0].wait()
    gain = gain_ref[2:3, :].astype(f32)
    for i in range(2):
        source = pl.ds(pl.multiple_of((2 * i + core) * quarter, 16), quarter)
        rows = slice(i * quarter, (i + 1) * quarter)
        values = embedded_ref[rows, :]
        for ref, side in ((own_ref, core), (peer_ref, 1 - core)):
            weight = proj[pl.ds(pl.multiple_of(side * half, 128), half), :]
            values += dot(ref[source, :], weight)
        stream[rows, :] = values
        normed_ref[rows, :] = (normalised(values)[0] * gain).astype(bf16)
    for j in range(4):
        copies[1 + j].wait()

        pre = dot(normed_ref[...], up[j])
        cdf = 0.5 * (1.0 + lax.erf(pre * math.sqrt(0.5)))
        density = jnp.exp(-0.5 * pre * pre) * (1.0 / math.sqrt(2 * math.pi))
        slope[j] = cdf + pre * density
        value = (pre * cdf).astype(bf16)
        hiddens[j][...] = value
    total = stream[...]
    for j in range(4):
        copies[5 + j].wait()
        total += dot(hiddens[j][...], down[j])
    low[...] = total.astype(bf16)
    head_sums = [jnp.zeros(head_ref.shape, f32)] * 2
    head_cols = channels // 2
    lane_at = LANES - head_cols
    for i in range(2):
        rows = slice(i * quarter, (i + 1) * quarter)
        part = jnp.where(far == i, near_ref[...].astype(f32), far_ref[...].astype(f32))
        patches, cot = part[:channels], part[channels : 2 * channels]
        logdet_cot = jnp.sum(part[2 * channels :], axis=0, keepdims=True)
        head_out = back_dot(head_weight_ref[...], low[rows, :])
        mean_shift, logscale = head_out[:channels], head_out[channels:]
        factor = jnp.exp(-logscale)
        latent = (patches - mean_shift) * factor
        direct = cot * factor

        @pl.when(far == i)
        def _():
            latent_ref[...] = latent
            logdet_ref[...] = -jnp.sum(logscale, axis=0, keepdims=True)
            direct_ref[...] = direct

        d_head = jnp.concatenate([-direct, -cot * latent - logdet_cot]).astype(bf16)
        d_two = token_sum(d_head, head_weight_ref[...])
        d_two_ref[rows, :] = d_two
        d_mlp_ref[rows, :] = d_two.astype(bf16)
        for k, index in enumerate((place, place ^ 1)):
            chosen = pick(
                2 * channels,
                LANES,
                lambda row, lane: (lane - lane_at + index * head_cols == row) & (lane >= lane_at),
            )
            columns = token_sum(d_head, chosen).astype(bf16)
            head_sums[k] += token_sum(low[rows, :], columns)
    head_ref[...] = head_sums[0]
    head_send_ref[...] = head_sums[1].astype(bf16)
    for j in range(4):
        value = (back_dot(d_mlp_ref[...], down[j]) * slope[j]).astype(bf16)
        d_hiddens[j][...] = value


def turn_kernel(
    ids_ref,
    d_hidden_ref,
    d_hidden_send_ref,
    d_hidden_rest,
    up_ref,
    stream,
    d_two_ref,
    gain_ref,
    d_one_ref,
    d_attn_ref,
    gain_part_ref,
):
    tokens, width = stream.shape
    quarter = tokens // 2
    ff = d_hidden_ref.shape[1]
    place = ids_ref[1]
    gain = gain_ref[2:3, :].astype(f32)
    d_hiddens = d_hidden_ref, d_hidden_send_ref, d_hidden_rest.at[0], d_hidden_rest.at[1]
    grads = jnp.zeros((tokens, width), f32)
    for j, d_hidden in enumerate(d_hiddens):
        columns = pl.ds(pl.multiple_of((place ^ j) * ff, 128), ff)
        grads += back_dot(d_hidden[...], up_ref[:, columns])
    for i in range(2):
        rows = slice(i * quarter, (i + 1) * quarter)
        share = grads[rows]
        n, inverse = normalised(stream[rows, :])
        part = jnp.sum(share * n, axis=0, keepdims=True)
        gain_part_ref[...] = part if i == 0 else gain_part_ref[...] + part
        d_one = d_two_ref[rows, :] + norm_back(share, gain, n, inverse)
        d_one_ref[rows, :] = d_one
        d_attn_ref[rows, :] = d_one.astype(bf16)


def back_front_kernel(
    own_ref,
    peer_ref,
    embedded_ref,
    d_one_ref,
    gain_ref,
    part_ref,
    d_embed_ref,
):
    tokens, width = embedded_ref.shape
    gain = gain_ref[1:2, :].astype(f32)
    step = tokens // 6
    total = jnp.zeros((1, width), f32)
    for i in range(6):
        rows = slice(i * step, (i + 1) * step)
        grads = own_ref[rows, :] + peer_ref[rows, :].astype(f32)
        n, inverse = normalised(embedded_ref[rows, :])
        total += jnp.sum(grads * n, axis=0, keepdims=True)
        d_embed_ref[rows, :] = (d_one_ref[rows, :] + norm_back(grads, gain, n, inverse)).astype(
            bf16
        )
    row = lax.broadcasted_iota(jnp.int32, (EXTRA, width), 0)
    both = jnp.where(row % 2 == 0, total, part_ref[...])
    coarse = both.astype(bf16).astype(f32)
    rest = jnp.where(row < 2, coarse, jnp.where(row < 4, both - coarse, 0.0))
    d_embed_ref[tokens : tokens + EXTRA, :] = rest.astype(bf16)


def place_blocks(total, outs, me, size, steps, start=0):
    columns = slice(start, start + outs[0].shape[-1])
    if len(outs) == 1:
        outs[0][...] = total[:, columns].astype(bf16)
        return
    keep, send = outs
    for k, j in enumerate(block_order(steps)):
        block = total[pl.ds(pl.multiple_of((me ^ j) * size, 16), size), columns].astype(bf16)
        if k < keep.shape[0]:
            keep[k] = block
        else:
            send[k - keep.shape[0]] = block


def pair_sum_kernel(size, steps, ids_ref, left_ref, left_peer_ref, right_ref, right_peer_ref, *rest):
    *outs, total = rest
    columns = total.shape[1]
    total[...] = token_sum(left_ref[...], right_ref[:, :columns]) + token_sum(
        left_peer_ref[...], right_peer_ref[:, :columns]
    )
    place_blocks(total, outs, ids_ref[0], size, steps)


def heads_part(total, at, t, normed_ref, d_qkv_ref, far):
    half = d_qkv_ref.shape[1] // 3
    group = half // 2
    low = d_qkv_ref[:, t * half : t * half + group]
    high = d_qkv_ref[:, t * half + group : (t + 1) * half]
    picked = jnp.where(far == 0, low.astype(f32), high.astype(f32)).astype(bf16)
    total[:, at : at + group] = token_sum(normed_ref[...], picked)


def queries_sum_kernel(size, steps, ids_ref, normed_ref, d_qkv_ref, *rest):
    *outs, total = rest
    for t in range(2):
        heads_part(total, t * total.shape[1] // 2, t, normed_ref, d_qkv_ref, ids_ref[1] >> 1)
    place_blocks(total, outs, ids_ref[0], size, steps)


def values_sum_kernel(
    size,
    steps,
    ids_ref,
    normed_ref,
    d_qkv_ref,
    attended_ref,
    attended_peer_ref,
    d_attn_ref,
    d_attn_peer_ref,
    *rest,
):
    *outs, natural, total = rest
    place = ids_ref[1]
    core, far = place & 1, place >> 1
    length, width = normed_ref.shape
    quarter, half = length // 4, width // 2
    group = half // 2
    heads_part(total, 0, 2, normed_ref, d_qkv_ref, far)
    columns = pl.ds(pl.multiple_of(far * half, 128), half)
    for ref, side in ((d_attn_ref, core), (d_attn_peer_ref, 1 - core)):
        for i in range(2):
            rows = pl.ds(pl.multiple_of((2 * i + side) * quarter, 16), quarter)
            natural[rows, :] = ref[i * quarter : (i + 1) * quarter, columns]
    for ref, side in ((attended_ref, core), (attended_peer_ref, 1 - core)):
        sums = token_sum(ref[...], natural[...])
        rows = pl.ds(pl.multiple_of(side * half, 16), half)
        total[rows, group:] = jnp.where(core == 0, sums[:, :group], sums[:, group:])
    place_blocks(total, outs, ids_ref[0], size, steps)


def table_sum_kernel(
    size,
    steps,
    plan,
    ids_ref,
    d_ref,
    d_peer_ref,
    part_0_ref,
    part_1_ref,
    part_2_ref,
    part_3_ref,
    head_ref,
    head_peer_ref,
    direct_ref,
    embed_ref,
    *rest,
):
    *outs, patches_ref, before_rows, to_own, to_peer, following, total = rest
    position_cols, embed_cols, slot_cols = plan
    slot_at = position_cols + embed_cols
    label_at = slot_at + slot_cols
    gain_at = label_at + 2
    me, place = ids_ref[0], ids_ref[1]
    core, far = place & 1, place >> 1
    channels, quarter = direct_ref.shape
    tokens = 2 * quarter
    length = 2 * tokens
    units = length // UNIT
    labels_at = UNITS_AT + units
    images = ids_ref.shape[0] - labels_at
    parts = (part_0_ref, part_1_ref, part_2_ref, part_3_ref)
    chosen = pick(
        part_0_ref.shape[0],
        LANES,
        lambda row, lane: (row == lane - position_cols + place * embed_cols)
        & (lane >= position_cols)
        & (lane < slot_at),
    )
    before_rows[0:8, :] = jnp.zeros((8, LANES), f32)
    for j, part in enumerate(parts):
        at = pl.multiple_of((place ^ j) * quarter + 8, 8)
        before_rows[pl.ds(at, quarter), :] = token_sum(part[...], chosen)
    firsts = unit_firsts(ids_ref, units)
    row = lax.broadcasted_iota(jnp.int32, (UNIT, LANES), 0)
    lane = lax.broadcasted_iota(jnp.int32, (UNIT, LANES), 1)
    for u in range(length // UNIT):
        block = u - firsts[u]
        before = before_rows[u * UNIT + 7 : u * UNIT + 7 + UNIT, :]
        before = jnp.where((row == 0) & (block == 0), 0.0, before)
        position = lane + place * position_cols == row + block * UNIT
        slot = lane - slot_at + place * slot_cols == me * images + ids_ref[UNITS_AT + u]
        ones = ((lane < position_cols) & position) | (
            (lane >= slot_at) & (lane < label_at) & slot
        )
        value = jnp.where(ones, 1.0, before).astype(bf16)
        q = u * UNIT // quarter
        inside = (q >> 1) * quarter + u * UNIT - q * quarter

        @pl.when(core == (q & 1))
        def _():
            to_own[inside : inside + UNIT, :] = value

        @pl.when(core != (q & 1))
        def _():
            to_peer[inside : inside + UNIT, :] = value

    gain_rows = pick(EXTRA, LANES, lambda row, lane: (lane == gain_at + row % 2) & (row < 4))
    to_own[tokens:, :] = gain_rows
    to_peer[tokens:, :] = gain_rows
    total[...] = (
        token_sum(d_ref[...], to_own[...])
        + token_sum(d_peer_ref[...], to_peer[...])
        + head_ref[...]
        + head_peer_ref[...].astype(f32)
    )
    if slot_cols:
        row = lax.broadcasted_iota(jnp.int32, (size, LANES), 0)
        lane = lax.broadcasted_iota(jnp.int32, (size, LANES), 1)
        label = jnp.zeros((size, LANES), jnp.int32)
        for s in range(images):
            label = jnp.where(row == me * images + s, ids_ref[labels_at + s], label)
        code = jnp.where(
            lane == label_at, label >> 3, jnp.where(lane == label_at + 1, label & 7, 0)
        ).astype(f32)
        for b in range(total.shape[0] // size):
            total[b * size : (b + 1) * size, :] += code
    place_blocks(total, outs, me, size, steps)
    following[:quarter, :] = d_ref[pl.ds(pl.multiple_of(far * quarter, 16), quarter), :].astype(f32)
    at = pl.multiple_of(((place + 1) >> 1) * quarter, 16)
    following[quarter:, :] = d_peer_ref[pl.ds(at, EXTRA), :].astype(f32)
    row = lax.broadcasted_iota(jnp.int32, (quarter, following.shape[1]), 0)
    dropped = (row == quarter - 1) & (place == 3)
    for w in range(1, quarter // UNIT + 1):
        u = jnp.minimum(place * (quarter // UNIT) + w, units - 1)
        opens = ids_ref[UNITS_AT + u] != ids_ref[UNITS_AT + u - 1]
        dropped = dropped | ((row == w * UNIT - 1) & opens)
    shifted = jnp.where(dropped, 0.0, following[1 : quarter + 1, :]).astype(bf16)
    patches_ref[...] = direct_ref[...] + back_dot(embed_ref[...], shifted)


def mlp_out_kernel(ids_ref, *refs):
    *parts, up_ref, down_ref = refs
    ff = up_ref.shape[1] // 4
    for j, part in enumerate(parts):
        columns = pl.ds(pl.multiple_of((ids_ref[1] ^ j) * ff, 128), ff)
        up_ref[:, columns] = part[:, :ff].astype(f32)
        down_ref[:, columns] = part[:, ff:].astype(f32)


def heads_out(stack, qkv_ref, proj_ref):
    width = proj_ref.shape[1]
    group = width // 4
    starts = (0, group, -2 * group, -group)
    for i, q in enumerate((0, 2, 1, 3)):
        for t, start in enumerate(starts[:3]):
            put = t * width + i * group
            qkv_ref[:, put : put + group] = stack[q, :, start % stack.shape[2] : start % stack.shape[2] + group]
        proj_ref[:, i * group : (i + 1) * group] = stack[i, :, stack.shape[2] - group :]


def heads_out_kernel(ids_ref, *refs):
    *parts, qkv_ref, proj_ref, stack = refs
    for j, part in enumerate(parts):
        stack[ids_ref[1] ^ j] = part[...].astype(f32)
    heads_out(stack, qkv_ref, proj_ref)


def last_out_kernel(plan, ids_ref, *refs):
    *parts, qkv_ref, proj_ref, embed_ref, position_ref, class_ref, head_ref, gain_one_ref, gain_two_ref, bias_ref, stack = refs
    position_cols, embed_cols, slot_cols, head_cols, at = plan
    slot_at = position_cols + embed_cols
    label_at = slot_at + slot_cols
    gain_at = label_at + 2
    head_at = LANES - head_cols
    for j, part in enumerate(parts):
        stack[ids_ref[1] ^ j] = part[...].astype(f32)
    heads_out(stack, qkv_ref, proj_ref)
    embed = position = head = slots = bias = None

    def added(total, term):
        return term if total is None else total + term

    for q in range(4):
        part = stack[q, :, at : at + LANES].astype(bf16)

        def placed(start, cols):
            return pick(
                LANES,
                4 * cols,
                lambda row, lane: (lane == row - start + q * cols)
                & (row >= start)
                & (row < start + cols),
            )

        position = added(position, dot(part, placed(0, position_cols)))
        head = added(head, dot(part, placed(head_at, head_cols)))
        slots = added(slots, dot(part, placed(slot_at, slot_cols)))
        chosen = pick(
            embed_ref.shape[0],
            LANES,
            lambda row, lane: (row == lane - position_cols + q * embed_cols)
            & (lane >= position_cols)
            & (lane < slot_at),
        )
        embed = added(embed, back_dot(chosen, part))
        chosen = pick(
            8, LANES, lambda row, lane: (row == 0) & (lane >= slot_at) & (lane < label_at)
        )
        bias = added(bias, back_dot(chosen, part))
    embed_ref[...] = embed
    position_ref[...] = position
    head_ref[...] = head
    bias_ref[...] = bias[0:1, :]
    first = stack[0, :, at : at + LANES].astype(bf16)
    gains = back_dot(pick(8, LANES, lambda row, lane: (lane == row + gain_at) & (row < 2)), first)
    gain_one_ref[...] = gains[0:1, :]
    gain_two_ref[...] = gains[1:2, :]
    codes = stack[0, :, at : at + LANES]
    coded = codes[:, label_at : label_at + 1] * 8.0 + codes[:, label_at + 1 : label_at + 2]
    shape = (4 * slot_cols, class_ref.shape[1])
    label = jnp.broadcast_to(coded[: 4 * slot_cols].astype(jnp.int32), shape)
    hot = (lax.broadcasted_iota(jnp.int32, shape, 1) == label).astype(f32).astype(bf16)
    class_ref[...] = dot(slots.astype(bf16), hot)


def after(value, *others):
    return lax.optimization_barrier((value, *others))[0]


def shape_of(dims, dtype):
    return jax.ShapeDtypeStruct(dims, dtype)


def call(kernel, places, outs, scratch, operands, flops=0, room=16, others=()):
    spaces = {
        "s": pl.BlockSpec(memory_space=pltpu.SMEM),
        "v": pl.BlockSpec(memory_space=pltpu.VMEM),
        "h": pl.BlockSpec(memory_space=pltpu.HBM),
    }
    taken = len(operands)

    def body(*refs):
        kernel(*refs[:taken], *refs[taken + len(others) :])

    return pl.pallas_call(
        body,
        name=getattr(kernel, "func", kernel).__name__,
        out_shape=outs,
        in_specs=[spaces[p] for p in places] + [pl.BlockSpec(memory_space=pl.ANY)] * len(others),
        out_specs=[spaces["v"]] * len(outs),
        scratch_shapes=scratch,
        compiler_params=pltpu.CompilerParams(vmem_limit_bytes=room * 2**20),
    )(*operands, *others)


def groups_kernel(groups, *refs):
    count = 2 * sum(groups)
    pairs, outs = iter(refs[:count]), iter(refs[count:])
    for group in groups:
        sums, start = None, 0
        for _ in range(group):
            kept, arrived = next(pairs), next(pairs)
            columns = slice(start, start + kept.shape[2])
            start = columns.stop
            if sums is None:
                sums = [next(outs)] if kept.shape[0] == 1 else [next(outs), next(outs)]
            half = (kept.shape[0] + 1) // 2
            for k, out in enumerate(sums):
                rows = slice(k * half, (k + 1) * half)
                out[:, :, columns] = (kept[rows].astype(f32) + arrived[rows].astype(f32)).astype(bf16)


def last_step_kernel(kept_ref, arrived_ref, out_ref):
    out_ref[...] = (kept_ref[0].astype(f32) + arrived_ref[0].astype(f32)).astype(bf16)


def shards(
    patches,
    segment_ids,
    labels,
    embed_weight,
    embed_bias,
    position_table,
    class_table,
    attn_gain,
    qkv_weight,
    proj_weight,
    mlp_gain,
    up_weight,
    down_weight,
    head_weight,
    latent_grad,
    logdet_grad,
):
    _, quarter, channels = patches.shape
    length = segment_ids.shape[1]
    width = qkv_weight.shape[0]
    hidden_width = up_weight.shape[1]
    tokens = 2 * quarter
    ff = hidden_width // 4
    half_width = width // 2
    group = half_width // 2
    count = lax.axis_size("dp")
    me = lax.axis_index("dp")
    r = lax.axis_index("narrow")
    core = r & 1
    ids = jnp.concatenate(
        [jnp.stack([me, r]).astype(jnp.int32), segment_ids[0, ::UNIT], labels[0]]
    )
    line = jnp.arange(8, dtype=jnp.int32)[:, None]
    vectors = jnp.where(
        line == 0, embed_bias[None], jnp.where(line == 1, attn_gain[None], mlp_gain[None])
    )
    near_steps, far_steps = halving_steps(count), halving_steps(count, True)
    size = width // count
    sem = pltpu.SemaphoreType.DMA

    images = labels.shape[1]
    slots = images * count
    position_cols, embed_cols = position_table.shape[0] // 4, channels // 4
    head_cols = channels // 2
    slot_cols = slots // 4
    compact = position_cols + embed_cols + slot_cols + 4 + head_cols <= LANES and slots <= size
    slot_cols = slot_cols if compact else 0
    gain_at = position_cols + embed_cols + slot_cols + 2

    coarse = lax.reduce_precision(logdet_grad, 8, 7)
    own_part = jnp.concatenate(
        [
            patches[0].T,
            latent_grad[0].T,
            coarse.astype(bf16),
            (logdet_grad - coarse).astype(bf16),
        ]
    )
    far_part = swap(own_part, "narrow", 2)
    parts = [
        own_part,
        swap(own_part, "narrow", 1),
        far_part,
        swap(far_part, "narrow", 1),
    ]
    base, allowed = call(
        base_kernel,
        "svvh",
        [shape_of((length, width), f32), shape_of((length, BIG + TILE), f32)],
        [
            pltpu.VMEM(position_table.shape, bf16),
            pltpu.VMEM((16, width), f32),
            sem((1,)),
        ],
        (ids, vectors, class_table, position_table),
        2 * 16 * width * class_table.shape[0],
    )
    embedded, normed_one = call(
        embed_kernel,
        "s" + 7 * "v",
        [shape_of((tokens, width), f32), shape_of((length, width), bf16)],
        [pltpu.VMEM((length + 8, width), f32)],
        (ids, *parts, base, vectors, embed_weight),
    )
    qkv, attended = call(
        attention_kernel,
        "svvh",
        [shape_of((length, 3 * half_width), bf16), shape_of((length, half_width), bf16)],
        [pltpu.VMEM((3, width, half_width), bf16), sem((3,))],
        (ids, normed_one, allowed, qkv_weight),
        0,
        FRONT_ROOM,
    )
    attended_peer = swap(attended, "narrow", 1)
    (
        latent,
        logdet,
        direct,
        normed_two,
        hidden,
        hidden_send,
        d_mlp,
        d_hidden,
        d_hidden_send,
        d_hidden_rest,
        stream,
        d_two,
        head_keep,
        head_send,
    ) = call(
        middle_kernel,
        "s" + 7 * "v" + "hhh",
        [
            shape_of((channels, quarter), f32),
            shape_of((1, quarter), f32),
            shape_of((channels, quarter), f32),
            shape_of((tokens, width), bf16),
            shape_of((tokens, ff), bf16),
            shape_of((tokens, ff), bf16),
            shape_of((tokens, width), bf16),
            shape_of((tokens, ff), bf16),
            shape_of((tokens, ff), bf16),
            shape_of((2, tokens, ff), bf16),
            shape_of((tokens, width), f32),
            shape_of((tokens, width), f32),
            shape_of((width, LANES), f32),
            shape_of((width, LANES), bf16),
        ],
        [
            pltpu.VMEM((width, width), bf16),
            pltpu.VMEM((4, width, ff), bf16),
            pltpu.VMEM((4, ff, width), bf16),
            pltpu.VMEM((2, tokens, ff), bf16),
            pltpu.VMEM((4, tokens, ff), f32),
            pltpu.VMEM((tokens, width), bf16),
            sem((9,)),
        ],
        (
            ids,
            embedded,
            attended,
            attended_peer,
            vectors,
            head_weight.T,
            own_part,
            far_part,
            proj_weight,
            up_weight,
            down_weight,
        ),
        8 * tokens * width * hidden_width,
        MIDDLE_ROOM,
    )

    aligned = size % 16 == 0 and count > 1

    def block_shapes(cols):
        if aligned:
            return [shape_of((count // 2, size, cols), bf16)] * 2
        return [shape_of((width, cols), bf16)]

    def blocks_of(outs, steps):
        if aligned:
            return outs
        blocks = relative_blocks(outs[0], me, steps)
        return blocks[: max(1, count // 2)], blocks[max(1, count // 2) :]

    def stepped(kept, arrived):
        total = kept.astype(f32) + arrived.astype(f32)
        half = (total.shape[0] + 1) // 2
        return total[:half].astype(bf16), total[half:].astype(bf16)

    def join(*blocks):
        return [jnp.concatenate(pair, axis=2) for pair in zip(*blocks)]

    def four(part, turn):
        far_one = swap(part, "narrow", 2, turn)
        return [part, swap(part, "narrow", 1), far_one, swap(far_one, "narrow", 1)]

    d_one, d_attn, gain_part_two = call(
        turn_kernel,
        "s" + 7 * "v",
        [
            shape_of((tokens, width), f32),
            shape_of((tokens, width), bf16),
            shape_of((1, width), f32),
        ],
        [],
        (ids, d_hidden, d_hidden_send, d_hidden_rest, up_weight, stream, d_two, vectors),
    )
    d_attn_peer = swap(d_attn, "narrow", 1)
    normed_pair = normed_two, swap(normed_two, "narrow", 1)
    d_hidden_pair = d_hidden, swap(d_hidden_send, "narrow", 1)
    d_mlp_pair = d_mlp, swap(d_mlp, "narrow", 1)
    hidden_pair = hidden, swap(hidden_send, "narrow", 1)

    def pair_sum(steps, left, right):
        return blocks_of(
            call(
                functools.partial(pair_sum_kernel, size, steps),
                "svvvv",
                block_shapes(ff),
                [pltpu.VMEM((width, ff), f32)],
                (ids, *left, *right),
                4 * tokens * width * ff,
            ),
            steps,
        )

    up_blocks = pair_sum(near_steps, normed_pair, d_hidden_pair)
    down_blocks = pair_sum(far_steps, (after(d_mlp, *up_blocks), d_mlp_pair[1]), hidden_pair)
    up_in = swap(up_blocks[1], "dp", near_steps[0])
    down_in = swap(down_blocks[1], "dp", far_steps[0])
    d_qkv, d_normed, d_normed_send = call(
        back_attention_kernel,
        "s" + 5 * "v" + "h",
        [
            shape_of((length, 3 * half_width), bf16),
            shape_of((tokens, width), f32),
            shape_of((tokens, width), bf16),
        ],
        [
            pltpu.VMEM((length, half_width), bf16),
            pltpu.VMEM((3, width, half_width), bf16),
            sem((3,)),
        ],
        (
            ids,
            after(qkv, *up_blocks, *down_blocks),
            d_attn,
            d_attn_peer,
            proj_weight,
            allowed,
            qkv_weight,
        ),
        10 * length * length * half_width,
        28,
    )
    d_normed_peer = swap(d_normed_send, "narrow", 1)
    one_blocks = blocks_of(
        call(
            functools.partial(queries_sum_kernel, size, near_steps),
            "svv",
            block_shapes(2 * group),
            [pltpu.VMEM((width, 2 * group), f32)],
            (ids, normed_one, d_qkv),
        ),
        near_steps,
    )
    up_in, down_in, _ = lax.optimization_barrier((up_in, down_in, d_normed_send))
    if aligned and count > 2:
        shape = shape_of((up_in.shape[0] // 2, size, ff), bf16)
        outs = call(
            functools.partial(groups_kernel, (1, 1)),
            "v" * 4,
            [shape] * 4,
            [],
            (up_blocks[0], up_in, down_blocks[0], down_in),
            others=(one_blocks[0],),
        )
        up_blocks, down_blocks = outs[:2], outs[2:]
    else:
        up_blocks = stepped(up_blocks[0], up_in)
        down_blocks = stepped(down_blocks[0], down_in)
    up_in = swap(up_blocks[1], "dp", near_steps[1])
    down_in = swap(down_blocks[1], "dp", far_steps[1])
    [d_embed] = call(
        back_front_kernel,
        6 * "v",
        [shape_of((tokens + EXTRA, width), bf16)],
        [],
        (
            d_normed,
            after(d_normed_peer, *up_blocks, *down_blocks),
            embedded,
            d_one,
            vectors,
            gain_part_two,
        ),
        6 * tokens * width * width,
    )
    d_embed_peer = swap(d_embed, "narrow", 1)
    two_blocks = blocks_of(
        call(
            functools.partial(values_sum_kernel, size, far_steps),
            "s" + 6 * "v",
            block_shapes(2 * group),
            [pltpu.VMEM((length, half_width), bf16), pltpu.VMEM((width, 2 * group), f32)],
            (ids, normed_one, d_qkv, attended, attended_peer, d_attn, d_attn_peer),
            others=(d_embed,),
        ),
        far_steps,
    )
    one_in = swap(one_blocks[1], "dp", near_steps[0], 1)
    two_in = swap(two_blocks[1], "dp", far_steps[0], 1)
    up_in, down_in, _, _ = lax.optimization_barrier(
        (up_in, down_in, one_blocks[0], two_blocks[0])
    )
    mlp_blocks = join(stepped(up_blocks[0], up_in), stepped(down_blocks[0], down_in))
    mlp_in = swap(mlp_blocks[1], "dp", near_steps[2])
    def class_blocks():
        def natural(mine, peers):
            a, b, c, d = mine[:quarter], mine[quarter:], peers[:quarter], peers[quarter:]
            return jnp.where(
                core == 0, jnp.concatenate([a, c, b, d]), jnp.concatenate([c, a, d, b])
            )

        segment_hot = (
            segment_ids[0][:, None] == jnp.arange(images, dtype=jnp.int32)[None, :]
        ).astype(bf16)
        label_hot = (
            labels[0][:, None] == jnp.arange(class_table.shape[0], dtype=jnp.int32)
        ).astype(bf16)
        segment_part = token_sum(natural(d_embed[:tokens], d_embed_peer[:tokens]), segment_hot)
        class_part = dot(segment_part.astype(bf16), label_hot)
        class_cols = class_table.shape[0] // 4
        part = jnp.concatenate(
            [
                lax.dynamic_slice_in_dim(class_part, r * class_cols, class_cols, 1),
                jnp.sum(segment_part, axis=1, keepdims=True),
            ],
            axis=1,
        )
        blocks = relative_blocks(part.astype(bf16), me, near_steps)
        return blocks[: count // 2], blocks[count // 2 :]

    *table_outs, patches_grad = call(
        functools.partial(
            table_sum_kernel, size, near_steps, (position_cols, embed_cols, slot_cols)
        ),
        "s" + 10 * "v",
        [*block_shapes(LANES), shape_of((channels, quarter), f32)],
        [
            pltpu.VMEM((length + 8, LANES), f32),
            pltpu.VMEM((tokens + EXTRA, LANES), bf16),
            pltpu.VMEM((tokens + EXTRA, LANES), bf16),
            pltpu.VMEM((quarter + EXTRA, width), f32),
            pltpu.VMEM((width, LANES), f32),
        ],
        (
            ids,
            d_embed,
            after(d_embed_peer, *mlp_blocks),
            *parts,
            head_keep,
            swap(head_send, "narrow", 1),
            direct,
            embed_weight,
        ),
        2 * length * width * LANES,
    )
    table_blocks = blocks_of(table_outs, near_steps)
    if not compact:
        table_blocks = join(table_blocks, class_blocks())
    table_in = swap(table_blocks[1], "dp", near_steps[0], 2)
    one_in, two_in, table_in = lax.optimization_barrier((one_in, two_in, table_in))
    if aligned and count > 2:
        blocks = one_blocks[0].shape[0] // 2
        one_cols, two_cols = one_in.shape[2] + table_in.shape[2], two_in.shape[2]
        outs = call(
            functools.partial(groups_kernel, (2, 1)),
            "v" * 6,
            [shape_of((blocks, size, one_cols), bf16)] * 2
            + [shape_of((blocks, size, two_cols), bf16)] * 2,
            [],
            (one_blocks[0], one_in, table_blocks[0], table_in, two_blocks[0], two_in),
        )
        one_blocks, two_blocks = outs[:2], outs[2:]
    else:
        one_blocks = join(stepped(one_blocks[0], one_in), stepped(table_blocks[0], table_in))
        two_blocks = stepped(two_blocks[0], two_in)
    one_in = swap(one_blocks[1], "dp", near_steps[1], 1)
    two_in = swap(two_blocks[1], "dp", far_steps[1], 1)
    one_in, two_in = lax.optimization_barrier((one_in, two_in))
    last_blocks = join(stepped(one_blocks[0], one_in), stepped(two_blocks[0], two_in))
    last_in = swap(last_blocks[1], "dp", near_steps[2], 1)

    def finished(blocks, arrived, turn, *others):
        kept = blocks[0]
        for step in near_steps[3:]:
            kept, sent = stepped(kept, arrived)
            arrived = swap(sent, "dp", step, turn)
        [part] = call(
            last_step_kernel,
            "vv",
            [shape_of(kept.shape[1:], bf16)],
            [],
            (kept, arrived),
            others=others,
        )
        return part

    mlp_parts = four(finished(mlp_blocks, mlp_in, 0, one_blocks[0], two_blocks[0]), 0)
    up_grad, down_grad = call(
        mlp_out_kernel,
        "svvvv",
        [shape_of((size, hidden_width), f32), shape_of((size, hidden_width), f32)],
        [],
        (ids, *mlp_parts),
        0,
    )
    last_part = finished(last_blocks, last_in, 1)
    last_far = after(swap(last_part, "narrow", 2, 1), up_grad)
    last_parts = [last_part, swap(last_part, "narrow", 1), last_far, swap(last_far, "narrow", 1)]
    last_shapes = [shape_of((size, 3 * width), f32), shape_of((size, width), f32)]
    last_scratch = [pltpu.VMEM((4, *last_part.shape), f32)]
    if compact:
        (
            qkv_grad,
            proj_grad,
            embed_grad,
            position_grad,
            class_grad,
            head_grad,
            gain_one,
            gain_two,
            bias,
        ) = call(
            functools.partial(
                last_out_kernel, (position_cols, embed_cols, slot_cols, head_cols, 2 * group)
            ),
            "svvvv",
            [
                *last_shapes,
                shape_of((channels, size), f32),
                shape_of((size, position_table.shape[0]), f32),
                shape_of((size, class_table.shape[0]), f32),
                shape_of((size, 2 * channels), f32),
                shape_of((1, size), f32),
                shape_of((1, size), f32),
                shape_of((1, size), f32),
            ],
            last_scratch,
            (ids, *last_parts),
            0,
        )
        attngain_grad, mlpgain_grad, bias_grad = gain_one[0], gain_two[0], bias[0]
    else:
        qkv_grad, proj_grad = call(
            heads_out_kernel, "svvvv", last_shapes, last_scratch, (ids, *last_parts), 0
        )
        shares = jnp.stack(last_parts).astype(f32)[:, :, 2 * group : -2 * group]
        shares = [lax.dynamic_index_in_dim(shares, r ^ i, 0, keepdims=False) for i in range(4)]
        class_cols = class_table.shape[0] // 4

        def joined(start, cols):
            return jnp.concatenate([share[:, start : start + cols] for share in shares], axis=1)

        position_grad = joined(0, position_cols)
        embed_grad = joined(position_cols, embed_cols).T
        class_grad = joined(LANES, class_cols)
        head_grad = joined(LANES - head_cols, head_cols)
        attngain_grad = shares[0][:, gain_at]
        mlpgain_grad = shares[0][:, gain_at + 1]
        bias_grad = shares[0][:, LANES + class_cols]
    return (
        latent.T[None],
        logdet,
        patches_grad.T[None],
        embed_grad,
        bias_grad,
        position_grad.T,
        class_grad.T,
        attngain_grad,
        qkv_grad,
        proj_grad,
        mlpgain_grad,
        up_grad,
        down_grad.T,
        head_grad,
    )


def solution(mesh):
    return jax.shard_map(
        shards,
        mesh=mesh,
        in_specs=(
            P("dp", "narrow", None),
            P("dp", None),
            P("dp", None),
            P(),
            P(),
            P(),
            P(),
            P(),
            P(),
            P(),
            P(),
            P(),
            P(),
            P(),
            P("dp", "narrow", None),
            P("dp", "narrow"),
        ),
        out_specs=(
            P("dp", "narrow", None),
            P("dp", "narrow"),
            P("dp", "narrow", None),
            P(None, "dp"),
            P("dp"),
            P(None, "dp"),
            P(None, "dp"),
            P("dp"),
            P("dp", None),
            P("dp", None),
            P("dp"),
            P("dp", None),
            P(None, "dp"),
            P("dp", None),
        ),
        check_vma=False,
    )
```

```python
import functools
import math

import jax
import jax.numpy as jnp
from jax import lax
from jax.experimental import pallas as pl
from jax.experimental.pallas import tpu as pltpu
from jax.sharding import PartitionSpec as P

HD = 64
UNIT = 64
BIG = 256
TILE = 128
EXTRA = 16
FRONT_ROOM = 28
MIDDLE_ROOM = 36
LANES = 128
bf16, f32 = jnp.bfloat16, jnp.float32
epsilon = 1e-05
masked_score = -1e30


def dot(left, right):
    return jnp.dot(left, right, preferred_element_type=f32)


def token_sum(left, right):
    return lax.dot_general(left, right, (((0,), (0,)), ((), ())), preferred_element_type=f32)


def back_dot(grads, weight):
    return lax.dot_general(grads, weight, (((1,), (1,)), ((), ())), preferred_element_type=f32)


def swap(value, axis, step, turn=0):
    count = lax.axis_size(axis)
    turned = [(i + turn) % count for i in range(count)]
    return lax.ppermute(value, axis, [(i, i ^ step) for i in turned])


def normalised(values):
    center = jnp.mean(values, axis=-1, keepdims=True)
    offsets = values - center
    inverse = lax.rsqrt(jnp.mean(offsets * offsets, axis=-1, keepdims=True) + epsilon)
    return offsets * inverse, inverse


def norm_back(grads, gain, normed, inverse):
    e = grads * gain
    mean_e = jnp.mean(e, axis=-1, keepdims=True)
    mean_en = jnp.mean(e * normed, axis=-1, keepdims=True)
    return inverse * (e - mean_e - normed * mean_en)


def halving_steps(count, far_first=False):
    steps = [1 << i for i in range(count.bit_length() - 1)]
    if far_first and len(steps) > 1:
        steps[:2] = steps[1], steps[0]
    return steps


def block_order(steps):
    order = [0]
    for step in reversed(steps):
        order = order + [j ^ step for j in order]
    return order


def relative_blocks(grad, me, steps):
    order = block_order(steps)
    size = grad.shape[0] // len(order)
    return jnp.stack([lax.dynamic_slice_in_dim(grad, (me ^ j) * size, size, 0) for j in order])


UNITS_AT = 2


def unit_firsts(ids_ref, units):
    firsts = [jnp.int32(0)]
    for u in range(1, units):
        same = ids_ref[UNITS_AT + u] == ids_ref[UNITS_AT + u - 1]
        firsts.append(jnp.where(same, firsts[-1], u))
    return firsts


def allowed_bias(row_start, firsts):
    begin, end = window_of(row_start)
    shape = (TILE, end - begin)
    row = lax.broadcasted_iota(jnp.int32, shape, 0)
    key = lax.broadcasted_iota(jnp.int32, shape, 1) + begin
    unit = row_start // UNIT
    first = jnp.where(row < UNIT, firsts[unit] * UNIT, firsts[unit + 1] * UNIT)
    return jnp.where((key >= first) & (key <= row + row_start), 0.0, masked_score)


def stacked(block, masks):
    return jnp.concatenate([block * masks[0], block * masks[1]])


def head_masks():
    lane = lax.broadcasted_iota(jnp.int32, (1, 2 * HD), 1)
    low = (lane < HD).astype(f32)
    return low.astype(bf16), (1.0 - low).astype(bf16)


def window_of(start):
    return max(0, start - BIG), start + TILE


def pick(rows, lanes, to_lane):
    row = lax.broadcasted_iota(jnp.int32, (rows, lanes), 0)
    lane = lax.broadcasted_iota(jnp.int32, (rows, lanes), 1)
    return to_lane(row, lane).astype(f32).astype(bf16)


def base_kernel(
    ids_ref, vector_ref, class_ref, position_ref, base_ref, allowed_ref, image_rows
):
    length = base_ref.shape[0]
    units = length // UNIT
    firsts = unit_firsts(ids_ref, units)
    for start in range(0, length, TILE):
        begin, end = window_of(start)
        allowed_ref[start : start + TILE, : end - begin] = allowed_bias(start, firsts)
    shape = (image_rows.shape[0], class_ref.shape[0])
    row = lax.broadcasted_iota(jnp.int32, shape, 0)
    label = jnp.full(shape, -1, jnp.int32)
    for s in range(ids_ref.shape[0] - UNITS_AT - units):
        label = jnp.where(row == s, ids_ref[UNITS_AT + units + s], label)
    hot = (lax.broadcasted_iota(jnp.int32, shape, 1) == label).astype(f32).astype(bf16)
    image_rows[...] = dot(hot, class_ref[...]) + vector_ref[0:1, :].astype(f32)
    for u in range(units):
        block = u - firsts[u]
        table = position_ref[pl.ds(pl.multiple_of(block * UNIT, UNIT), UNIT), :]
        image = image_rows[pl.ds(ids_ref[UNITS_AT + u], 1), :]
        base_ref[u * UNIT : (u + 1) * UNIT, :] = table.astype(f32) + image


def embed_kernel(
    ids_ref,
    part_0_ref,
    part_1_ref,
    part_2_ref,
    part_3_ref,
    base_ref,
    vector_ref,
    embed_ref,
    embedded_ref,
    normed_ref,
    patch_rows,
):
    length, width = normed_ref.shape
    quarter = length // 4
    channels = embed_ref.shape[0]
    place = ids_ref[1]
    core = place & 1
    firsts = unit_firsts(ids_ref, length // UNIT)
    patch_rows[0:8, :] = jnp.zeros((8, width), f32)
    for j, part in enumerate((part_0_ref, part_1_ref, part_2_ref, part_3_ref)):
        at = pl.multiple_of((place ^ j) * quarter + 8, 8)
        patch_rows[pl.ds(at, quarter), :] = token_sum(part[:channels, :], embed_ref[...])
    gain = vector_ref[1:2, :].astype(f32)
    inner = lax.broadcasted_iota(jnp.int32, (UNIT, width), 0)
    for u in range(length // UNIT):
        rows = slice(u * UNIT, (u + 1) * UNIT)
        before = patch_rows[u * UNIT + 7 : u * UNIT + 7 + UNIT, :]
        before = jnp.where((inner == 0) & (firsts[u] == u), 0.0, before)
        values = before + base_ref[rows, :]
        q = u * UNIT // quarter
        inside = (q >> 1) * quarter + u * UNIT - q * quarter

        @pl.when(core == (q & 1))
        def _():
            embedded_ref[pl.ds(inside, UNIT), :] = values

        normed_ref[rows, :] = (normalised(values)[0] * gain).astype(bf16)


def attention_kernel(ids_ref, normed_ref, allowed, weight_ref, qkv_ref, attended_ref):
    length, width = normed_ref.shape
    half = width // 2
    core = ids_ref[1] & 1
    starts = range(0, length, TILE)
    for t in range(3):
        columns = pl.ds(pl.multiple_of(t * width + core * half, 128), half)
        qkv_ref[:, t * half : (t + 1) * half] = dot(
            normed_ref[...], weight_ref[:, columns]
        ).astype(bf16)
    masks = head_masks()
    low_lanes = lax.broadcasted_iota(jnp.int32, (TILE, 2 * HD), 1) < HD

    def pair_step(pair, carry):
        lanes = [pl.ds(pl.multiple_of(t * half + pair * 2 * HD, 128), 2 * HD) for t in range(3)]
        scores = []
        for start in starts:
            begin, end = window_of(start)
            q = stacked(qkv_ref[start : start + TILE, lanes[0]], masks)
            scores.append(back_dot(q, qkv_ref[begin:end, lanes[1]]))
        raised, totals = [], []
        for start, block in zip(starts, scores):
            begin, end = window_of(start)
            bias = allowed[start : start + TILE, : end - begin]
            masked = block * (1.0 / math.sqrt(HD)) + jnp.concatenate([bias, bias])
            power = jnp.exp(masked - jnp.max(masked, axis=-1, keepdims=True))
            raised.append(power.astype(bf16))
            totals.append(1.0 / jnp.sum(power, axis=-1, keepdims=True))
        for start, power, inverse in zip(starts, raised, totals):
            begin, end = window_of(start)
            out = dot(power, qkv_ref[begin:end, lanes[2]]) * inverse
            attended_ref[start : start + TILE, lanes[0]] = jnp.where(
                low_lanes, out[:TILE], out[TILE:]
            ).astype(bf16)
        return carry

    lax.fori_loop(0, half // (2 * HD), pair_step, 0, unroll=True)


def back_attention_kernel(
    ids_ref,
    qkv_ref,
    mine_ref,
    peer_ref,
    proj_ref,
    allowed,
    weight_ref,
    grads,
    own_ref,
    send_ref,
    mixed,
):
    length = qkv_ref.shape[0]
    half = qkv_ref.shape[1] // 3
    quarter = length // 4
    core = ids_ref[1] & 1
    width = weight_ref.shape[0]
    proj = proj_ref[pl.ds(pl.multiple_of(core * half, 128), half), :]
    for ref, side in ((mine_ref, core), (peer_ref, 1 - core)):
        product = back_dot(ref[...], proj).astype(bf16)
        for i in range(2):
            rows = pl.ds(pl.multiple_of((2 * i + side) * quarter, 16), quarter)
            mixed[rows, :] = product[i * quarter : (i + 1) * quarter]
    masks = head_masks()
    low_lanes = lax.broadcasted_iota(jnp.int32, (TILE, 2 * HD), 1) < HD
    scale = 1.0 / math.sqrt(HD)
    starts = range(0, length, TILE)

    def pair_step(pair, carry):
        lanes = [pl.ds(pl.multiple_of(t * half + pair * 2 * HD, 128), 2 * HD) for t in range(3)]
        queries, outer, scores, d_weights = [], [], [], []
        for start in starts:
            begin, end = window_of(start)
            queries.append(stacked(qkv_ref[start : start + TILE, lanes[0]], masks))
            outer.append(stacked(mixed[start : start + TILE, lanes[0]], masks))
            scores.append(back_dot(queries[-1], qkv_ref[begin:end, lanes[1]]))
            d_weights.append(back_dot(outer[-1], qkv_ref[begin:end, lanes[2]]))
        weights, d_scores = [], []
        for start, block, d_block in zip(starts, scores, d_weights):
            begin, end = window_of(start)
            bias = allowed[start : start + TILE, : end - begin]
            masked = block * scale + jnp.concatenate([bias, bias])
            power = jnp.exp(masked - jnp.max(masked, axis=-1, keepdims=True))
            weight = power * (1.0 / jnp.sum(power, axis=-1, keepdims=True))
            centre = jnp.sum(weight * d_block, axis=-1, keepdims=True)
            weights.append(weight.astype(bf16))
            d_scores.append((weight * (d_block - centre)).astype(bf16))
        for i, start in enumerate(starts):
            begin, end = window_of(start)
            out = dot(d_scores[i], qkv_ref[begin:end, lanes[1]])
            grads[start : start + TILE, lanes[0]] = (
                jnp.where(low_lanes, out[:TILE], out[TILE:]) * scale
            ).astype(bf16)
        d_keys = [token_sum(d, q) for d, q in zip(d_scores, queries)]
        d_values = [token_sum(w, o) for w, o in zip(weights, outer)]
        for at in starts:
            for t, sums, factor in ((1, d_keys, scale), (2, d_values, 1.0)):
                total = None
                for start, block in zip(starts, sums):
                    begin, end = window_of(start)
                    if begin <= at < end:
                        term = block[at - begin : at - begin + TILE]
                        total = term if total is None else total + term
                grads[at : at + TILE, lanes[t]] = (total * factor).astype(bf16)
        return carry

    lax.fori_loop(0, half // (2 * HD), pair_step, 0, unroll=True)
    for ref, side in ((send_ref, 1 - core), (own_ref, core)):
        for i in range(2):
            rows = pl.ds(pl.multiple_of((2 * i + side) * quarter, 16), quarter)
            total = None
            for t in range(3):
                term = back_dot(
                    grads[rows, t * half : (t + 1) * half],
                    weight_ref[:, pl.ds(pl.multiple_of(t * width + core * half, 128), half)],
                )
                total = term if total is None else total + term
            ref[i * quarter : (i + 1) * quarter, :] = total.astype(ref.dtype)


def middle_kernel(
    ids_ref,
    embedded_ref,
    own_ref,
    peer_ref,
    gain_ref,
    head_weight_ref,
    near_ref,
    far_ref,
    proj,
    up_hbm,
    down_hbm,
    latent_ref,
    logdet_ref,
    direct_ref,
    normed_ref,
    hidden_ref,
    hidden_send_ref,
    d_mlp_ref,
    d_hidden_ref,
    d_hidden_send_ref,
    d_hidden_rest,
    stream,
    d_two_ref,
    head_ref,
    head_send_ref,
    up,
    down,
    hidden_rest,
    slope,
    low,
    sems,
):
    tokens, width = embedded_ref.shape
    quarter = tokens // 2
    half = width // 2
    ff = up.shape[2]
    place = ids_ref[1]
    core, far = place & 1, place >> 1
    channels = latent_ref.shape[0]
    hiddens = hidden_ref, hidden_send_ref, hidden_rest.at[0], hidden_rest.at[1]
    d_hiddens = d_hidden_ref, d_hidden_send_ref, d_hidden_rest.at[0], d_hidden_rest.at[1]
    copies = [None]
    for j in range(4):
        columns = pl.ds(pl.multiple_of((place ^ j) * ff, 128), ff)
        copies.append(pltpu.make_async_copy(up_hbm.at[:, columns], up.at[j], sems.at[1 + j]))
        copies[-1].start()
    for j in range(4):
        rows = pl.ds(pl.multiple_of((place ^ j) * ff, 128), ff)
        copies.append(pltpu.make_async_copy(down_hbm.at[rows, :], down.at[j], sems.at[5 + j]))
        copies[-1].start()
    gain = gain_ref[2:3, :].astype(f32)
    for i in range(2):
        source = pl.ds(pl.multiple_of((2 * i + core) * quarter, 16), quarter)
        rows = slice(i * quarter, (i + 1) * quarter)
        values = embedded_ref[rows, :]
        for ref, side in ((own_ref, core), (peer_ref, 1 - core)):
            weight = proj[pl.ds(pl.multiple_of(side * half, 128), half), :]
            values += dot(ref[source, :], weight)
        stream[rows, :] = values
        normed_ref[rows, :] = (normalised(values)[0] * gain).astype(bf16)
    for j in range(4):
        copies[1 + j].wait()

        pre = dot(normed_ref[...], up[j])
        cdf = 0.5 * (1.0 + lax.erf(pre * math.sqrt(0.5)))
        density = jnp.exp(-0.5 * pre * pre) * (1.0 / math.sqrt(2 * math.pi))
        slope[j] = cdf + pre * density
        value = (pre * cdf).astype(bf16)
        hiddens[j][...] = value
    total = stream[...]
    for j in range(4):
        copies[5 + j].wait()
        total += dot(hiddens[j][...], down[j])
    low[...] = total.astype(bf16)
    head_sums = [jnp.zeros(head_ref.shape, f32)] * 2
    head_cols = channels // 2
    lane_at = LANES - head_cols
    for i in range(2):
        rows = slice(i * quarter, (i + 1) * quarter)
        part = jnp.where(far == i, near_ref[...].astype(f32), far_ref[...].astype(f32))
        patches, cot = part[:channels], part[channels : 2 * channels]
        logdet_cot = jnp.sum(part[2 * channels :], axis=0, keepdims=True)
        head_out = back_dot(head_weight_ref[...], low[rows, :])
        mean_shift, logscale = head_out[:channels], head_out[channels:]
        factor = jnp.exp(-logscale)
        latent = (patches - mean_shift) * factor
        direct = cot * factor

        @pl.when(far == i)
        def _():
            latent_ref[...] = latent
            logdet_ref[...] = -jnp.sum(logscale, axis=0, keepdims=True)
            direct_ref[...] = direct

        d_head = jnp.concatenate([-direct, -cot * latent - logdet_cot]).astype(bf16)
        d_two = token_sum(d_head, head_weight_ref[...])
        d_two_ref[rows, :] = d_two
        d_mlp_ref[rows, :] = d_two.astype(bf16)
        for k, index in enumerate((place, place ^ 1)):
            chosen = pick(
                2 * channels,
                LANES,
                lambda row, lane: (lane - lane_at + index * head_cols == row) & (lane >= lane_at),
            )
            columns = token_sum(d_head, chosen).astype(bf16)
            head_sums[k] += token_sum(low[rows, :], columns)
    head_ref[...] = head_sums[0]
    head_send_ref[...] = head_sums[1].astype(bf16)
    for j in range(4):
        value = (back_dot(d_mlp_ref[...], down[j]) * slope[j]).astype(bf16)
        d_hiddens[j][...] = value


def turn_kernel(
    ids_ref,
    d_hidden_ref,
    d_hidden_send_ref,
    d_hidden_rest,
    up_ref,
    stream,
    d_two_ref,
    gain_ref,
    d_one_ref,
    d_attn_ref,
    gain_part_ref,
):
    tokens, width = stream.shape
    quarter = tokens // 2
    ff = d_hidden_ref.shape[1]
    place = ids_ref[1]
    gain = gain_ref[2:3, :].astype(f32)
    d_hiddens = d_hidden_ref, d_hidden_send_ref, d_hidden_rest.at[0], d_hidden_rest.at[1]
    grads = jnp.zeros((tokens, width), f32)
    for j, d_hidden in enumerate(d_hiddens):
        columns = pl.ds(pl.multiple_of((place ^ j) * ff, 128), ff)
        grads += back_dot(d_hidden[...], up_ref[:, columns])
    for i in range(2):
        rows = slice(i * quarter, (i + 1) * quarter)
        share = grads[rows]
        n, inverse = normalised(stream[rows, :])
        part = jnp.sum(share * n, axis=0, keepdims=True)
        gain_part_ref[...] = part if i == 0 else gain_part_ref[...] + part
        d_one = d_two_ref[rows, :] + norm_back(share, gain, n, inverse)
        d_one_ref[rows, :] = d_one
        d_attn_ref[rows, :] = d_one.astype(bf16)


def back_front_kernel(
    own_ref,
    peer_ref,
    embedded_ref,
    d_one_ref,
    gain_ref,
    part_ref,
    d_embed_ref,
):
    tokens, width = embedded_ref.shape
    gain = gain_ref[1:2, :].astype(f32)
    step = tokens // 6
    total = jnp.zeros((1, width), f32)
    for i in range(6):
        rows = slice(i * step, (i + 1) * step)
        grads = own_ref[rows, :] + peer_ref[rows, :].astype(f32)
        n, inverse = normalised(embedded_ref[rows, :])
        total += jnp.sum(grads * n, axis=0, keepdims=True)
        d_embed_ref[rows, :] = (d_one_ref[rows, :] + norm_back(grads, gain, n, inverse)).astype(
            bf16
        )
    row = lax.broadcasted_iota(jnp.int32, (EXTRA, width), 0)
    both = jnp.where(row % 2 == 0, total, part_ref[...])
    coarse = both.astype(bf16).astype(f32)
    rest = jnp.where(row < 2, coarse, jnp.where(row < 4, both - coarse, 0.0))
    d_embed_ref[tokens : tokens + EXTRA, :] = rest.astype(bf16)


def place_blocks(total, outs, me, size, steps, start=0):
    columns = slice(start, start + outs[0].shape[-1])
    if len(outs) == 1:
        outs[0][...] = total[:, columns].astype(bf16)
        return
    keep, send = outs
    for k, j in enumerate(block_order(steps)):
        block = total[pl.ds(pl.multiple_of((me ^ j) * size, 16), size), columns].astype(bf16)
        if k < keep.shape[0]:
            keep[k] = block
        else:
            send[k - keep.shape[0]] = block


def pair_sum_kernel(size, steps, ids_ref, left_ref, left_peer_ref, right_ref, right_peer_ref, *rest):
    *outs, total = rest
    columns = total.shape[1]
    total[...] = token_sum(left_ref[...], right_ref[:, :columns]) + token_sum(
        left_peer_ref[...], right_peer_ref[:, :columns]
    )
    place_blocks(total, outs, ids_ref[0], size, steps)


def heads_part(total, at, t, normed_ref, d_qkv_ref, far):
    half = d_qkv_ref.shape[1] // 3
    group = half // 2
    low = d_qkv_ref[:, t * half : t * half + group]
    high = d_qkv_ref[:, t * half + group : (t + 1) * half]
    picked = jnp.where(far == 0, low.astype(f32), high.astype(f32)).astype(bf16)
    total[:, at : at + group] = token_sum(normed_ref[...], picked)


def queries_sum_kernel(size, steps, ids_ref, normed_ref, d_qkv_ref, *rest):
    *outs, total = rest
    for t in range(2):
        heads_part(total, t * total.shape[1] // 2, t, normed_ref, d_qkv_ref, ids_ref[1] >> 1)
    place_blocks(total, outs, ids_ref[0], size, steps)


def values_sum_kernel(
    size,
    steps,
    ids_ref,
    normed_ref,
    d_qkv_ref,
    attended_ref,
    attended_peer_ref,
    d_attn_ref,
    d_attn_peer_ref,
    *rest,
):
    *outs, natural, total = rest
    place = ids_ref[1]
    core, far = place & 1, place >> 1
    length, width = normed_ref.shape
    quarter, half = length // 4, width // 2
    group = half // 2
    heads_part(total, 0, 2, normed_ref, d_qkv_ref, far)
    columns = pl.ds(pl.multiple_of(far * half, 128), half)
    for ref, side in ((d_attn_ref, core), (d_attn_peer_ref, 1 - core)):
        for i in range(2):
            rows = pl.ds(pl.multiple_of((2 * i + side) * quarter, 16), quarter)
            natural[rows, :] = ref[i * quarter : (i + 1) * quarter, columns]
    for ref, side in ((attended_ref, core), (attended_peer_ref, 1 - core)):
        sums = token_sum(ref[...], natural[...])
        rows = pl.ds(pl.multiple_of(side * half, 16), half)
        total[rows, group:] = jnp.where(core == 0, sums[:, :group], sums[:, group:])
    place_blocks(total, outs, ids_ref[0], size, steps)


def table_sum_kernel(
    size,
    steps,
    plan,
    ids_ref,
    d_ref,
    d_peer_ref,
    part_0_ref,
    part_1_ref,
    part_2_ref,
    part_3_ref,
    head_ref,
    head_peer_ref,
    direct_ref,
    embed_ref,
    *rest,
):
    *outs, patches_ref, before_rows, to_own, to_peer, following, total = rest
    position_cols, embed_cols, slot_cols = plan
    slot_at = position_cols + embed_cols
    label_at = slot_at + slot_cols
    gain_at = label_at + 2
    me, place = ids_ref[0], ids_ref[1]
    core, far = place & 1, place >> 1
    channels, quarter = direct_ref.shape
    tokens = 2 * quarter
    length = 2 * tokens
    units = length // UNIT
    labels_at = UNITS_AT + units
    images = ids_ref.shape[0] - labels_at
    parts = (part_0_ref, part_1_ref, part_2_ref, part_3_ref)
    chosen = pick(
        part_0_ref.shape[0],
        LANES,
        lambda row, lane: (row == lane - position_cols + place * embed_cols)
        & (lane >= position_cols)
        & (lane < slot_at),
    )
    before_rows[0:8, :] = jnp.zeros((8, LANES), f32)
    for j, part in enumerate(parts):
        at = pl.multiple_of((place ^ j) * quarter + 8, 8)
        before_rows[pl.ds(at, quarter), :] = token_sum(part[...], chosen)
    firsts = unit_firsts(ids_ref, units)
    row = lax.broadcasted_iota(jnp.int32, (UNIT, LANES), 0)
    lane = lax.broadcasted_iota(jnp.int32, (UNIT, LANES), 1)
    for u in range(length // UNIT):
        block = u - firsts[u]
        before = before_rows[u * UNIT + 7 : u * UNIT + 7 + UNIT, :]
        before = jnp.where((row == 0) & (block == 0), 0.0, before)
        position = lane + place * position_cols == row + block * UNIT
        slot = lane - slot_at + place * slot_cols == me * images + ids_ref[UNITS_AT + u]
        ones = ((lane < position_cols) & position) | (
            (lane >= slot_at) & (lane < label_at) & slot
        )
        value = jnp.where(ones, 1.0, before).astype(bf16)
        q = u * UNIT // quarter
        inside = (q >> 1) * quarter + u * UNIT - q * quarter

        @pl.when(core == (q & 1))
        def _():
            to_own[inside : inside + UNIT, :] = value

        @pl.when(core != (q & 1))
        def _():
            to_peer[inside : inside + UNIT, :] = value

    gain_rows = pick(EXTRA, LANES, lambda row, lane: (lane == gain_at + row % 2) & (row < 4))
    to_own[tokens:, :] = gain_rows
    to_peer[tokens:, :] = gain_rows
    total[...] = (
        token_sum(d_ref[...], to_own[...])
        + token_sum(d_peer_ref[...], to_peer[...])
        + head_ref[...]
        + head_peer_ref[...].astype(f32)
    )
    if slot_cols:
        row = lax.broadcasted_iota(jnp.int32, (size, LANES), 0)
        lane = lax.broadcasted_iota(jnp.int32, (size, LANES), 1)
        label = jnp.zeros((size, LANES), jnp.int32)
        for s in range(images):
            label = jnp.where(row == me * images + s, ids_ref[labels_at + s], label)
        code = jnp.where(
            lane == label_at, label >> 3, jnp.where(lane == label_at + 1, label & 7, 0)
        ).astype(f32)
        for b in range(total.shape[0] // size):
            total[b * size : (b + 1) * size, :] += code
    place_blocks(total, outs, me, size, steps)
    following[:quarter, :] = d_ref[pl.ds(pl.multiple_of(far * quarter, 16), quarter), :].astype(f32)
    at = pl.multiple_of(((place + 1) >> 1) * quarter, 16)
    following[quarter:, :] = d_peer_ref[pl.ds(at, EXTRA), :].astype(f32)
    row = lax.broadcasted_iota(jnp.int32, (quarter, following.shape[1]), 0)
    dropped = (row == quarter - 1) & (place == 3)
    for w in range(1, quarter // UNIT + 1):
        u = jnp.minimum(place * (quarter // UNIT) + w, units - 1)
        opens = ids_ref[UNITS_AT + u] != ids_ref[UNITS_AT + u - 1]
        dropped = dropped | ((row == w * UNIT - 1) & opens)
    shifted = jnp.where(dropped, 0.0, following[1 : quarter + 1, :]).astype(bf16)
    patches_ref[...] = direct_ref[...] + back_dot(embed_ref[...], shifted)


def mlp_out_kernel(ids_ref, *refs):
    *parts, up_ref, down_ref = refs
    ff = up_ref.shape[1] // 4
    for j, part in enumerate(parts):
        columns = pl.ds(pl.multiple_of((ids_ref[1] ^ j) * ff, 128), ff)
        up_ref[:, columns] = part[:, :ff].astype(f32)
        down_ref[:, columns] = part[:, ff:].astype(f32)


def heads_out(stack, qkv_ref, proj_ref):
    width = proj_ref.shape[1]
    group = width // 4
    starts = (0, group, -2 * group, -group)
    for i, q in enumerate((0, 2, 1, 3)):
        for t, start in enumerate(starts[:3]):
            put = t * width + i * group
            qkv_ref[:, put : put + group] = stack[q, :, start % stack.shape[2] : start % stack.shape[2] + group]
        proj_ref[:, i * group : (i + 1) * group] = stack[i, :, stack.shape[2] - group :]


def heads_out_kernel(ids_ref, *refs):
    *parts, qkv_ref, proj_ref, stack = refs
    for j, part in enumerate(parts):
        stack[ids_ref[1] ^ j] = part[...].astype(f32)
    heads_out(stack, qkv_ref, proj_ref)


def last_out_kernel(plan, ids_ref, *refs):
    *parts, qkv_ref, proj_ref, embed_ref, position_ref, class_ref, head_ref, gain_one_ref, gain_two_ref, bias_ref, stack = refs
    position_cols, embed_cols, slot_cols, head_cols, at = plan
    slot_at = position_cols + embed_cols
    label_at = slot_at + slot_cols
    gain_at = label_at + 2
    head_at = LANES - head_cols
    for j, part in enumerate(parts):
        stack[ids_ref[1] ^ j] = part[...].astype(f32)
    heads_out(stack, qkv_ref, proj_ref)
    embed = position = head = slots = bias = None

    def added(total, term):
        return term if total is None else total + term

    for q in range(4):
        part = stack[q, :, at : at + LANES].astype(bf16)

        def placed(start, cols):
            return pick(
                LANES,
                4 * cols,
                lambda row, lane: (lane == row - start + q * cols)
                & (row >= start)
                & (row < start + cols),
            )

        position = added(position, dot(part, placed(0, position_cols)))
        head = added(head, dot(part, placed(head_at, head_cols)))
        slots = added(slots, dot(part, placed(slot_at, slot_cols)))
        chosen = pick(
            embed_ref.shape[0],
            LANES,
            lambda row, lane: (row == lane - position_cols + q * embed_cols)
            & (lane >= position_cols)
            & (lane < slot_at),
        )
        embed = added(embed, back_dot(chosen, part))
        chosen = pick(
            8, LANES, lambda row, lane: (row == 0) & (lane >= slot_at) & (lane < label_at)
        )
        bias = added(bias, back_dot(chosen, part))
    embed_ref[...] = embed
    position_ref[...] = position
    head_ref[...] = head
    bias_ref[...] = bias[0:1, :]
    first = stack[0, :, at : at + LANES].astype(bf16)
    gains = back_dot(pick(8, LANES, lambda row, lane: (lane == row + gain_at) & (row < 2)), first)
    gain_one_ref[...] = gains[0:1, :]
    gain_two_ref[...] = gains[1:2, :]
    codes = stack[0, :, at : at + LANES]
    coded = codes[:, label_at : label_at + 1] * 8.0 + codes[:, label_at + 1 : label_at + 2]
    shape = (4 * slot_cols, class_ref.shape[1])
    label = jnp.broadcast_to(coded[: 4 * slot_cols].astype(jnp.int32), shape)
    hot = (lax.broadcasted_iota(jnp.int32, shape, 1) == label).astype(f32).astype(bf16)
    class_ref[...] = dot(slots.astype(bf16), hot)


def after(value, *others):
    return lax.optimization_barrier((value, *others))[0]


def shape_of(dims, dtype):
    return jax.ShapeDtypeStruct(dims, dtype)


def call(kernel, places, outs, scratch, operands, flops=0, room=16, others=()):
    spaces = {
        "s": pl.BlockSpec(memory_space=pltpu.SMEM),
        "v": pl.BlockSpec(memory_space=pltpu.VMEM),
        "h": pl.BlockSpec(memory_space=pltpu.HBM),
    }
    taken = len(operands)

    def body(*refs):
        kernel(*refs[:taken], *refs[taken + len(others) :])

    return pl.pallas_call(
        body,
        name=getattr(kernel, "func", kernel).__name__,
        out_shape=outs,
        in_specs=[spaces[p] for p in places] + [pl.BlockSpec(memory_space=pl.ANY)] * len(others),
        out_specs=[spaces["v"]] * len(outs),
        scratch_shapes=scratch,
        compiler_params=pltpu.CompilerParams(vmem_limit_bytes=room * 2**20),
    )(*operands, *others)


def groups_kernel(groups, *refs):
    count = 2 * sum(groups)
    pairs, outs = iter(refs[:count]), iter(refs[count:])
    for group in groups:
        sums, start = None, 0
        for _ in range(group):
            kept, arrived = next(pairs), next(pairs)
            columns = slice(start, start + kept.shape[2])
            start = columns.stop
            if sums is None:
                sums = [next(outs)] if kept.shape[0] == 1 else [next(outs), next(outs)]
            half = (kept.shape[0] + 1) // 2
            for k, out in enumerate(sums):
                rows = slice(k * half, (k + 1) * half)
                out[:, :, columns] = (kept[rows].astype(f32) + arrived[rows].astype(f32)).astype(bf16)


def last_step_kernel(kept_ref, arrived_ref, out_ref):
    out_ref[...] = (kept_ref[0].astype(f32) + arrived_ref[0].astype(f32)).astype(bf16)


def shards(
    patches,
    segment_ids,
    labels,
    embed_weight,
    embed_bias,
    position_table,
    class_table,
    attn_gain,
    qkv_weight,
    proj_weight,
    mlp_gain,
    up_weight,
    down_weight,
    head_weight,
    latent_grad,
    logdet_grad,
):
    _, quarter, channels = patches.shape
    length = segment_ids.shape[1]
    width = qkv_weight.shape[0]
    hidden_width = up_weight.shape[1]
    tokens = 2 * quarter
    ff = hidden_width // 4
    half_width = width // 2
    group = half_width // 2
    count = lax.axis_size("dp")
    me = lax.axis_index("dp")
    r = lax.axis_index("narrow")
    core = r & 1
    ids = jnp.concatenate(
        [jnp.stack([me, r]).astype(jnp.int32), segment_ids[0, ::UNIT], labels[0]]
    )
    line = jnp.arange(8, dtype=jnp.int32)[:, None]
    vectors = jnp.where(
        line == 0, embed_bias[None], jnp.where(line == 1, attn_gain[None], mlp_gain[None])
    )
    near_steps, far_steps = halving_steps(count), halving_steps(count, True)
    size = width // count
    sem = pltpu.SemaphoreType.DMA

    images = labels.shape[1]
    slots = images * count
    position_cols, embed_cols = position_table.shape[0] // 4, channels // 4
    head_cols = channels // 2
    slot_cols = slots // 4
    compact = position_cols + embed_cols + slot_cols + 4 + head_cols <= LANES and slots <= size
    slot_cols = slot_cols if compact else 0
    gain_at = position_cols + embed_cols + slot_cols + 2

    coarse = lax.reduce_precision(logdet_grad, 8, 7)
    own_part = jnp.concatenate(
        [
            patches[0].T,
            latent_grad[0].T,
            coarse.astype(bf16),
            (logdet_grad - coarse).astype(bf16),
        ]
    )
    far_part = swap(own_part, "narrow", 2)
    parts = [
        own_part,
        swap(own_part, "narrow", 1),
        far_part,
        swap(far_part, "narrow", 1),
    ]
    base, allowed = call(
        base_kernel,
        "svvv",
        [shape_of((length, width), f32), shape_of((length, BIG + TILE), f32)],
        [
            pltpu.VMEM((16, width), f32),
        ],
        (ids, vectors, class_table, position_table),
        2 * 16 * width * class_table.shape[0],
    )
    embedded, normed_one = call(
        embed_kernel,
        "s" + 7 * "v",
        [shape_of((tokens, width), f32), shape_of((length, width), bf16)],
        [pltpu.VMEM((length + 8, width), f32)],
        (ids, *parts, base, vectors, embed_weight),
    )
    qkv, attended = call(
        attention_kernel,
        "svvv",
        [shape_of((length, 3 * half_width), bf16), shape_of((length, half_width), bf16)],
        [],
        (ids, normed_one, allowed, qkv_weight),
        0,
        FRONT_ROOM,
    )
    attended_peer = swap(attended, "narrow", 1)
    (
        latent,
        logdet,
        direct,
        normed_two,
        hidden,
        hidden_send,
        d_mlp,
        d_hidden,
        d_hidden_send,
        d_hidden_rest,
        stream,
        d_two,
        head_keep,
        head_send,
    ) = call(
        middle_kernel,
        "s" + 8 * "v" + "hh",
        [
            shape_of((channels, quarter), f32),
            shape_of((1, quarter), f32),
            shape_of((channels, quarter), f32),
            shape_of((tokens, width), bf16),
            shape_of((tokens, ff), bf16),
            shape_of((tokens, ff), bf16),
            shape_of((tokens, width), bf16),
            shape_of((tokens, ff), bf16),
            shape_of((tokens, ff), bf16),
            shape_of((2, tokens, ff), bf16),
            shape_of((tokens, width), f32),
            shape_of((tokens, width), f32),
            shape_of((width, LANES), f32),
            shape_of((width, LANES), bf16),
        ],
        [
            pltpu.VMEM((4, width, ff), bf16),
            pltpu.VMEM((4, ff, width), bf16),
            pltpu.VMEM((2, tokens, ff), bf16),
            pltpu.VMEM((4, tokens, ff), f32),
            pltpu.VMEM((tokens, width), bf16),
            sem((9,)),
        ],
        (
            ids,
            embedded,
            attended,
            attended_peer,
            vectors,
            head_weight.T,
            own_part,
            far_part,
            proj_weight,
            up_weight,
            down_weight,
        ),
        8 * tokens * width * hidden_width,
        MIDDLE_ROOM,
    )

    aligned = size % 16 == 0 and count > 1

    def block_shapes(cols):
        if aligned:
            return [shape_of((count // 2, size, cols), bf16)] * 2
        return [shape_of((width, cols), bf16)]

    def blocks_of(outs, steps):
        if aligned:
            return outs
        blocks = relative_blocks(outs[0], me, steps)
        return blocks[: max(1, count // 2)], blocks[max(1, count // 2) :]

    def stepped(kept, arrived):
        total = kept.astype(f32) + arrived.astype(f32)
        half = (total.shape[0] + 1) // 2
        return total[:half].astype(bf16), total[half:].astype(bf16)

    def join(*blocks):
        return [jnp.concatenate(pair, axis=2) for pair in zip(*blocks)]

    def four(part, turn):
        far_one = swap(part, "narrow", 2, turn)
        return [part, swap(part, "narrow", 1), far_one, swap(far_one, "narrow", 1)]

    d_one, d_attn, gain_part_two = call(
        turn_kernel,
        "s" + 7 * "v",
        [
            shape_of((tokens, width), f32),
            shape_of((tokens, width), bf16),
            shape_of((1, width), f32),
        ],
        [],
        (ids, d_hidden, d_hidden_send, d_hidden_rest, up_weight, stream, d_two, vectors),
    )
    d_attn_peer = swap(d_attn, "narrow", 1)
    normed_pair = normed_two, swap(normed_two, "narrow", 1)
    d_hidden_pair = d_hidden, swap(d_hidden_send, "narrow", 1)
    d_mlp_pair = d_mlp, swap(d_mlp, "narrow", 1)
    hidden_pair = hidden, swap(hidden_send, "narrow", 1)

    def pair_sum(steps, left, right):
        return blocks_of(
            call(
                functools.partial(pair_sum_kernel, size, steps),
                "svvvv",
                block_shapes(ff),
                [pltpu.VMEM((width, ff), f32)],
                (ids, *left, *right),
                4 * tokens * width * ff,
            ),
            steps,
        )

    up_blocks = pair_sum(near_steps, normed_pair, d_hidden_pair)
    down_blocks = pair_sum(far_steps, (after(d_mlp, *up_blocks), d_mlp_pair[1]), hidden_pair)
    up_in = swap(up_blocks[1], "dp", near_steps[0])
    down_in = swap(down_blocks[1], "dp", far_steps[0])
    d_qkv, d_normed, d_normed_send = call(
        back_attention_kernel,
        "s" + 6 * "v",
        [
            shape_of((length, 3 * half_width), bf16),
            shape_of((tokens, width), f32),
            shape_of((tokens, width), bf16),
        ],
        [
            pltpu.VMEM((length, half_width), bf16),
        ],
        (
            ids,
            after(qkv, *up_blocks, *down_blocks),
            d_attn,
            d_attn_peer,
            proj_weight,
            allowed,
            qkv_weight,
        ),
        10 * length * length * half_width,
        28,
    )
    d_normed_peer = swap(d_normed_send, "narrow", 1)
    one_blocks = blocks_of(
        call(
            functools.partial(queries_sum_kernel, size, near_steps),
            "svv",
            block_shapes(2 * group),
            [pltpu.VMEM((width, 2 * group), f32)],
            (ids, normed_one, d_qkv),
        ),
        near_steps,
    )
    up_in, down_in, _ = lax.optimization_barrier((up_in, down_in, d_normed_send))
    if aligned and count > 2:
        shape = shape_of((up_in.shape[0] // 2, size, ff), bf16)
        outs = call(
            functools.partial(groups_kernel, (1, 1)),
            "v" * 4,
            [shape] * 4,
            [],
            (up_blocks[0], up_in, down_blocks[0], down_in),
            others=(one_blocks[0],),
        )
        up_blocks, down_blocks = outs[:2], outs[2:]
    else:
        up_blocks = stepped(up_blocks[0], up_in)
        down_blocks = stepped(down_blocks[0], down_in)
    up_in = swap(up_blocks[1], "dp", near_steps[1])
    down_in = swap(down_blocks[1], "dp", far_steps[1])
    [d_embed] = call(
        back_front_kernel,
        6 * "v",
        [shape_of((tokens + EXTRA, width), bf16)],
        [],
        (
            d_normed,
            after(d_normed_peer, *up_blocks, *down_blocks),
            embedded,
            d_one,
            vectors,
            gain_part_two,
        ),
        6 * tokens * width * width,
    )
    d_embed_peer = swap(d_embed, "narrow", 1)
    two_blocks = blocks_of(
        call(
            functools.partial(values_sum_kernel, size, far_steps),
            "s" + 6 * "v",
            block_shapes(2 * group),
            [pltpu.VMEM((length, half_width), bf16), pltpu.VMEM((width, 2 * group), f32)],
            (ids, normed_one, d_qkv, attended, attended_peer, d_attn, d_attn_peer),
            others=(d_embed,),
        ),
        far_steps,
    )
    one_in = swap(one_blocks[1], "dp", near_steps[0], 1)
    two_in = swap(two_blocks[1], "dp", far_steps[0], 1)
    up_in, down_in, _, _ = lax.optimization_barrier(
        (up_in, down_in, one_blocks[0], two_blocks[0])
    )
    mlp_blocks = join(stepped(up_blocks[0], up_in), stepped(down_blocks[0], down_in))
    mlp_in = swap(mlp_blocks[1], "dp", near_steps[2])
    def class_blocks():
        def natural(mine, peers):
            a, b, c, d = mine[:quarter], mine[quarter:], peers[:quarter], peers[quarter:]
            return jnp.where(
                core == 0, jnp.concatenate([a, c, b, d]), jnp.concatenate([c, a, d, b])
            )

        segment_hot = (
            segment_ids[0][:, None] == jnp.arange(images, dtype=jnp.int32)[None, :]
        ).astype(bf16)
        label_hot = (
            labels[0][:, None] == jnp.arange(class_table.shape[0], dtype=jnp.int32)
        ).astype(bf16)
        segment_part = token_sum(natural(d_embed[:tokens], d_embed_peer[:tokens]), segment_hot)
        class_part = dot(segment_part.astype(bf16), label_hot)
        class_cols = class_table.shape[0] // 4
        part = jnp.concatenate(
            [
                lax.dynamic_slice_in_dim(class_part, r * class_cols, class_cols, 1),
                jnp.sum(segment_part, axis=1, keepdims=True),
            ],
            axis=1,
        )
        blocks = relative_blocks(part.astype(bf16), me, near_steps)
        return blocks[: count // 2], blocks[count // 2 :]

    *table_outs, patches_grad = call(
        functools.partial(
            table_sum_kernel, size, near_steps, (position_cols, embed_cols, slot_cols)
        ),
        "s" + 10 * "v",
        [*block_shapes(LANES), shape_of((channels, quarter), f32)],
        [
            pltpu.VMEM((length + 8, LANES), f32),
            pltpu.VMEM((tokens + EXTRA, LANES), bf16),
            pltpu.VMEM((tokens + EXTRA, LANES), bf16),
            pltpu.VMEM((quarter + EXTRA, width), f32),
            pltpu.VMEM((width, LANES), f32),
        ],
        (
            ids,
            d_embed,
            after(d_embed_peer, *mlp_blocks),
            *parts,
            head_keep,
            swap(head_send, "narrow", 1),
            direct,
            embed_weight,
        ),
        2 * length * width * LANES,
    )
    table_blocks = blocks_of(table_outs, near_steps)
    if not compact:
        table_blocks = join(table_blocks, class_blocks())
    table_in = swap(table_blocks[1], "dp", near_steps[0], 2)
    one_in, two_in, table_in = lax.optimization_barrier((one_in, two_in, table_in))
    if aligned and count > 2:
        blocks = one_blocks[0].shape[0] // 2
        one_cols, two_cols = one_in.shape[2] + table_in.shape[2], two_in.shape[2]
        outs = call(
            functools.partial(groups_kernel, (2, 1)),
            "v" * 6,
            [shape_of((blocks, size, one_cols), bf16)] * 2
            + [shape_of((blocks, size, two_cols), bf16)] * 2,
            [],
            (one_blocks[0], one_in, table_blocks[0], table_in, two_blocks[0], two_in),
        )
        one_blocks, two_blocks = outs[:2], outs[2:]
    else:
        one_blocks = join(stepped(one_blocks[0], one_in), stepped(table_blocks[0], table_in))
        two_blocks = stepped(two_blocks[0], two_in)
    one_in = swap(one_blocks[1], "dp", near_steps[1], 1)
    two_in = swap(two_blocks[1], "dp", far_steps[1], 1)
    one_in, two_in = lax.optimization_barrier((one_in, two_in))
    last_blocks = join(stepped(one_blocks[0], one_in), stepped(two_blocks[0], two_in))
    last_in = swap(last_blocks[1], "dp", near_steps[2], 1)

    def finished(blocks, arrived, turn, *others):
        kept = blocks[0]
        for step in near_steps[3:]:
            kept, sent = stepped(kept, arrived)
            arrived = swap(sent, "dp", step, turn)
        [part] = call(
            last_step_kernel,
            "vv",
            [shape_of(kept.shape[1:], bf16)],
            [],
            (kept, arrived),
            others=others,
        )
        return part

    mlp_parts = four(finished(mlp_blocks, mlp_in, 0, one_blocks[0], two_blocks[0]), 0)
    up_grad, down_grad = call(
        mlp_out_kernel,
        "svvvv",
        [shape_of((size, hidden_width), f32), shape_of((size, hidden_width), f32)],
        [],
        (ids, *mlp_parts),
        0,
    )
    last_part = finished(last_blocks, last_in, 1)
    last_far = after(swap(last_part, "narrow", 2, 1), up_grad)
    last_parts = [last_part, swap(last_part, "narrow", 1), last_far, swap(last_far, "narrow", 1)]
    last_shapes = [shape_of((size, 3 * width), f32), shape_of((size, width), f32)]
    last_scratch = [pltpu.VMEM((4, *last_part.shape), f32)]
    if compact:
        (
            qkv_grad,
            proj_grad,
            embed_grad,
            position_grad,
            class_grad,
            head_grad,
            gain_one,
            gain_two,
            bias,
        ) = call(
            functools.partial(
                last_out_kernel, (position_cols, embed_cols, slot_cols, head_cols, 2 * group)
            ),
            "svvvv",
            [
                *last_shapes,
                shape_of((channels, size), f32),
                shape_of((size, position_table.shape[0]), f32),
                shape_of((size, class_table.shape[0]), f32),
                shape_of((size, 2 * channels), f32),
                shape_of((1, size), f32),
                shape_of((1, size), f32),
                shape_of((1, size), f32),
            ],
            last_scratch,
            (ids, *last_parts),
            0,
        )
        attngain_grad, mlpgain_grad, bias_grad = gain_one[0], gain_two[0], bias[0]
    else:
        qkv_grad, proj_grad = call(
            heads_out_kernel, "svvvv", last_shapes, last_scratch, (ids, *last_parts), 0
        )
        shares = jnp.stack(last_parts).astype(f32)[:, :, 2 * group : -2 * group]
        shares = [lax.dynamic_index_in_dim(shares, r ^ i, 0, keepdims=False) for i in range(4)]
        class_cols = class_table.shape[0] // 4

        def joined(start, cols):
            return jnp.concatenate([share[:, start : start + cols] for share in shares], axis=1)

        position_grad = joined(0, position_cols)
        embed_grad = joined(position_cols, embed_cols).T
        class_grad = joined(LANES, class_cols)
        head_grad = joined(LANES - head_cols, head_cols)
        attngain_grad = shares[0][:, gain_at]
        mlpgain_grad = shares[0][:, gain_at + 1]
        bias_grad = shares[0][:, LANES + class_cols]
    return (
        latent.T[None],
        logdet,
        patches_grad.T[None],
        embed_grad,
        bias_grad,
        position_grad.T,
        class_grad.T,
        attngain_grad,
        qkv_grad,
        proj_grad,
        mlpgain_grad,
        up_grad,
        down_grad.T,
        head_grad,
    )


def solution(mesh):
    return jax.shard_map(
        shards,
        mesh=mesh,
        in_specs=(
            P("dp", "narrow", None),
            P("dp", None),
            P("dp", None),
            P(),
            P(),
            P(),
            P(),
            P(),
            P(),
            P(),
            P(),
            P(),
            P(),
            P(),
            P("dp", "narrow", None),
            P("dp", "narrow"),
        ),
        out_specs=(
            P("dp", "narrow", None),
            P("dp", "narrow"),
            P("dp", "narrow", None),
            P(None, "dp"),
            P("dp"),
            P(None, "dp"),
            P(None, "dp"),
            P("dp"),
            P("dp", None),
            P("dp", None),
            P("dp"),
            P("dp", None),
            P(None, "dp"),
            P("dp", None),
        ),
        check_vma=False,
    )
```
